32 devices in a mesh: expert: 16 (over z, y, x), dp: 2 (over core).
Axes of the slice: x: 2, y: 2, z: 4, core: 2. Of those that a mesh axis runs over, the one named last changes fastest.
Arguments:
- tokens: bfloat16 [2048, 2048], P(('expert', 'dp')), may hold values from -6 to 6
- grad_out: bfloat16 [2048, 2048], P(('expert', 'dp')), may hold values from -6 to 6
- expert_ids: int32 [2048, 8], P(('expert', 'dp')), may hold values from 0 to 15, all different within a row; in each aligned block of 64 rows (0 to 63, 64 to 127, ...) at most 48 rows name the same one
- router_weights: float32 [2048, 8], P(('expert', 'dp')), may hold values from 0.02 to 0.25
- codes_in: int32 [16, 2, 2048, 256], P('expert', None, 'dp'), may hold values from 0 to 4095
- codes_out: int32 [16, 256, 2048], P('expert', None, 'dp'), may hold values from 0 to 4095
- clip_in: float32 [16, 2, 2, 16, 768], P('expert'), may hold values from -1 to 3
- range_in: float32 [16, 2, 2, 16, 768], P('expert'), may hold values from 0.01 to 0.06
- clip_out: float32 [16, 2, 6, 2048], P('expert'), may hold values from -1 to 3
- range_out: float32 [16, 2, 6, 2048], P('expert'), may hold values from 0.018 to 0.1
Outputs:
- grad_tokens: bfloat16 [2048, 2048], P(('expert', 'dp'))
- grad_clip_in: float32 [16, 2, 2, 16, 768], P('expert', None, None, 'dp')
- grad_clip_out: float32 [16, 2, 6, 2048], P('expert', None, None, 'dp')
The draws below stay inside these ranges and needn't reach their ends.
Inputs may be any that keep to these rules, and one draw needn't show every extreme that they name: `expert_ids`: each row names 8 different experts; among the rows of one device no expert is named by more than 48 rows, and in some device some expert is named by exactly 48 rows.
All inputs are finite; a program needn't handle non-finite values.
Results may differ from the reference program's by a relative error of at most 0.0082.
Values may be sent and summed in bfloat16 or wider, within the bound.
No kernel may reach another device: no remote copies, remote signals or barrier semaphores. Data moves between devices by JAX's collectives and lax.ppermute only.
A program may use at most 128 MiB of HBM per device.

```python
import math
import jax
import jax.numpy as jnp
import numpy as np
from jax import lax

D = 2048
FF = 768
TOP = 8
GROUP = 128
TOK_DEV = 64
EXPERTS = 16
CAP = 48
TOKENS = 2048
G_IN = 16
G_OUT = 6


def plant(array, key, least, high):
    longest = array.shape.index(max(array.shape))
    spots = []
    for shift in (0, 1):
        where = [jax.random.randint(jax.random.fold_in(key, axis), (), 0, length) for axis, length in enumerate(array.shape)]
        where[longest] = (where[longest] + shift) % array.shape[longest]
        spots.append(tuple(where))
    return array.at[spots[0]].set(least).at[spots[1]].set(high)


def block_scale(stream_key, dims, shards, smallest, high):
    gain = 1.0
    for position, blocks in shards:
        heights = jax.random.uniform(jax.random.fold_in(jax.random.fold_in(stream_key, 6), position), (blocks,), jnp.float32, smallest / len(shards), high / len(shards))
        gain = gain * jnp.repeat(jnp.exp(heights), dims[position] // blocks).reshape((-1,) + (1,) * (len(dims) - 1 - position))
    return gain


def deal_out(key, own, number, rows, amount, top, limit, lean):
    ranking = jax.random.permutation(key, amount)
    heavy_load, common = portions_of(amount, rows * top, limit, lean, True), portions_of(amount, rows * top, limit, lean, False)
    places = jnp.arange(amount)

    def named(sizes, offset_by):
        used = int((sizes > 0).sum())
        fixed = max(1, used // 4)
        passed = fixed + (places - fixed + offset_by * (used - fixed)) % max(1, amount - fixed)
        return jnp.zeros((amount,), jnp.int32).at[ranking[jnp.where(places < fixed, places, passed)]].set(jnp.asarray(sizes, jnp.int32))

    sizes = jnp.where(number % 4 == 0, named(heavy_load, number // 4), named(common, number - number // 4 - 1))
    mixed = jax.random.permutation(jax.random.fold_in(own, 3), amount)
    donor, sink = mixed[0:amount // 2 * 2:2], mixed[1:amount // 2 * 2:2]
    margin = jnp.minimum(sizes[donor] - 1, limit - sizes[sink]) // 2
    margin = jnp.where((donor == ranking[0]) | (sink == ranking[0]) | (sizes[sink] == 0), 0, jnp.maximum(margin, 0))
    passed = jax.random.randint(jax.random.fold_in(own, 4), (amount // 2,), 0, 1 << 20) % (margin + 1)
    sizes = sizes.at[donor].add(-passed).at[sink].add(passed)
    labels = jnp.searchsorted(jnp.cumsum(sizes), jnp.arange(rows * top), side="right").astype(jnp.int32)
    listing = labels.reshape(top, rows).T
    listing = listing[jax.random.permutation(jax.random.fold_in(own, 1), rows)]
    offset_by = jax.random.randint(jax.random.fold_in(own, 2), (rows, 1), 0, top)
    return jnp.take_along_axis(listing, (jnp.arange(top)[None, :] + offset_by) % top, axis=1)


def portions_of(number_of, total, limit, skew, full):
    weights = [(1 << 20) // math.isqrt(grade ** skew) + 1 for grade in range(1, number_of + 1)]
    largest = limit if full else min(limit, max(-(-total // number_of), total * weights[0] // sum(weights)))
    least = 1 if total - largest >= number_of - 1 else 0
    given, spare = [largest] + [least] * (number_of - 1), total - largest - least * (number_of - 1)
    while spare > 0:
        movable = [i for i in range(1, number_of) if given[i] < largest] or [i for i in range(1, number_of) if given[i] < limit]
        whole, left = sum([weights[i] for i in movable]), spare
        for i in movable:
            extra = min(limit - given[i], max(1, left * weights[i] // whole), spare)
            given[i] = given[i] + extra
            spare = spare - extra
    return np.array(given)


def gaussian(key, extent, scale, most, cuts=(), kind=jnp.bfloat16):
    entries = scale * jax.random.normal(key, extent, jnp.float32)
    if cuts:
        entries = entries * block_scale(key, extent, cuts, -0.22, 0.18)
    return jnp.clip(entries, -most, most).astype(kind)


def setup_inputs(seed: int = 0) -> dict:
    key_list = jax.random.split(jax.random.key(seed), 11)
    tokens = gaussian(key_list[0], (TOKENS, D), 1.0, 6.0, ((0, 32),))
    grad_out = gaussian(key_list[1], (TOKENS, D), 1.0, 6.0, ((0, 32),))
    expert_ids_keys = jax.random.split(jax.random.fold_in(key_list[2], 1), TOKENS // TOK_DEV)
    expert_ids_turns = jax.random.permutation(jax.random.fold_in(key_list[2], 3), TOKENS // TOK_DEV)
    expert_ids = jax.vmap(lambda own, number: deal_out(jax.random.fold_in(key_list[2], 2), own, number, TOK_DEV, EXPERTS, TOP, CAP, 2))(expert_ids_keys, expert_ids_turns).reshape((TOKENS, TOP))
    router_weights = jnp.clip(0.02 + 0.23 * jax.random.uniform(key_list[3], (TOKENS, TOP), jnp.float32) ** block_scale(key_list[3], (TOKENS, TOP), ((0, 32),), -0.2, 0.2), 0.02, 0.25)
    codes_in = plant(jax.random.randint(key_list[4], (EXPERTS, 2, D, FF // 3), 0, 4096), jax.random.fold_in(key_list[4], 1), 0, 4095).astype(jnp.int32)
    codes_out = plant(jax.random.randint(key_list[5], (EXPERTS, FF // 3, D), 0, 4096), jax.random.fold_in(key_list[5], 1), 0, 4095).astype(jnp.int32)
    clip_in = jnp.clip(-1.0 + 4.0 * jax.random.uniform(key_list[6], (EXPERTS, 2, 2, G_IN, FF), jnp.float32) ** block_scale(key_list[6], (EXPERTS, 2, 2, G_IN, FF), ((0, 16),), -0.2, 0.2), -1.0, 3.0)
    range_in = jnp.clip(jnp.exp(math.log(0.06) - 1.7917595 * jax.random.uniform(key_list[7], (EXPERTS, 2, 2, G_IN, FF), jnp.float32) ** block_scale(key_list[7], (EXPERTS, 2, 2, G_IN, FF), ((0, 16),), -0.2, 0.2)), 0.01, 0.06)
    clip_out = jnp.clip(-1.0 + 4.0 * jax.random.uniform(key_list[8], (EXPERTS, 2, G_OUT, D), jnp.float32) ** block_scale(key_list[8], (EXPERTS, 2, G_OUT, D), ((0, 16),), -0.2, 0.2), -1.0, 3.0)
    range_out = jnp.clip(jnp.exp(math.log(0.1) - 1.7147985 * jax.random.uniform(key_list[9], (EXPERTS, 2, G_OUT, D), jnp.float32) ** block_scale(key_list[9], (EXPERTS, 2, G_OUT, D), ((0, 16),), -0.2, 0.2)), 0.018, 0.1)
    return dict(tokens=tokens, grad_out=grad_out, expert_ids=expert_ids, router_weights=router_weights, codes_in=codes_in, codes_out=codes_out, clip_in=clip_in, range_in=range_in, clip_out=clip_out, range_out=range_out)


def unpack_columns(packed):
    shifts = 4 * jnp.arange(3, dtype=jnp.int32)
    nibble = jnp.bitwise_and(jnp.right_shift(packed[..., None], shifts), 15)
    new_shape = packed.shape[:-1] + (packed.shape[-1] * 3,)
    return nibble.reshape(new_shape).astype(jnp.bfloat16)


def unpack_rows(packed):
    shifts = 4 * jnp.arange(3, dtype=jnp.int32)
    nibble = jnp.bitwise_and(jnp.right_shift(packed[:, None, :], shifts[:, None]), 15)
    return nibble.reshape(packed.shape[0] * 3, packed.shape[1]).astype(jnp.bfloat16)


def dequantize(code_rows, clip_pair, range_pair):
    upper_end = jax.nn.sigmoid(clip_pair[0]) * range_pair[0]
    lower_end = jax.nn.sigmoid(clip_pair[1]) * range_pair[1]
    step_size = (upper_end + lower_end) / 15.0
    groups = code_rows.shape[0] // GROUP
    blocked = code_rows.reshape(groups, GROUP, code_rows.shape[1])
    weight = step_size[:, None, :] * blocked - lower_end[:, None, :]
    return weight.reshape(code_rows.shape).astype(jnp.bfloat16)


def group_terms(grad_weight, weight, clip_pair, range_pair):
    upper_end = jax.nn.sigmoid(clip_pair[0]) * range_pair[0]
    lower_end = jax.nn.sigmoid(clip_pair[1]) * range_pair[1]
    groups = grad_weight.shape[0] // GROUP
    blocked = grad_weight.reshape(groups, GROUP, grad_weight.shape[1])
    shifted = weight.astype(jnp.float32).reshape(blocked.shape) + lower_end[:, None, :]
    weighted = jnp.sum(blocked * shifted, axis=1) / (upper_end + lower_end)
    return jnp.stack([weighted, weighted - jnp.sum(blocked, axis=1)])


def clip_grads(group_sums, clip_pair, range_pair):
    sig_upper = jax.nn.sigmoid(clip_pair[0])
    sig_lower = jax.nn.sigmoid(clip_pair[1])
    return jnp.stack([group_sums[0] * range_pair[0] * sig_upper * (1.0 - sig_upper),
                      group_sums[1] * range_pair[1] * sig_lower * (1.0 - sig_lower)])


def contract(left_side, right_side, left_dim, right_dim):
    return lax.dot_general(left_side, right_side, (((left_dim,), (right_dim,)), ((), ())),
                           preferred_element_type=jnp.float32)


def expert_forward(token_rows, gate_weight, up_weight):
    gate_pre = jnp.dot(token_rows, gate_weight, preferred_element_type=jnp.float32)
    up_pre = jnp.dot(token_rows, up_weight, preferred_element_type=jnp.float32)
    gate_sig = jax.nn.sigmoid(gate_pre)
    gate_act = gate_pre * gate_sig
    hidden = (gate_act * up_pre).astype(jnp.bfloat16)
    return gate_pre, up_pre, gate_sig, gate_act, hidden


def expert_backward(forward_parts, slope_rows, gate_weight, up_weight, down_weight):
    gate_pre, up_pre, gate_sig, gate_act, hidden = forward_parts
    grad_hidden = contract(slope_rows, down_weight, 1, 1)
    grad_gate = (grad_hidden * up_pre * gate_sig * (1.0 + gate_pre * (1.0 - gate_sig))).astype(jnp.bfloat16)
    grad_up = (grad_hidden * gate_act).astype(jnp.bfloat16)
    grad_rows = (contract(grad_gate, gate_weight, 1, 1) + contract(grad_up, up_weight, 1, 1)).astype(jnp.bfloat16)
    return grad_gate, grad_up, grad_rows


def reference(tokens, grad_out, expert_ids, router_weights, codes_in, codes_out, clip_in, range_in, clip_out, range_out):
    blocks = TOKENS // TOK_DEV
    assign = TOK_DEV * TOP
    flat_ids = expert_ids.reshape(blocks, assign)
    onehot = (flat_ids[:, :, None] == jnp.arange(EXPERTS, dtype=jnp.int32)[None, None, :]).astype(jnp.int32)
    before = jnp.sum((jnp.cumsum(onehot, axis=1) - onehot) * onehot, axis=2)
    block_idx = jnp.arange(blocks, dtype=jnp.int32)[:, None] * jnp.ones((1, assign), jnp.int32)
    token_row = block_idx * TOK_DEV + (jnp.arange(assign, dtype=jnp.int32) // TOP)[None, :]
    slot_token = jnp.full((blocks, EXPERTS, CAP), -1, jnp.int32).at[block_idx, flat_ids, before].set(token_row)
    slot_weight = jnp.zeros((blocks, EXPERTS, CAP), jnp.float32).at[block_idx, flat_ids, before].set(
        router_weights.reshape(blocks, assign))

    def per_expert(running, expert):
        code_in = unpack_columns(codes_in[expert])
        code_out = unpack_rows(codes_out[expert])
        gate_weight = dequantize(code_in[0], clip_in[expert, 0], range_in[expert, 0])
        up_weight = dequantize(code_in[1], clip_in[expert, 1], range_in[expert, 1])
        down_weight = dequantize(code_out, clip_out[expert], range_out[expert])
        slot_rows = slot_token[:, expert, :].reshape(-1)
        is_live = slot_rows >= 0
        safe_rows = jnp.maximum(slot_rows, 0)
        token_rows = jnp.where(is_live[:, None], tokens[safe_rows], jnp.zeros((), jnp.bfloat16))
        route_scale = slot_weight[:, expert, :].reshape(-1)
        slope_rows = (route_scale[:, None] * grad_out[safe_rows].astype(jnp.float32)).astype(jnp.bfloat16)
        forward_parts = expert_forward(token_rows, gate_weight, up_weight)
        grad_gate, grad_up, grad_rows = expert_backward(forward_parts, slope_rows, gate_weight, up_weight, down_weight)
        running = running.at[safe_rows].add(grad_rows.astype(jnp.float32))
        sums_in = jnp.stack([group_terms(contract(token_rows, grad_gate, 0, 0), gate_weight, clip_in[expert, 0], range_in[expert, 0]),
                             group_terms(contract(token_rows, grad_up, 0, 0), up_weight, clip_in[expert, 1], range_in[expert, 1])])
        sums_out = group_terms(contract(forward_parts[4], slope_rows, 0, 0), down_weight, clip_out[expert], range_out[expert])
        out_in = jnp.stack([clip_grads(sums_in[0], clip_in[expert, 0], range_in[expert, 0]),
                            clip_grads(sums_in[1], clip_in[expert, 1], range_in[expert, 1])])
        out_out = clip_grads(sums_out, clip_out[expert], range_out[expert])
        return running, (out_in, out_out)

    running, (grad_clip_in, grad_clip_out) = lax.scan(
        per_expert, jnp.zeros((TOKENS, D), jnp.float32), jnp.arange(EXPERTS, dtype=jnp.int32))
    return running.astype(jnp.bfloat16), grad_clip_in, grad_clip_out
```

```python
import jax
import jax.numpy as jnp
from jax import lax
from jax.sharding import PartitionSpec as P

GROUP = 128


def unpack_columns(packed):
    shifts = 4 * jnp.arange(3, dtype=jnp.int32)
    nibble = jnp.bitwise_and(jnp.right_shift(packed[..., None], shifts), 15)
    new_shape = packed.shape[:-1] + (packed.shape[-1] * 3,)
    return nibble.reshape(new_shape).astype(jnp.bfloat16)


def unpack_rows(packed):
    shifts = 4 * jnp.arange(3, dtype=jnp.int32)
    nibble = jnp.bitwise_and(jnp.right_shift(packed[:, None, :], shifts[:, None]), 15)
    return nibble.reshape(packed.shape[0] * 3, packed.shape[1]).astype(jnp.bfloat16)


def dequantize(code_rows, clip_pair, range_pair):
    upper_end = jax.nn.sigmoid(clip_pair[0]) * range_pair[0]
    lower_end = jax.nn.sigmoid(clip_pair[1]) * range_pair[1]
    step_size = (upper_end + lower_end) / 15.0
    groups = code_rows.shape[0] // GROUP
    blocked = code_rows.reshape(groups, GROUP, code_rows.shape[1])
    weight = step_size[:, None, :] * blocked - lower_end[:, None, :]
    return weight.reshape(code_rows.shape).astype(jnp.bfloat16)


def group_terms(grad_weight, weight, clip_pair, range_pair):
    upper_end = jax.nn.sigmoid(clip_pair[0]) * range_pair[0]
    lower_end = jax.nn.sigmoid(clip_pair[1]) * range_pair[1]
    groups = grad_weight.shape[0] // GROUP
    blocked = grad_weight.reshape(groups, GROUP, grad_weight.shape[1])
    shifted = weight.astype(jnp.float32).reshape(blocked.shape) + lower_end[:, None, :]
    weighted = jnp.sum(blocked * shifted, axis=1) / (upper_end + lower_end)
    return jnp.stack([weighted, weighted - jnp.sum(blocked, axis=1)])


def clip_grads(group_sums, clip_pair, range_pair):
    sig_upper = jax.nn.sigmoid(clip_pair[0])
    sig_lower = jax.nn.sigmoid(clip_pair[1])
    return jnp.stack(
        [
            group_sums[0] * range_pair[0] * sig_upper * (1.0 - sig_upper),
            group_sums[1] * range_pair[1] * sig_lower * (1.0 - sig_lower),
        ]
    )


def contract(left_side, right_side, left_dim, right_dim):
    return lax.dot_general(
        left_side,
        right_side,
        (((left_dim,), (right_dim,)), ((), ())),
        preferred_element_type=jnp.float32,
    )


def expert_forward(token_rows, gate_weight, up_weight):
    gate_pre = jnp.dot(token_rows, gate_weight, preferred_element_type=jnp.float32)
    up_pre = jnp.dot(token_rows, up_weight, preferred_element_type=jnp.float32)
    gate_sig = jax.nn.sigmoid(gate_pre)
    gate_act = gate_pre * gate_sig
    hidden = (gate_act * up_pre).astype(jnp.bfloat16)
    return (gate_pre, up_pre, gate_sig, gate_act, hidden)


def expert_backward(forward_parts, slope_rows, gate_weight, up_weight, down_weight):
    gate_pre, up_pre, gate_sig, gate_act, hidden = forward_parts
    grad_hidden = contract(slope_rows, down_weight, 1, 1)
    grad_gate = (grad_hidden * up_pre * gate_sig * (1.0 + gate_pre * (1.0 - gate_sig))).astype(
        jnp.bfloat16
    )
    grad_up = (grad_hidden * gate_act).astype(jnp.bfloat16)
    grad_rows = (
        contract(grad_gate, gate_weight, 1, 1) + contract(grad_up, up_weight, 1, 1)
    ).astype(jnp.bfloat16)
    return (grad_gate, grad_up, grad_rows)


def body(
    tokens,
    grad_out,
    expert_ids,
    router_weights,
    codes_in,
    codes_out,
    clip_in,
    range_in,
    clip_out,
    range_out,
):
    experts = lax.axis_size("expert")
    model_width = tokens.shape[1]
    mine = lax.axis_index("expert")
    experts_row = jnp.arange(experts, dtype=jnp.int32)
    weight_table = jnp.sum(
        jnp.where(expert_ids[:, :, None] == experts_row[None, None, :], router_weights[:, :, None], 0.0),
        axis=1,
    )
    table_all = lax.all_gather(weight_table, "expert", axis=0, tiled=True)
    token_rows = lax.all_gather(tokens, "expert", axis=0, tiled=True)
    grad_all = lax.all_gather(grad_out, "expert", axis=0, tiled=True)
    route = jnp.sum(jnp.where(experts_row[None, :] == mine, table_all, 0.0), axis=1)
    slope_rows = (route[:, None] * grad_all.astype(jnp.float32)).astype(jnp.bfloat16)
    dp_count = lax.axis_size("dp")
    dp_index = lax.axis_index("dp")
    share_in = clip_in.shape[3] // dp_count
    share_out = model_width // dp_count
    clip_share_in = lax.dynamic_slice_in_dim(clip_in[0], dp_index * share_in, share_in, 2)
    range_share_in = lax.dynamic_slice_in_dim(range_in[0], dp_index * share_in, share_in, 2)
    clip_share_out = lax.dynamic_slice_in_dim(clip_out[0], dp_index * share_out, share_out, 2)
    range_share_out = lax.dynamic_slice_in_dim(range_out[0], dp_index * share_out, share_out, 2)
    code_share_in = unpack_columns(codes_in[0])
    code_share_out = unpack_rows(codes_out[0])
    gate_share = dequantize(code_share_in[0], clip_share_in[0], range_share_in[0])
    up_share = dequantize(code_share_in[1], clip_share_in[1], range_share_in[1])
    down_share = dequantize(code_share_out, clip_share_out, range_share_out)
    gate_weight, up_weight = (
        lax.all_gather(gate_share, "dp", axis=0, tiled=True),
        lax.all_gather(up_share, "dp", axis=0, tiled=True),
    )
    down_weight = lax.all_gather(down_share, "dp", axis=1, tiled=True)
    forward_parts = expert_forward(token_rows, gate_weight, up_weight)
    grad_gate, grad_up, grad_rows = expert_backward(
        forward_parts, slope_rows, gate_weight, up_weight, down_weight
    )
    grad_tokens = lax.psum_scatter(grad_rows, "expert", scatter_dimension=0, tiled=True)
    sums_in = jnp.stack(
        [
            group_terms(
                contract(token_rows, grad_gate, 0, 0), gate_weight, clip_in[0, 0], range_in[0, 0]
            ),
            group_terms(
                contract(token_rows, grad_up, 0, 0), up_weight, clip_in[0, 1], range_in[0, 1]
            ),
        ]
    )
    sums_out = group_terms(
        contract(forward_parts[4], slope_rows, 0, 0), down_weight, clip_out[0], range_out[0]
    )
    part_in, part_out = (
        lax.psum_scatter(
            sums_in.astype(jnp.bfloat16), "dp", scatter_dimension=2, tiled=True
        ).astype(jnp.float32),
        lax.psum_scatter(
            sums_out.astype(jnp.bfloat16), "dp", scatter_dimension=2, tiled=True
        ).astype(jnp.float32),
    )
    out_in = jnp.stack(
        [
            clip_grads(part_in[0], clip_share_in[0], range_share_in[0]),
            clip_grads(part_in[1], clip_share_in[1], range_share_in[1]),
        ]
    )[None]
    out_out = clip_grads(part_out, clip_share_out, range_share_out)[None]
    return (grad_tokens, out_in, out_out)


def solution(mesh):
    return jax.shard_map(
        body,
        mesh=mesh,
        in_specs=(
            P(("expert", "dp"), None),
            P(("expert", "dp"), None),
            P(("expert", "dp"), None),
            P(("expert", "dp"), None),
            P("expert", None, "dp", None),
            P("expert", None, "dp"),
            P("expert", None, None, None, None),
            P("expert", None, None, None, None),
            P("expert", None, None, None),
            P("expert", None, None, None),
        ),
        out_specs=(
            P(("expert", "dp"), None),
            P("expert", None, None, "dp", None),
            P("expert", None, None, "dp"),
        ),
        check_vma=False,
    )
```

```python
import functools

import jax
import jax.numpy as jnp
from jax import lax
from jax.experimental import pallas as pl
from jax.experimental.pallas import tpu as pltpu
from jax.sharding import PartitionSpec as P

GROUP = 128
PACK = 3
CHUNK = 16
TILE = 256
LIMIT = 56 * 1024 * 1024
F32 = jnp.float32
BF16 = jnp.bfloat16


def dot_nn(a, b):
    return lax.dot_general(a, b, (((1,), (0,)), ((), ())), preferred_element_type=F32)


def dot_nt(a, b):
    return lax.dot_general(a, b, (((1,), (1,)), ((), ())), preferred_element_type=F32)


def dot_tn(a, b):
    return lax.dot_general(a, b, (((0,), (0,)), ((), ())), preferred_element_type=F32)


def sigmoid(v):
    return 1.0 / (1.0 + jnp.exp(-v))


def plane_order(size):
    third = size // PACK
    row = lax.broadcasted_iota(jnp.int32, (size, size), 0)
    col = lax.broadcasted_iota(jnp.int32, (size, size), 1)
    plane = jnp.zeros_like(col)
    for j in range(1, PACK):
        plane = plane + (col >= j * third).astype(jnp.int32)
    return (row == PACK * (col - plane * third) + plane).astype(F32)


def exact_dot(a, b, dims):
    return lax.dot_general(
        a, b, (dims, ((), ())), precision=lax.Precision.HIGHEST, preferred_element_type=F32
    )


def whole_spec(shape):
    zeros = (0,) * len(shape)
    return pl.BlockSpec(shape, lambda *_: zeros)


def pack_kernel(experts, grad_ref, ids_ref, weights_ref, out_ref):
    rows, width = grad_ref.shape
    extra = out_ref.shape[1] - width
    out_ref[:, :width] = grad_ref[...]
    lane = lax.broadcasted_iota(jnp.int32, (rows, extra), 1)
    part = lane // experts
    expert = lane - part * experts
    table = jnp.zeros((rows, extra), F32)
    for k in range(ids_ref.shape[1]):
        table = table + jnp.where(ids_ref[:, k : k + 1] == expert, weights_ref[:, k : k + 1], 0.0)
    high = table.astype(BF16)
    rest = table - high.astype(F32)
    middle = rest.astype(BF16)
    low = (rest - middle.astype(F32)).astype(BF16)
    out_ref[:, width:] = jnp.where(
        part == 0,
        high.astype(F32),
        jnp.where(part == 1, middle.astype(F32), low.astype(F32)),
    ).astype(BF16)


def pack_grad(grad_out, expert_ids, router_weights, experts):
    rows, width = grad_out.shape
    extra = -(-3 * experts // 128) * 128
    return pl.pallas_call(
        functools.partial(pack_kernel, experts),
        out_shape=jax.ShapeDtypeStruct((rows, width + extra), BF16),
        name="pack_grad",
    )(grad_out, expert_ids, router_weights)


def weight_kernel(codes_in, codes_out, clip_in, range_in, clip_out, range_out, gu_ref, d_ref):
    hidden = clip_in.shape[3]
    third = hidden // PACK
    groups = clip_in.shape[2]
    order = plane_order(hidden)
    for p in range(2):
        upper = sigmoid(clip_in[p, 0]) * range_in[p, 0]
        lower = sigmoid(clip_in[p, 1]) * range_in[p, 1]
        ends = exact_dot(jnp.concatenate([(upper + lower) / 15.0, lower], axis=0), order, ((1,), (0,)))
        for g in range(groups):
            packed = codes_in[p, g * GROUP : (g + 1) * GROUP, :]
            for j in range(PACK):
                code = jnp.bitwise_and(jnp.right_shift(packed, 4 * j), 15).astype(F32)
                cols = slice(j * third, (j + 1) * third)
                gu_ref[p, g * GROUP : (g + 1) * GROUP, cols] = (
                    ends[g : g + 1, cols] * code - ends[groups + g : groups + g + 1, cols]
                ).astype(BF16)
    upper = sigmoid(clip_out[0]) * range_out[0]
    lower = sigmoid(clip_out[1]) * range_out[1]
    step = (upper + lower) / 15.0
    row = lax.broadcasted_iota(jnp.int32, (CHUNK, 1), 0)
    for start in range(0, third, CHUNK):
        packed = codes_out[start : start + CHUNK, :]
        for j in range(PACK):
            first = (PACK * start + j) // GROUP
            last = (PACK * (start + CHUNK - 1) + j) // GROUP
            step_rows, lower_rows = step[first : first + 1], lower[first : first + 1]
            for g in range(first + 1, last + 1):
                late = PACK * (row + start) + j >= g * GROUP
                step_rows = jnp.where(late, step[g : g + 1], step_rows)
                lower_rows = jnp.where(late, lower[g : g + 1], lower_rows)
            code = jnp.bitwise_and(jnp.right_shift(packed, 4 * j), 15).astype(F32)
            d_ref[j * third + start : j * third + start + CHUNK, :] = (
                step_rows * code - lower_rows
            ).astype(BF16)


def make_weights(codes_in, codes_out, clip_in, range_in, clip_out, range_out):
    depth, hidden = codes_in.shape[1], clip_in.shape[3]
    return pl.pallas_call(
        weight_kernel,
        out_shape=(
            jax.ShapeDtypeStruct((2, depth, hidden), BF16),
            jax.ShapeDtypeStruct((hidden, codes_out.shape[1]), BF16),
        ),
        compiler_params=pltpu.CompilerParams(vmem_limit_bytes=LIMIT),
        cost_estimate=pl.CostEstimate(flops=10**9, bytes_accessed=10**7, transcendentals=0),
        name="make_weights",
    )(codes_in, codes_out, clip_in, range_in, clip_out, range_out)


def set_kernel(experts, place, *refs):
    tokens, grads = refs[0:4], refs[4:8]
    gu_mine, gu_other, d_mine, d_other = refs[8:12]
    partials = refs[12:16]
    x_ref, s_ref, h_ref, gg_ref, gu_ref = refs[16:21]
    total = refs[21]
    rows, width = tokens[0].shape
    half = width // 2
    j = pl.program_id(0)
    mine = pl.ds(pl.multiple_of(place[0] * half, half), half)
    other = pl.ds(pl.multiple_of((1 - place[0]) * half, half), half)

    @pl.when(j == 0)
    def _():
        for i in range(4):
            span = slice(i * rows, (i + 1) * rows)
            x_ref[span, :] = tokens[i][...]
            beside = grads[i][:, width:].astype(F32)
            lane = lax.broadcasted_iota(jnp.int32, beside.shape, 1)
            keep = (lane == place[1]) | (lane == place[1] + experts) | (lane == place[1] + 2 * experts)
            scale = jnp.sum(jnp.where(keep, beside, 0.0), axis=1, keepdims=True)
            s_ref[span, :] = (scale * grads[i][:, :width].astype(F32)).astype(BF16)

    x_mine, x_other = x_ref[:, mine], x_ref[:, other]
    gate_pre = dot_nn(x_mine, gu_mine[0]) + dot_nn(x_other, gu_other[0])
    up_pre = dot_nn(x_mine, gu_mine[1]) + dot_nn(x_other, gu_other[1])
    grad_hidden = dot_nt(s_ref[:, mine], d_mine[...]) + dot_nt(s_ref[:, other], d_other[...])
    sig = sigmoid(gate_pre)
    act = gate_pre * sig
    h_ref[...] = (act * up_pre).astype(BF16)
    grad_gate = (grad_hidden * up_pre * sig * (1.0 + gate_pre * (1.0 - sig))).astype(BF16)
    grad_up = (grad_hidden * act).astype(BF16)
    gg_ref[...] = grad_gate
    gu_ref[...] = grad_up
    for span, weights in ((mine, gu_mine), (other, gu_other)):
        part = dot_nt(grad_gate, weights[0]) + dot_nt(grad_up, weights[1])

        @pl.when(j == 0)
        def _():
            total[:, span] = part

        @pl.when(j > 0)
        def _():
            total[:, span] = total[:, span] + part

    @pl.when(j == pl.num_programs(0) - 1)
    def _():
        for i in range(4):
            partials[i][...] = total[i * rows : (i + 1) * rows, :].astype(BF16)


def run_set(place, tokens, grads, weights, experts):
    rows, width = tokens[0].shape
    gu_mine, gu_other, d_mine, d_other = weights
    hidden, half = d_mine.shape
    third = hidden // PACK
    all_rows = 4 * rows
    gu_spec = pl.BlockSpec((2, half, third), lambda j, *_: (0, 0, j))
    d_spec = pl.BlockSpec((third, half), lambda j, *_: (j, 0))
    h_spec = pl.BlockSpec((all_rows, third), lambda j, *_: (0, j))
    wide = jax.ShapeDtypeStruct((all_rows, width), BF16)
    narrow = jax.ShapeDtypeStruct((all_rows, hidden), BF16)
    out = pl.pallas_call(
        functools.partial(set_kernel, experts),
        grid_spec=pltpu.PrefetchScalarGridSpec(
            num_scalar_prefetch=1,
            grid=(PACK,),
            in_specs=[whole_spec(t.shape) for t in tokens]
            + [whole_spec(g.shape) for g in grads]
            + [gu_spec, gu_spec, d_spec, d_spec],
            out_specs=[whole_spec((rows, width))] * 4
            + [whole_spec((all_rows, width))] * 2
            + [h_spec] * 3,
            scratch_shapes=[pltpu.VMEM((all_rows, width), F32)],
        ),
        out_shape=[jax.ShapeDtypeStruct((rows, width), BF16)] * 4 + [wide] * 2 + [narrow] * 3,
        compiler_params=pltpu.CompilerParams(vmem_limit_bytes=LIMIT),
        cost_estimate=pl.CostEstimate(
            flops=10 * all_rows * width * hidden,
            bytes_accessed=6 * width * hidden + 16 * all_rows * width,
            transcendentals=all_rows * hidden,
        ),
        name="expert_set",
    )(place, *tokens, *grads, gu_mine, gu_other, d_mine, d_other)
    return out[:4], out[4:]


def sums_kernel(place, *refs):
    x_ref, s_ref, h_ref, gg_ref, gu_ref = refs[0:5]
    weights_in, weights_out = refs[5:7], refs[7:9]
    before, outs = refs[9:13], refs[13:17]
    t = pl.program_id(0)
    width = x_ref.shape[1]
    half = width // 2
    hidden = h_ref.shape[1]
    third = hidden // PACK
    groups_out = outs[1].shape[1]
    for side in range(2):
        base = jnp.where(side == 0, place[0], 1 - place[0]) * half + t * TILE
        span = pl.ds(pl.multiple_of(base, TILE), TILE)
        sums_in, sums_out = outs[2 * side], outs[2 * side + 1]
        old_in, old_out = before[2 * side], before[2 * side + 1]
        x_cols = x_ref[:, span]
        for p, g_ref in enumerate((gg_ref, gu_ref)):
            grad = dot_tn(x_cols, g_ref[...])
            weighted = grad * weights_in[side][p].astype(F32)
            for g in range(TILE // GROUP):
                rows = slice(g * GROUP, (g + 1) * GROUP)
                spot = pl.ds(t * (TILE // GROUP) + g, 1)
                sums_in[p, 0, spot, :] = old_in[p, 0, spot, :] + jnp.sum(weighted[rows], axis=0, keepdims=True)
                sums_in[p, 1, spot, :] = old_in[p, 1, spot, :] + jnp.sum(grad[rows], axis=0, keepdims=True)
        grad = dot_tn(h_ref[...], s_ref[:, span])
        weighted = grad * weights_out[side][...].astype(F32)
        cols = pl.ds(pl.multiple_of(t * TILE, TILE), TILE)
        for g in range(groups_out):
            for kind, values in enumerate((weighted, grad)):
                found = old_out[kind, g : g + 1, cols]
                for j in range(PACK):
                    low = -((j - GROUP * g) // PACK)
                    high = -((j - GROUP * (g + 1)) // PACK)
                    start, stop = low // 8 * 8, -(-high // 8) * 8
                    block = values[j * third + start : j * third + stop]
                    row = lax.broadcasted_iota(jnp.int32, block.shape, 0) + start
                    inside = (row >= low) & (row < high)
                    found = found + jnp.sum(jnp.where(inside, block, 0.0), axis=0, keepdims=True)
                sums_out[kind, g : g + 1, cols] = found


def run_sums(place, stored, weights, before):
    x, s, h, gg, gu = stored
    gu_mine, gu_other, d_mine, d_other = weights
    all_rows, width = x.shape
    hidden = h.shape[1]
    half = width // 2
    in_spec = pl.BlockSpec((2, TILE, hidden), lambda t, *_: (0, t, 0))
    out_spec = pl.BlockSpec((hidden, TILE), lambda t, *_: (0, t))
    return pl.pallas_call(
        sums_kernel,
        grid_spec=pltpu.PrefetchScalarGridSpec(
            num_scalar_prefetch=1,
            grid=(half // TILE,),
            in_specs=[whole_spec(a.shape) for a in stored]
            + [in_spec, in_spec, out_spec, out_spec]
            + [whole_spec(b.shape) for b in before],
            out_specs=[whole_spec(b.shape) for b in before],
        ),
        out_shape=[jax.ShapeDtypeStruct(b.shape, F32) for b in before],
        compiler_params=pltpu.CompilerParams(vmem_limit_bytes=LIMIT),
        cost_estimate=pl.CostEstimate(
            flops=6 * all_rows * width * hidden,
            bytes_accessed=6 * width * hidden + 4 * all_rows * width,
            transcendentals=0,
        ),
        name="group_sums",
    )(place, x, s, h, gg, gu, gu_mine, gu_other, d_mine, d_other, *before)


def clip_kernel(mine_in, got_in, mine_out, got_out, clip_in, range_in, clip_out, range_out, in_ref, out_ref):
    hidden = clip_in.shape[3]
    groups = clip_in.shape[2]
    order = plane_order(hidden)

    def finish(weighted, plain, clip, span):
        sig_upper, sig_lower = sigmoid(clip[0]), sigmoid(clip[1])
        upper, lower = sig_upper * span[0], sig_lower * span[1]
        upper_sum = (weighted + lower * plain) / (upper + lower)
        lower_sum = upper_sum - plain
        return (
            upper_sum * span[0] * sig_upper * (1.0 - sig_upper),
            lower_sum * span[1] * sig_lower * (1.0 - sig_lower),
        )

    for p in range(2):
        sums = jnp.concatenate(
            [mine_in[p, 0] + got_in[p, 0], mine_in[p, 1] + got_in[p, 1]], axis=0
        )
        natural = exact_dot(sums, order, ((1,), (1,)))
        in_ref[p, 0], in_ref[p, 1] = finish(
            natural[:groups], natural[groups:], (clip_in[p, 0], clip_in[p, 1]), (range_in[p, 0], range_in[p, 1])
        )
    out_ref[0], out_ref[1] = finish(
        mine_out[0] + got_out[0],
        mine_out[1] + got_out[1],
        (clip_out[0], clip_out[1]),
        (range_out[0], range_out[1]),
    )


def clip_gradients(sums, shares):
    return pl.pallas_call(
        clip_kernel,
        out_shape=(
            jax.ShapeDtypeStruct(shares[0].shape, F32),
            jax.ShapeDtypeStruct(shares[2].shape, F32),
        ),
        compiler_params=pltpu.CompilerParams(vmem_limit_bytes=LIMIT),
        name="clip_gradients",
    )(*sums, *shares)


def added(*parts):
    return sum(part.astype(F32) for part in parts).astype(BF16)


def body(
    tokens,
    grad_out,
    expert_ids,
    router_weights,
    codes_in,
    codes_out,
    clip_in,
    range_in,
    clip_out,
    range_out,
):
    experts = lax.axis_size("expert")
    width = tokens.shape[1]
    rows = tokens.shape[0]
    dp = lax.axis_index("dp")
    place = jnp.stack([dp, lax.axis_index("expert")]).astype(jnp.int32)

    def swap(array, mask):
        return lax.ppermute(array, "expert", [(i, i ^ mask) for i in range(experts)])

    def swap_core(array):
        return lax.ppermute(array, "dp", [(0, 1), (1, 0)])

    sets = experts // 4
    grad_rows = pack_grad(grad_out, expert_ids, router_weights, experts)

    own_t = [tokens] + [swap(tokens, 4 * r) for r in range(1, sets)]
    own_g = [grad_rows] + [swap(grad_rows, 4 * r) for r in range(1, sets)]
    all_t, all_g = [], []
    for r in range(sets):
        t_x, t_y = swap(own_t[r], 1), swap(own_t[r], 2)
        g_x, g_y = swap(own_g[r], 1), swap(own_g[r], 2)
        if r % 2 == 0:
            t_d, g_d = swap(t_x, 2), swap(g_y, 1)
        else:
            t_d, g_d = swap(all_t[r - 1][3], 4), swap(all_g[r - 1][3], 4)
        all_t.append((own_t[r], t_x, t_y, t_d))
        all_g.append((own_g[r], g_x, g_y, g_d))

    share_in = clip_in.shape[3] // 2
    share_out = width // 2
    shares = (
        lax.dynamic_slice_in_dim(clip_in[0], dp * share_in, share_in, 2),
        lax.dynamic_slice_in_dim(range_in[0], dp * share_in, share_in, 2),
        lax.dynamic_slice_in_dim(clip_out[0], dp * share_out, share_out, 2),
        lax.dynamic_slice_in_dim(range_out[0], dp * share_out, share_out, 2),
    )
    gu_mine, d_mine = make_weights(codes_in[0], codes_out[0], *shares)
    weights = (gu_mine, swap_core(gu_mine), d_mine, swap_core(d_mine))

    sums = [jnp.zeros(s, F32) for s in 2 * ((2, 2, share_in, clip_in.shape[4]), (2, clip_out.shape[2], share_out))]
    partials = []
    for r in range(sets):
        parts, stored = run_set(place, all_t[r], all_g[r], weights, experts)
        partials.append(list(parts))
        sums = run_sums(place, stored, weights, sums)

    cut = rows // 2
    for r in range(1, sets, 2):
        partials[r - 1][3] = added(partials[r - 1][3], swap(partials[r][3], 4))
    final = None
    for r in [*range(1, sets), 0]:
        own, p_x, p_y, p_d = partials[r]
        if r % 2 == 0:
            over_x, over_y = swap(p_d[:cut], 1), swap(p_d[cut:], 2)
            p_y = jnp.concatenate([added(p_y[:cut], over_x), p_y[cut:]], axis=0)
            p_x = jnp.concatenate([p_x[:cut], added(p_x[cut:], over_y)], axis=0)
        got = (own, swap(p_x, 1), swap(p_y, 2))
        if r == 0:
            final = got if final is None else final + got
        else:
            final = (swap(added(*got), 4 * r),) + (() if final is None else final)
    grad_tokens = added(*final)

    got_in, got_out = swap_core(sums[2]), swap_core(sums[3])
    grad_in, grad_clip_out = clip_gradients((sums[0], got_in, sums[1], got_out), shares)
    return grad_tokens, grad_in[None], grad_clip_out[None]


def solution(mesh):
    return jax.shard_map(
        body,
        mesh=mesh,
        in_specs=(
            P(("expert", "dp"), None),
            P(("expert", "dp"), None),
            P(("expert", "dp"), None),
            P(("expert", "dp"), None),
            P("expert", None, "dp", None),
            P("expert", None, "dp"),
            P("expert", None, None, None, None),
            P("expert", None, None, None, None),
            P("expert", None, None, None),
            P("expert", None, None, None),
        ),
        out_specs=(
            P(("expert", "dp"), None),
            P("expert", None, None, "dp", None),
            P("expert", None, None, "dp"),
        ),
        check_vma=False,
    )
```

```python
import functools

import jax
import jax.numpy as jnp
from jax import lax
from jax.experimental import pallas as pl
from jax.experimental.pallas import tpu as pltpu
from jax.sharding import PartitionSpec as P

GROUP = 128
PACK = 3
CHUNK = 16
TILE = 256
LIMIT = 56 * 1024 * 1024
F32 = jnp.float32
BF16 = jnp.bfloat16


def dot_nn(a, b):
    return lax.dot_general(a, b, (((1,), (0,)), ((), ())), preferred_element_type=F32)


def dot_nt(a, b):
    return lax.dot_general(a, b, (((1,), (1,)), ((), ())), preferred_element_type=F32)


def dot_tn(a, b):
    return lax.dot_general(a, b, (((0,), (0,)), ((), ())), preferred_element_type=F32)


def sigmoid(v):
    return 1.0 / (1.0 + jnp.exp(-v))


def plane_order(size):
    third = size // PACK
    row = lax.broadcasted_iota(jnp.int32, (size, size), 0)
    col = lax.broadcasted_iota(jnp.int32, (size, size), 1)
    plane = jnp.zeros_like(col)
    for j in range(1, PACK):
        plane = plane + (col >= j * third).astype(jnp.int32)
    return (row == PACK * (col - plane * third) + plane).astype(F32).astype(BF16)


def three_parts(a):
    high = a.astype(BF16)
    rest = a - high.astype(F32)
    middle = rest.astype(BF16)
    low = (rest - middle.astype(F32)).astype(BF16)
    return high, middle, low


def placed(a, order, contract):
    parts = [contract(part, order) for part in three_parts(a)]
    return parts[0] + parts[1] + parts[2]


def whole_spec(shape):
    zeros = (0,) * len(shape)
    return pl.BlockSpec(shape, lambda *_: zeros)


ANYWHERE = pl.BlockSpec(memory_space=pl.ANY)


def pack_kernel(experts, token_ref, grad_ref, ids_ref, weights_ref, out_ref):
    rows, width = grad_ref.shape
    extra = out_ref.shape[1] - 2 * width
    out_ref[:, :width] = token_ref[...]
    out_ref[:, width : 2 * width] = grad_ref[...]
    lane = lax.broadcasted_iota(jnp.int32, (rows, extra), 1)
    part = lane // experts
    expert = lane - part * experts
    table = jnp.zeros((rows, extra), F32)
    for k in range(ids_ref.shape[1]):
        table = table + jnp.where(ids_ref[:, k : k + 1] == expert, weights_ref[:, k : k + 1], 0.0)
    high, middle, low = three_parts(table)
    out_ref[:, 2 * width :] = jnp.where(
        part == 0,
        high.astype(F32),
        jnp.where(part == 1, middle.astype(F32), low.astype(F32)),
    ).astype(BF16)


def pack_rows(tokens, grad_out, expert_ids, router_weights, experts):
    rows, width = grad_out.shape
    extra = -(-3 * experts // 128) * 128
    return pl.pallas_call(
        functools.partial(pack_kernel, experts),
        out_shape=jax.ShapeDtypeStruct((rows, 2 * width + extra), BF16),
        name="pack_rows",
    )(tokens, grad_out, expert_ids, router_weights)


def weight_kernel(
    place, codes_in, codes_out, clip_in, range_in, clip_out, range_out, after, gu_ref, d_ref, ends
):
    del place, after
    hidden = clip_in.shape[3]
    third = hidden // PACK
    groups = clip_in.shape[2]
    t = pl.program_id(0)
    here = codes_in.shape[1] // GROUP

    @pl.when(t == 0)
    def _():
        order = plane_order(hidden)
        for p in range(2):
            upper = sigmoid(clip_in[p, 0]) * range_in[p, 0]
            lower = sigmoid(clip_in[p, 1]) * range_in[p, 1]
            ends[p] = placed(jnp.concatenate([(upper + lower) / 15.0, lower], axis=0), order, dot_nn)

    for p in range(2):
        for g in range(here):
            packed = codes_in[p, g * GROUP : (g + 1) * GROUP, :]
            step_row = ends[p, pl.ds(t * here + g, 1), :]
            lower_row = ends[p, pl.ds(groups + t * here + g, 1), :]
            for j in range(PACK):
                code = jnp.bitwise_and(jnp.right_shift(packed, 4 * j), 15).astype(F32)
                cols = slice(j * third, (j + 1) * third)
                gu_ref[p, g * GROUP : (g + 1) * GROUP, cols] = (
                    step_row[:, cols] * code - lower_row[:, cols]
                ).astype(BF16)
    upper = sigmoid(clip_out[0]) * range_out[0]
    lower = sigmoid(clip_out[1]) * range_out[1]
    step = (upper + lower) / 15.0
    row = lax.broadcasted_iota(jnp.int32, (CHUNK, 1), 0)
    for start in range(0, third, CHUNK):
        packed = codes_out[start : start + CHUNK, :]
        for j in range(PACK):
            first = (PACK * start + j) // GROUP
            last = (PACK * (start + CHUNK - 1) + j) // GROUP
            step_rows, lower_rows = step[first : first + 1], lower[first : first + 1]
            for g in range(first + 1, last + 1):
                late = PACK * (row + start) + j >= g * GROUP
                step_rows = jnp.where(late, step[g : g + 1], step_rows)
                lower_rows = jnp.where(late, lower[g : g + 1], lower_rows)
            code = jnp.bitwise_and(jnp.right_shift(packed, 4 * j), 15).astype(F32)
            d_ref[j * third + start : j * third + start + CHUNK, :] = (
                step_rows * code - lower_rows
            ).astype(BF16)


def make_weights(place, codes_in, codes_out, clips, after):
    clip_in, range_in, clip_out, range_out = clips
    depth, third = codes_in.shape[1:]
    hidden = clip_in.shape[3]
    share = clip_in.shape[2] // 2
    steps = depth // TILE
    in_clip = pl.BlockSpec((2, 2, share, hidden), lambda t, place: (0, 0, place[0], 0))
    out_clip = pl.BlockSpec((2, clip_out.shape[1], TILE), lambda t, place: (0, 0, place[0] * steps + t))
    return pl.pallas_call(
        weight_kernel,
        grid_spec=pltpu.PrefetchScalarGridSpec(
            num_scalar_prefetch=1,
            grid=(steps,),
            in_specs=[
                pl.BlockSpec((2, TILE, third), lambda t, *_: (0, t, 0)),
                pl.BlockSpec((third, TILE), lambda t, *_: (0, t)),
                in_clip,
                in_clip,
                out_clip,
                out_clip,
                ANYWHERE,
            ],
            out_specs=[
                pl.BlockSpec((2, TILE, hidden), lambda t, *_: (0, t, 0)),
                pl.BlockSpec((hidden, TILE), lambda t, *_: (0, t)),
            ],
            scratch_shapes=[pltpu.VMEM((2, 2 * share, hidden), F32)],
        ),
        out_shape=(
            jax.ShapeDtypeStruct((2, depth, hidden), BF16),
            jax.ShapeDtypeStruct((hidden, depth), BF16),
        ),
        compiler_params=pltpu.CompilerParams(vmem_limit_bytes=LIMIT),
        cost_estimate=pl.CostEstimate(flops=10**7, bytes_accessed=10**7, transcendentals=0),
        name="make_weights",
    )(place, codes_in, codes_out, clip_in, range_in, clip_out, range_out, after)


def set_kernel(experts, place, *refs):
    blocks = refs[0:4]
    gu_sides, d_sides = refs[4:6], refs[6:8]
    partials = refs[8:12]
    x_ref, s_ref, h_ref, g_ref = refs[12:16]
    gu_held, d_held, arrived = refs[16:19]
    rows, width = partials[0].shape
    half = width // 2
    hidden = h_ref.shape[1]
    third = hidden // PACK
    spans = (
        pl.ds(pl.multiple_of(place[0] * half, half), half),
        pl.ds(pl.multiple_of((1 - place[0]) * half, half), half),
    )

    def chunk(j):
        cols = pl.ds(j * third, third)
        copies = []
        for side in range(2):
            copies.append(
                pltpu.make_async_copy(
                    gu_sides[side].at[:, :, cols], gu_held.at[side, :, :, cols], arrived.at[j, side]
                )
            )
            copies.append(
                pltpu.make_async_copy(d_sides[side].at[cols, :], d_held.at[side, cols, :], arrived.at[j, 2 + side])
            )
        return copies

    for j in range(PACK):
        for copy in chunk(j):
            copy.start()
    for i in range(4):
        span = slice(i * rows, (i + 1) * rows)
        x_ref[span, :] = blocks[i][:, :width]
        beside = blocks[i][:, 2 * width :].astype(F32)
        lane = lax.broadcasted_iota(jnp.int32, beside.shape, 1)
        keep = (lane == place[1]) | (lane == place[1] + experts) | (lane == place[1] + 2 * experts)
        scale = jnp.sum(jnp.where(keep, beside, 0.0), axis=1, keepdims=True)
        s_ref[span, :] = (scale * blocks[i][:, width : 2 * width].astype(F32)).astype(BF16)
    for j in range(PACK):
        for copy in chunk(j):
            copy.wait()
        cols = slice(j * third, (j + 1) * third)
        gate_pre = dot_nn(x_ref[:, spans[0]], gu_held[0, 0, :, cols]) + dot_nn(
            x_ref[:, spans[1]], gu_held[1, 0, :, cols]
        )
        up_pre = dot_nn(x_ref[:, spans[0]], gu_held[0, 1, :, cols]) + dot_nn(
            x_ref[:, spans[1]], gu_held[1, 1, :, cols]
        )
        grad_hidden = dot_nt(s_ref[:, spans[0]], d_held[0, cols, :]) + dot_nt(
            s_ref[:, spans[1]], d_held[1, cols, :]
        )
        sig = sigmoid(gate_pre)
        act = gate_pre * sig
        h_ref[:, cols] = (act * up_pre).astype(BF16)
        g_ref[0, :, cols] = (grad_hidden * up_pre * sig * (1.0 + gate_pre * (1.0 - sig))).astype(BF16)
        g_ref[1, :, cols] = (grad_hidden * act).astype(BF16)
    for side in range(2):
        base = jnp.where(side == 0, place[0], 1 - place[0]) * half

        @pl.loop(0, half // TILE)
        def _(n):
            depth = pl.ds(pl.multiple_of(n * TILE, TILE), TILE)
            part = dot_nt(g_ref[0], gu_held[side, 0, depth, :]) + dot_nt(g_ref[1], gu_held[side, 1, depth, :])
            cols = pl.ds(pl.multiple_of(base + n * TILE, TILE), TILE)
            for i in range(4):
                partials[i][:, cols] = part[i * rows : (i + 1) * rows, :].astype(BF16)


def run_set(place, blocks, weights, experts):
    rows = blocks[0].shape[0]
    gu_mine, gu_other, d_mine, d_other = weights
    hidden, half = d_mine.shape
    width = 2 * half
    all_rows = 4 * rows
    wide = jax.ShapeDtypeStruct((all_rows, width), BF16)
    stored = [
        wide,
        wide,
        jax.ShapeDtypeStruct((all_rows, hidden), BF16),
        jax.ShapeDtypeStruct((2, all_rows, hidden), BF16),
    ]
    part = jax.ShapeDtypeStruct((rows, width), BF16)
    out = pl.pallas_call(
        functools.partial(set_kernel, experts),
        grid_spec=pltpu.PrefetchScalarGridSpec(
            num_scalar_prefetch=1,
            grid=(1,),
            in_specs=[whole_spec(b.shape) for b in blocks] + [ANYWHERE] * 4,
            out_specs=[whole_spec(part.shape)] * 4 + [whole_spec(a.shape) for a in stored],
            scratch_shapes=[
                pltpu.VMEM((2, 2, half, hidden), BF16),
                pltpu.VMEM((2, hidden, half), BF16),
                pltpu.SemaphoreType.DMA((PACK, 4)),
            ],
        ),
        out_shape=[part] * 4 + stored,
        compiler_params=pltpu.CompilerParams(vmem_limit_bytes=LIMIT),
        cost_estimate=pl.CostEstimate(
            flops=10 * all_rows * width * hidden,
            bytes_accessed=6 * width * hidden + 16 * all_rows * width,
            transcendentals=all_rows * hidden,
        ),
        name="expert_set",
    )(place, *blocks, gu_mine, gu_other, d_mine, d_other)
    return list(out[:4]), out[4:]


def group_marks(size, count, span, planes):
    row = lax.broadcasted_iota(jnp.int32, (size, count), 0)
    group = lax.broadcasted_iota(jnp.int32, (size, count), 1)
    if planes > 1:
        third = size // planes
        plane = jnp.zeros_like(row)
        for j in range(1, planes):
            plane = plane + (row >= j * third).astype(jnp.int32)
        row = planes * (row - plane * third) + plane
    return ((row >= group * span) & (row < (group + 1) * span)).astype(F32).astype(BF16)


def two_parts(a):
    high = a.astype(BF16)
    return high, (a - high.astype(F32)).astype(BF16)


def sums_kernel(place, *refs):
    x_ref, s_ref, h_ref, g_ref = refs[0:4]
    weights_in, weights_out = refs[4:6], refs[6:8]
    before, outs = refs[8:12], refs[12:16]
    t = pl.program_id(0)
    width = x_ref.shape[1]
    half = width // 2
    hidden = h_ref.shape[1]
    third = hidden // PACK
    share = outs[0].shape[2]
    groups_out = outs[1].shape[1]

    @pl.when(t == 0)
    def _():
        marks = group_marks(half, share, GROUP, 1)
        hidden_sums = two_parts(dot_nn(h_ref[...], group_marks(hidden, groups_out, GROUP, PACK)))
        for side in range(2):
            base = jnp.where(side == 0, place[0], 1 - place[0]) * half
            span = pl.ds(pl.multiple_of(base, half), half)
            row_sums = two_parts(dot_nn(x_ref[:, span], marks))
            for p in range(2):
                outs[2 * side][p, 1] = (
                    before[2 * side][p, 1] + dot_tn(row_sums[0], g_ref[p]) + dot_tn(row_sums[1], g_ref[p])
                )
            outs[2 * side + 1][1] = (
                before[2 * side + 1][1]
                + dot_tn(hidden_sums[0], s_ref[:, span])
                + dot_tn(hidden_sums[1], s_ref[:, span])
            )

    for side in range(2):
        base = jnp.where(side == 0, place[0], 1 - place[0]) * half + t * TILE
        span = pl.ds(pl.multiple_of(base, TILE), TILE)
        sums_in, sums_out = outs[2 * side], outs[2 * side + 1]
        old_in, old_out = before[2 * side], before[2 * side + 1]
        x_cols = x_ref[:, span]
        for p in range(2):
            weighted = dot_tn(x_cols, g_ref[p]) * weights_in[side][p].astype(F32)
            for g in range(TILE // GROUP):
                spot = pl.ds(t * (TILE // GROUP) + g, 1)
                found = jnp.sum(weighted[g * GROUP : (g + 1) * GROUP], axis=0, keepdims=True)
                sums_in[p, 0, spot, :] = old_in[p, 0, spot, :] + found
        weighted = dot_tn(h_ref[...], s_ref[:, span]) * weights_out[side][...].astype(F32)
        cols = pl.ds(pl.multiple_of(t * TILE, TILE), TILE)
        for g in range(groups_out):
            found = old_out[0, g : g + 1, cols]
            for j in range(PACK):
                low = -((j - GROUP * g) // PACK)
                high = -((j - GROUP * (g + 1)) // PACK)
                inner, outer = -(-low // 8) * 8, high // 8 * 8
                found = found + jnp.sum(
                    weighted[j * third + inner : j * third + outer], axis=0, keepdims=True
                )
                for start in ({low // 8 * 8} if low % 8 else set()) | ({outer} if high % 8 else set()):
                    block = weighted[j * third + start : j * third + start + 8]
                    row = lax.broadcasted_iota(jnp.int32, block.shape, 0) + start
                    inside = (row >= low) & (row < high)
                    found = found + jnp.sum(jnp.where(inside, block, 0.0), axis=0, keepdims=True)
            sums_out[0, g : g + 1, cols] = found


def run_sums(place, stored, weights, before):
    x, s, h, g = stored
    gu_mine, gu_other, d_mine, d_other = weights
    all_rows, width = x.shape
    hidden = h.shape[1]
    half = width // 2
    in_spec = pl.BlockSpec((2, TILE, hidden), lambda t, *_: (0, t, 0))
    out_spec = pl.BlockSpec((hidden, TILE), lambda t, *_: (0, t))
    return pl.pallas_call(
        sums_kernel,
        grid_spec=pltpu.PrefetchScalarGridSpec(
            num_scalar_prefetch=1,
            grid=(half // TILE,),
            in_specs=[whole_spec(a.shape) for a in stored]
            + [in_spec, in_spec, out_spec, out_spec]
            + [whole_spec(b.shape) for b in before],
            out_specs=[whole_spec(b.shape) for b in before],
        ),
        out_shape=[jax.ShapeDtypeStruct(b.shape, F32) for b in before],
        compiler_params=pltpu.CompilerParams(vmem_limit_bytes=LIMIT),
        cost_estimate=pl.CostEstimate(
            flops=6 * all_rows * width * hidden,
            bytes_accessed=6 * width * hidden + 4 * all_rows * width,
            transcendentals=0,
        ),
        name="group_sums",
    )(place, x, s, h, g, gu_mine, gu_other, d_mine, d_other, *before)


def clip_kernel(
    place, mine_in, got_in, mine_out, got_out, clip_in, range_in, clip_out, range_out, in_ref, out_ref
):
    del place
    hidden = clip_in.shape[3]
    groups = clip_in.shape[2]
    order = plane_order(hidden)

    def finish(weighted, plain, clip, span):
        sig_upper, sig_lower = sigmoid(clip[0]), sigmoid(clip[1])
        upper, lower = sig_upper * span[0], sig_lower * span[1]
        upper_sum = (weighted + lower * plain) / (upper + lower)
        lower_sum = upper_sum - plain
        return (
            upper_sum * span[0] * sig_upper * (1.0 - sig_upper),
            lower_sum * span[1] * sig_lower * (1.0 - sig_lower),
        )

    for p in range(2):
        sums = jnp.concatenate(
            [mine_in[p, 0] + got_in[p, 0], mine_in[p, 1] + got_in[p, 1]], axis=0
        )
        natural = placed(sums, order, dot_nt)
        in_ref[p, 0], in_ref[p, 1] = finish(
            natural[:groups], natural[groups:], (clip_in[p, 0], clip_in[p, 1]), (range_in[p, 0], range_in[p, 1])
        )
    out_ref[0], out_ref[1] = finish(
        mine_out[0] + got_out[0],
        mine_out[1] + got_out[1],
        (clip_out[0], clip_out[1]),
        (range_out[0], range_out[1]),
    )


def clip_gradients(place, sums, clips):
    in_shape, out_shape = sums[0].shape, sums[2].shape
    in_clip = pl.BlockSpec(in_shape, lambda t, place: (0, 0, place[0], 0))
    out_clip = pl.BlockSpec(out_shape, lambda t, place: (0, 0, place[0]))
    return pl.pallas_call(
        clip_kernel,
        grid_spec=pltpu.PrefetchScalarGridSpec(
            num_scalar_prefetch=1,
            grid=(1,),
            in_specs=[whole_spec(a.shape) for a in sums] + [in_clip, in_clip, out_clip, out_clip],
            out_specs=[whole_spec(in_shape), whole_spec(out_shape)],
        ),
        out_shape=(
            jax.ShapeDtypeStruct(in_shape, F32),
            jax.ShapeDtypeStruct(out_shape, F32),
        ),
        compiler_params=pltpu.CompilerParams(vmem_limit_bytes=LIMIT),
        name="clip_gradients",
    )(place, *sums, *clips)


def added(*parts):
    return sum(part.astype(F32) for part in parts).astype(BF16)


def body(
    tokens,
    grad_out,
    expert_ids,
    router_weights,
    codes_in,
    codes_out,
    clip_in,
    range_in,
    clip_out,
    range_out,
):
    experts = lax.axis_size("expert")
    width = tokens.shape[1]
    dp = lax.axis_index("dp")
    place = jnp.stack([dp, lax.axis_index("expert")]).astype(jnp.int32)

    def swap(array, mask):
        return lax.ppermute(array, "expert", [(i, i ^ mask) for i in range(experts)])

    def swap_core(array):
        return lax.ppermute(array, "dp", [(0, 1), (1, 0)])

    sets = experts // 4
    packed = pack_rows(tokens, grad_out, expert_ids, router_weights, experts)
    clips = (clip_in[0], range_in[0], clip_out[0], range_out[0])
    gu_mine, d_mine = make_weights(place, codes_in[0], codes_out[0], clips, packed)
    weights = (gu_mine, swap_core(gu_mine), d_mine, swap_core(d_mine))

    order = [0] + [r for r in range(sets) if r % 4 > 1] + [r for r in range(1, sets) if r % 4 < 2]
    blocks, heads = {}, {0: packed}
    for r in order:
        if r not in heads:
            heads[r] = swap(packed, 4 * r) if r % 2 == 0 or r == 1 else swap(heads[r - 1], 4)
        own = heads[r]
        over_x, over_y = swap(own, 1), swap(own, 2)
        if r % 2 == 1:
            diagonal = swap(blocks[r - 1][3], 4)
        elif r % 4 == 0:
            diagonal = swap(over_x, 2)
        else:
            diagonal = swap(over_y, 1)
        blocks[r] = (own, over_x, over_y, diagonal)

    share_in, share_out = clip_in.shape[3] // 2, width // 2
    sums = [
        jnp.zeros(s, F32)
        for s in 2 * ((2, 2, share_in, clip_in.shape[4]), (2, clip_out.shape[2], share_out))
    ]
    partials = {}
    for r in order:
        partials[r], stored = run_set(place, blocks[r], weights, experts)
        sums = run_sums(place, stored, weights, sums)

    final = ()
    for r in [r for r in order if r % 2 == 0 and r > 0] + [0]:
        _, _, _, far = partials[r + 1]
        own, p_x, p_y, p_d = partials[r]
        p_d = added(p_d, swap(far, 4))
        if r % 4 == 0:
            p_x = added(p_x, swap(p_d, 2))
        else:
            p_y = added(p_y, swap(p_d, 1))
        odd, odd_x, odd_y, _ = partials[r + 1]
        beside = swap(added(odd, swap(odd_x, 1), swap(odd_y, 2)), 4)
        got = (own, swap(p_x, 1), swap(p_y, 2), beside)
        final = (swap(added(*got), 4 * r),) + final if r else got + final
    grad_tokens = added(*final)

    got_in, got_out = swap_core(sums[2]), swap_core(sums[3])
    grad_in, grad_clip_out = clip_gradients(place, (sums[0], got_in, sums[1], got_out), clips)
    return grad_tokens, grad_in[None], grad_clip_out[None]


def solution(mesh):
    return jax.shard_map(
        body,
        mesh=mesh,
        in_specs=(
            P(("expert", "dp"), None),
            P(("expert", "dp"), None),
            P(("expert", "dp"), None),
            P(("expert", "dp"), None),
            P("expert", None, "dp", None),
            P("expert", None, "dp"),
            P("expert", None, None, None, None),
            P("expert", None, None, None, None),
            P("expert", None, None, None),
            P("expert", None, None, None),
        ),
        out_specs=(
            P(("expert", "dp"), None),
            P("expert", None, None, "dp", None),
            P("expert", None, None, "dp"),
        ),
        check_vma=False,
    )
```

```python
import functools

import jax
import jax.numpy as jnp
from jax import lax
from jax.experimental import pallas as pl
from jax.experimental.pallas import tpu as pltpu
from jax.sharding import PartitionSpec as P

GROUP = 128
PACK = 3
CHUNK = 16
TILE = 256
LIMIT = 24 * 1024 * 1024
SMALL = 8 * 1024 * 1024
F32 = jnp.float32
BF16 = jnp.bfloat16


def dot_nn(a, b):
    return lax.dot_general(a, b, (((1,), (0,)), ((), ())), preferred_element_type=F32)


def dot_nt(a, b):
    return lax.dot_general(a, b, (((1,), (1,)), ((), ())), preferred_element_type=F32)


def dot_tn(a, b):
    return lax.dot_general(a, b, (((0,), (0,)), ((), ())), preferred_element_type=F32)


def sigmoid(v):
    return 1.0 / (1.0 + jnp.exp(-v))


def plane_order(size, back=False):
    third = size // PACK
    row = lax.broadcasted_iota(jnp.int32, (size, size), 1 if back else 0)
    col = lax.broadcasted_iota(jnp.int32, (size, size), 0 if back else 1)
    plane = jnp.zeros_like(col)
    for j in range(1, PACK):
        plane = plane + (col >= j * third).astype(jnp.int32)
    return (row == PACK * (col - plane * third) + plane).astype(F32).astype(BF16)


def three_parts(a):
    high = a.astype(BF16)
    rest = a - high.astype(F32)
    middle = rest.astype(BF16)
    low = (rest - middle.astype(F32)).astype(BF16)
    return high, middle, low


def placed(a, order):
    parts = [dot_nn(part, order) for part in three_parts(a)]
    return parts[0] + parts[1] + parts[2]


ANYWHERE = pl.BlockSpec(memory_space=pl.ANY)
INSIDE = pl.BlockSpec(memory_space=pltpu.VMEM)


class Calls:
    def __init__(self, keep):
        self.keep = keep

    def pin(self, array):
        return pltpu.with_memory_space_constraint(array, pltpu.VMEM) if self.keep else array

    def out(self, shape, dtype):
        return pltpu.VMEM(shape, dtype) if self.keep else jax.ShapeDtypeStruct(shape, dtype)

    def run(self, kernel, name, inputs, outputs, after=(), alias=None, limit=LIMIT, flops=0, free=()):
        count = len(inputs)

        def wrapped(*refs):
            kernel(*refs[:count], *refs[count + len(after) :])

        return pl.pallas_call(
            wrapped,
            in_specs=[INSIDE] * count + [ANYWHERE] * len(after),
            out_specs=[INSIDE] * len(outputs),
            out_shape=[
                jax.ShapeDtypeStruct(shape, dtype) if i in free else self.out(shape, dtype)
                for i, (shape, dtype) in enumerate(outputs)
            ],
            input_output_aliases=alias or {},
            compiler_params=pltpu.CompilerParams(vmem_limit_bytes=limit),
            cost_estimate=pl.CostEstimate(flops=flops, bytes_accessed=10**6, transcendentals=0),
            name=name,
        )(*[self.pin(a) for a in inputs], *after)


def pack_kernel(experts, token_ref, grad_ref, ids_ref, weights_ref, out_ref):
    rows, width = grad_ref.shape
    extra = out_ref.shape[1] - 2 * width
    out_ref[:, :width] = token_ref[...]
    out_ref[:, width : 2 * width] = grad_ref[...]
    line = lax.broadcasted_iota(jnp.int32, (extra, rows), 0)
    part = sum((line >= i * experts).astype(jnp.int32) for i in range(1, 4))
    expert = jnp.where(part < 3, line - part * experts, -1)
    table = jnp.zeros((extra, rows), F32)
    for k in range(ids_ref.shape[0]):
        table = table + jnp.where(ids_ref[k : k + 1, :] == expert, weights_ref[k : k + 1, :], 0.0)
    high, middle, low = three_parts(table)
    split = jnp.where(
        part == 0,
        high.astype(F32),
        jnp.where(part == 1, middle.astype(F32), low.astype(F32)),
    ).astype(BF16)
    same = lax.broadcasted_iota(jnp.int32, (extra, extra), 0) == lax.broadcasted_iota(jnp.int32, (extra, extra), 1)
    out_ref[:, 2 * width :] = dot_tn(split, same.astype(F32).astype(BF16)).astype(BF16)


def weight_kernel(codes_in, codes_out, clip_in, range_in, clip_out, range_out, gu_ref, d_ref):
    dp = lax.axis_index("dp")
    depth, third = codes_in.shape[1:]
    hidden = clip_in.shape[3]
    groups = depth // GROUP
    own = pl.ds(pl.multiple_of(dp * groups, groups), groups)
    order = plane_order(hidden)
    for p in range(2):
        upper = sigmoid(clip_in[p, 0, own, :]) * range_in[p, 0, own, :]
        lower = sigmoid(clip_in[p, 1, own, :]) * range_in[p, 1, own, :]
        ends = placed(jnp.concatenate([(upper + lower) / 15.0, lower], axis=0), order)
        for g in range(groups):
            packed = codes_in[p, g * GROUP : (g + 1) * GROUP, :]
            for j in range(PACK):
                code = jnp.bitwise_and(jnp.right_shift(packed, 4 * j), 15).astype(F32)
                cols = slice(j * third, (j + 1) * third)
                gu_ref[p, g * GROUP : (g + 1) * GROUP, cols] = (
                    ends[g : g + 1, cols] * code - ends[groups + g : groups + g + 1, cols]
                ).astype(BF16)
    own = pl.ds(pl.multiple_of(dp * depth, depth), depth)
    step, lower = [], []
    for g in range(clip_out.shape[0]):
        upper_end = sigmoid(clip_out[g, 0:1, own]) * range_out[g, 0:1, own]
        lower_end = sigmoid(clip_out[g, 1:2, own]) * range_out[g, 1:2, own]
        step.append((upper_end + lower_end) / 15.0)
        lower.append(lower_end)
    row = lax.broadcasted_iota(jnp.int32, (CHUNK, 1), 0)
    for start in range(0, third, CHUNK):
        packed = codes_out[start : start + CHUNK, :]
        for j in range(PACK):
            first = (PACK * start + j) // GROUP
            last = (PACK * (start + CHUNK - 1) + j) // GROUP
            step_rows, lower_rows = step[first], lower[first]
            for g in range(first + 1, last + 1):
                late = PACK * (row + start) + j >= g * GROUP
                step_rows = jnp.where(late, step[g], step_rows)
                lower_rows = jnp.where(late, lower[g], lower_rows)
            code = jnp.bitwise_and(jnp.right_shift(packed, 4 * j), 15).astype(F32)
            d_ref[j * third + start : j * third + start + CHUNK, :] = (
                step_rows * code - lower_rows
            ).astype(BF16)


def set_kernel(experts, first, *refs):
    blocks = refs[0:4]
    gu_sides, d_sides = refs[4:6], refs[6:8]
    refs = refs[8:] if first == 0 else refs[12:]
    partials = refs[0:4]
    x_ref, s_ref, h_ref, g_ref = refs[4:8]
    rows, width = partials[0].shape
    half = width // 2
    hidden = h_ref.shape[1]
    third = hidden // PACK
    dp, mine = lax.axis_index("dp"), lax.axis_index("expert")
    spans = (
        pl.ds(pl.multiple_of(dp * half, half), half),
        pl.ds(pl.multiple_of((1 - dp) * half, half), half),
    )
    here = slice(first, first + 4 * rows)
    for i in range(4):
        span = slice(first + i * rows, first + (i + 1) * rows)
        x_ref[span, :] = blocks[i][:, :width]
        beside = blocks[i][:, 2 * width :].astype(F32)
        lane = lax.broadcasted_iota(jnp.int32, beside.shape, 1)
        keep = (lane == mine) | (lane == mine + experts) | (lane == mine + 2 * experts)
        scale = jnp.sum(jnp.where(keep, beside, 0.0), axis=1, keepdims=True)
        s_ref[span, :] = (scale * blocks[i][:, width : 2 * width].astype(F32)).astype(BF16)
    for j in range(PACK):
        cols = slice(j * third, (j + 1) * third)
        gate_pre = dot_nn(x_ref[here, spans[0]], gu_sides[0][0, :, cols]) + dot_nn(
            x_ref[here, spans[1]], gu_sides[1][0, :, cols]
        )
        up_pre = dot_nn(x_ref[here, spans[0]], gu_sides[0][1, :, cols]) + dot_nn(
            x_ref[here, spans[1]], gu_sides[1][1, :, cols]
        )
        grad_hidden = dot_nt(s_ref[here, spans[0]], d_sides[0][cols, :]) + dot_nt(
            s_ref[here, spans[1]], d_sides[1][cols, :]
        )
        sig = sigmoid(gate_pre)
        act = gate_pre * sig
        h_ref[here, cols] = (act * up_pre).astype(BF16)
        g_ref[0, here, cols] = (grad_hidden * up_pre * sig * (1.0 + gate_pre * (1.0 - sig))).astype(BF16)
        g_ref[1, here, cols] = (grad_hidden * act).astype(BF16)
    for side in range(2):
        base = jnp.where(side == 0, dp, 1 - dp) * half

        @pl.loop(0, half // TILE)
        def _(n):
            depth = pl.ds(pl.multiple_of(n * TILE, TILE), TILE)
            part = dot_nt(g_ref[0, here, :], gu_sides[side][0, depth, :]) + dot_nt(
                g_ref[1, here, :], gu_sides[side][1, depth, :]
            )
            cols = pl.ds(pl.multiple_of(base + n * TILE, TILE), TILE)
            for i in range(4):
                partials[i][:, cols] = part[i * rows : (i + 1) * rows, :].astype(BF16)


def run_set(calls, blocks, weights, experts, pair, after):
    rows, width = blocks[0].shape[0], 2 * weights[2].shape[1]
    hidden = weights[2].shape[0]
    both = 8 * rows
    stored = [((both, width), BF16), ((both, width), BF16), ((both, hidden), BF16), ((2, both, hidden), BF16)]
    out = calls.run(
        functools.partial(set_kernel, experts, 0 if pair is None else 4 * rows),
        "expert_set",
        [*blocks, *weights, *(pair or ())],
        [((rows, width), BF16)] * 4 + stored,
        after=after,
        alias=None if pair is None else {8 + i: 4 + i for i in range(4)},
        flops=40 * rows * width * hidden,
    )
    return list(out[:4]), list(out[4:])


def group_marks(size, count, span, planes):
    row = lax.broadcasted_iota(jnp.int32, (size, count), 0)
    group = lax.broadcasted_iota(jnp.int32, (size, count), 1)
    if planes > 1:
        third = size // planes
        plane = jnp.zeros_like(row)
        for j in range(1, planes):
            plane = plane + (row >= j * third).astype(jnp.int32)
        row = planes * (row - plane * third) + plane
    return ((row >= group * span) & (row < (group + 1) * span)).astype(F32).astype(BF16)


def two_parts(a):
    high = a.astype(BF16)
    return high, (a - high.astype(F32)).astype(BF16)


def sums_kernel(other, more, x_ref, s_ref, h_ref, g_ref, weights_in, weights_out, *refs):
    old_in, old_out = refs[:2] if more else (None, None)
    sums_in, sums_out = refs[-2:]
    width = x_ref.shape[1]
    half = width // 2
    hidden = h_ref.shape[1]
    third = hidden // PACK
    share = sums_in.shape[2]
    groups_out = sums_out.shape[1]
    dp = lax.axis_index("dp")
    base = (1 - dp if other else dp) * half
    span = pl.ds(pl.multiple_of(base, half), half)

    def since(old, found, *where):
        return old[where] + found if more else found

    row_sums = two_parts(dot_nn(x_ref[:, span], group_marks(half, share, GROUP, 1)))
    for p in range(2):
        found = dot_tn(row_sums[0], g_ref[p]) + dot_tn(row_sums[1], g_ref[p])
        sums_in[p, 1] = since(old_in, found, p, 1)
    hidden_sums = two_parts(dot_nn(h_ref[...], group_marks(hidden, groups_out, GROUP, PACK)))
    found = dot_tn(hidden_sums[0], s_ref[:, span]) + dot_tn(hidden_sums[1], s_ref[:, span])
    sums_out[1] = since(old_out, found, 1)

    @pl.loop(0, half // TILE)
    def _(t):
        rows = pl.ds(pl.multiple_of(t * TILE, TILE), TILE)
        span = pl.ds(pl.multiple_of(base + t * TILE, TILE), TILE)
        x_cols = x_ref[:, span]
        for p in range(2):
            weighted = dot_tn(x_cols, g_ref[p]) * weights_in[p, rows, :].astype(F32)
            for g in range(TILE // GROUP):
                spot = pl.ds(t * (TILE // GROUP) + g, 1)
                found = jnp.sum(weighted[g * GROUP : (g + 1) * GROUP], axis=0, keepdims=True)
                sums_in[p, 0, spot, :] = since(old_in, found, p, 0, spot, slice(None))
        weighted = dot_tn(h_ref[...], s_ref[:, span]) * weights_out[:, rows].astype(F32)
        for g in range(groups_out):
            found = None
            for j in range(PACK):
                low = -((j - GROUP * g) // PACK)
                high = -((j - GROUP * (g + 1)) // PACK)
                inner, outer = -(-low // 8) * 8, high // 8 * 8
                part = jnp.sum(weighted[j * third + inner : j * third + outer], axis=0, keepdims=True)
                found = part if found is None else found + part
                for start in sorted(({low // 8 * 8} if low % 8 else set()) | ({outer} if high % 8 else set())):
                    block = weighted[j * third + start : j * third + start + 8]
                    row = lax.broadcasted_iota(jnp.int32, block.shape, 0) + start
                    inside = (row >= low) & (row < high)
                    found = found + jnp.sum(jnp.where(inside, block, 0.0), axis=0, keepdims=True)
            sums_out[0, g : g + 1, rows] = since(old_out, found, 0, slice(g, g + 1), rows)


def run_sums(calls, stored, weights, other, before, shapes, after):
    both, width = stored[0].shape
    hidden = stored[2].shape[1]
    side = weights[1::2] if other else weights[0::2]
    return calls.run(
        functools.partial(sums_kernel, other, before is not None),
        "group_sums",
        [*stored, *side, *(before or ())],
        [(shape, F32) for shape in shapes],
        after=after,
        flops=3 * both * width * hidden,
    )


def clip_kernel(mine_in, got_in, mine_out, got_out, clip_in, range_in, clip_out, range_out, in_ref, out_ref):
    dp = lax.axis_index("dp")
    hidden = clip_in.shape[3]
    groups = in_ref.shape[2]
    share = out_ref.shape[2]
    back = plane_order(hidden, True)

    def finish(weighted, plain, clip, span):
        sig_upper, sig_lower = sigmoid(clip[0]), sigmoid(clip[1])
        upper, lower = sig_upper * span[0], sig_lower * span[1]
        upper_sum = (weighted + lower * plain) / (upper + lower)
        lower_sum = upper_sum - plain
        return (
            upper_sum * span[0] * sig_upper * (1.0 - sig_upper),
            lower_sum * span[1] * sig_lower * (1.0 - sig_lower),
        )

    own = pl.ds(pl.multiple_of(dp * groups, groups), groups)
    for p in range(2):
        sums = jnp.concatenate(
            [mine_in[p, 0] + got_in[p, 0], mine_in[p, 1] + got_in[p, 1]], axis=0
        )
        natural = placed(sums, back)
        in_ref[p, 0], in_ref[p, 1] = finish(
            natural[:groups],
            natural[groups:],
            [clip_in[p, i, own, :] for i in range(2)],
            [range_in[p, i, own, :] for i in range(2)],
        )
    own = pl.ds(pl.multiple_of(dp * share, share), share)
    for g in range(out_ref.shape[0]):
        out_ref[g, 0:1, :], out_ref[g, 1:2, :] = finish(
            mine_out[0, g : g + 1, :] + got_out[0, g : g + 1, :],
            mine_out[1, g : g + 1, :] + got_out[1, g : g + 1, :],
            [clip_out[g, i : i + 1, own] for i in range(2)],
            [range_out[g, i : i + 1, own] for i in range(2)],
        )


def add_kernel(*refs):
    total = refs[0][...].astype(F32)
    for ref in refs[1:-1]:
        total = total + ref[...].astype(F32)
    refs[-1][...] = total.astype(refs[-1].dtype)


def body(
    tokens,
    grad_out,
    expert_ids,
    router_weights,
    codes_in,
    codes_out,
    clip_in,
    range_in,
    clip_out,
    range_out,
):
    experts = lax.axis_size("expert")
    rows, width = tokens.shape
    hidden = clip_in.shape[4]
    depth = codes_in.shape[2]
    extra = -(-3 * experts // 128) * 128
    sets = experts // 4
    calls = Calls(experts * rows * (3 * width + extra) * 2 < 2**24)

    def swap(array, mask):
        return lax.ppermute(array, "expert", [(i, i ^ mask) for i in range(experts)])

    def swap_core(array):
        return lax.ppermute(array, "dp", [(0, 1), (1, 0)])

    def added(*parts, after=(), free=()):
        return calls.run(
            add_kernel, "add_rows", list(parts), [(parts[0].shape, BF16)], after=after, limit=SMALL, free=free
        )[0]

    packed = calls.run(
        functools.partial(pack_kernel, experts),
        "pack_rows",
        [tokens, grad_out, expert_ids.T, router_weights.T],
        [((rows, 2 * width + extra), BF16)],
        limit=SMALL,
    )[0]

    order = [0] + [r for r in range(sets) if r % 4 > 1] + [r for r in range(1, sets) if r % 4 < 2]
    blocks, heads = {}, {0: packed}
    for r in order:
        if r not in heads:
            heads[r] = swap(packed, 4 * r) if r % 2 == 0 or r == 1 else swap(heads[r - 1], 4)
        own = heads[r]
        over_x, over_y = swap(own, 1), swap(own, 2)
        if r % 2 == 1:
            diagonal = swap(blocks[r - 1][3], 4)
        elif r % 4 == 0:
            diagonal = swap(over_x, 2)
        else:
            diagonal = swap(over_y, 1)
        blocks[r] = (own, over_x, over_y, diagonal)

    clips = (clip_in[0], range_in[0], clip_out[0].transpose(1, 0, 2), range_out[0].transpose(1, 0, 2))
    gu_mine, d_mine = calls.run(
        weight_kernel,
        "make_weights",
        [codes_in[0], codes_out[0], *clips],
        [((2, depth, hidden), BF16), ((hidden, depth), BF16)],
        after=(blocks[0][1],),
    )
    weights = (gu_mine, swap_core(gu_mine), d_mine, swap_core(d_mine))

    shapes = ((2, 2, depth // GROUP, hidden), (2, clip_out.shape[2], depth))
    partials, sums, after = {}, {True: None, False: None}, ()
    for first, second in zip(order[0::2], order[1::2]):
        partials[first], stored = run_set(calls, blocks[first], weights, experts, None, after)
        partials[second], stored = run_set(calls, blocks[second], weights, experts, stored, ())
        for other in (True, False):
            sums[other] = run_sums(calls, stored, weights, other, sums[other], shapes, ())
        after = (sums[False][0],)

    final = []
    for r in order[1:]:
        own, p_x, p_y, p_d = partials[r]
        if r == 1:
            partials[0][3] = added(partials[0][3], swap(p_d, 4))
        elif r % 4 in (0, 3):
            p_x = added(p_x, swap(p_d, 2))
        else:
            p_y = added(p_y, swap(p_d, 1))
        final.append(swap(added(own, swap(p_x, 1), swap(p_y, 2)), 4 * r))
    own, p_x, p_y, p_d = partials[0]
    p_x = added(p_x, swap(p_d, 2))
    grad_tokens = added(own, swap(p_x, 1), swap(p_y, 2), *final, free=(0,))

    mine_in, mine_out = sums[False]
    got_in, got_out = (swap_core(a) for a in sums[True])
    grad_in, grad_clip_out = calls.run(
        clip_kernel,
        "clip_gradients",
        [mine_in, got_in, mine_out, got_out, *clips],
        [((2, 2, depth // GROUP, hidden), F32), ((clip_out.shape[2], 2, depth), F32)],
        limit=SMALL,
        free=(0, 1),
    )
    return grad_tokens, grad_in[None], grad_clip_out.transpose(1, 0, 2)[None]


def solution(mesh):
    return jax.shard_map(
        body,
        mesh=mesh,
        in_specs=(
            P(("expert", "dp"), None),
            P(("expert", "dp"), None),
            P(("expert", "dp"), None),
            P(("expert", "dp"), None),
            P("expert", None, "dp", None),
            P("expert", None, "dp"),
            P("expert", None, None, None, None),
            P("expert", None, None, None, None),
            P("expert", None, None, None),
            P("expert", None, None, None),
        ),
        out_specs=(
            P(("expert", "dp"), None),
            P("expert", None, None, "dp", None),
            P("expert", None, None, "dp"),
        ),
        check_vma=False,
    )
```

```python
import functools

import jax
import jax.numpy as jnp
from jax import lax
from jax.experimental import pallas as pl
from jax.experimental.pallas import tpu as pltpu
from jax.sharding import PartitionSpec as P

GROUP = 128
PACK = 3
CHUNK = 16
TILE = 256
LIMIT = 24 * 1024 * 1024
SMALL = 8 * 1024 * 1024
F32 = jnp.float32
BF16 = jnp.bfloat16


def dot_nn(a, b):
    return lax.dot_general(a, b, (((1,), (0,)), ((), ())), preferred_element_type=F32)


def dot_nt(a, b):
    return lax.dot_general(a, b, (((1,), (1,)), ((), ())), preferred_element_type=F32)


def dot_tn(a, b):
    return lax.dot_general(a, b, (((0,), (0,)), ((), ())), preferred_element_type=F32)


def sigmoid(v):
    return 1.0 / (1.0 + jnp.exp(-v))


def plane_order(size, back=False):
    third = size // PACK
    row = lax.broadcasted_iota(jnp.int32, (size, size), 1 if back else 0)
    col = lax.broadcasted_iota(jnp.int32, (size, size), 0 if back else 1)
    plane = jnp.zeros_like(col)
    for j in range(1, PACK):
        plane = plane + (col >= j * third).astype(jnp.int32)
    return (row == PACK * (col - plane * third) + plane).astype(F32).astype(BF16)


def three_parts(a):
    high = a.astype(BF16)
    rest = a - high.astype(F32)
    middle = rest.astype(BF16)
    low = (rest - middle.astype(F32)).astype(BF16)
    return high, middle, low


def placed(a, order):
    parts = [dot_nn(part, order) for part in three_parts(a)]
    return parts[0] + parts[1] + parts[2]


ANYWHERE = pl.BlockSpec(memory_space=pl.ANY)
INSIDE = pl.BlockSpec(memory_space=pltpu.VMEM)


class Calls:
    def __init__(self, keep):
        self.keep = keep

    def pin(self, array):
        return pltpu.with_memory_space_constraint(array, pltpu.VMEM) if self.keep else array

    def out(self, shape, dtype):
        return pltpu.VMEM(shape, dtype) if self.keep else jax.ShapeDtypeStruct(shape, dtype)

    def run(self, kernel, name, inputs, outputs, after=(), alias=None, limit=LIMIT, raw=(), free=()):
        inputs = [*raw, *map(self.pin, inputs)]
        count = len(inputs)

        def wrapped(*refs):
            kernel(*refs[:count], *refs[count + len(after) :])

        return pl.pallas_call(
            wrapped,
            in_specs=[INSIDE] * count + [ANYWHERE] * len(after),
            out_specs=[INSIDE] * len(outputs),
            out_shape=[
                jax.ShapeDtypeStruct(shape, dtype) if i in free else self.out(shape, dtype)
                for i, (shape, dtype) in enumerate(outputs)
            ],
            input_output_aliases=alias or {},
            compiler_params=pltpu.CompilerParams(vmem_limit_bytes=limit),
            cost_estimate=pl.CostEstimate(flops=0, bytes_accessed=0, transcendentals=0),
            name=name,
        )(*inputs, *after)


def pack_kernel(experts, token_ref, grad_ref, ids_ref, weights_ref, out_ref):
    rows, width = grad_ref.shape
    extra = out_ref.shape[1] - 2 * width
    out_ref[:, :width] = token_ref[...]
    out_ref[:, width : 2 * width] = grad_ref[...]
    line = lax.broadcasted_iota(jnp.int32, (extra, rows), 0)
    part = sum((line >= i * experts).astype(jnp.int32) for i in range(1, 4))
    expert = jnp.where(part < 3, line - part * experts, -1)
    table = jnp.zeros((extra, rows), F32)
    for k in range(ids_ref.shape[0]):
        table = table + jnp.where(ids_ref[k : k + 1, :] == expert, weights_ref[k : k + 1, :], 0.0)
    high, middle, low = three_parts(table)
    split = jnp.where(
        part == 0,
        high.astype(F32),
        jnp.where(part == 1, middle.astype(F32), low.astype(F32)),
    ).astype(BF16)
    same = lax.broadcasted_iota(jnp.int32, (extra, extra), 0) == lax.broadcasted_iota(jnp.int32, (extra, extra), 1)
    out_ref[:, 2 * width :] = dot_tn(split, same.astype(F32).astype(BF16)).astype(BF16)


def weight_kernel(codes_in, codes_out, clip_in, range_in, clip_out, range_out, w_ref):
    dp = lax.axis_index("dp")
    depth, third = codes_in.shape[1:]
    hidden = clip_in.shape[3]
    groups = depth // GROUP
    own = pl.ds(pl.multiple_of(dp * groups, groups), groups)
    order = plane_order(hidden)
    for p in range(2):
        upper = sigmoid(clip_in[p, 0, own, :]) * range_in[p, 0, own, :]
        lower = sigmoid(clip_in[p, 1, own, :]) * range_in[p, 1, own, :]
        ends = placed(jnp.concatenate([(upper + lower) / 15.0, lower], axis=0), order)
        for g in range(groups):
            packed = codes_in[p, g * GROUP : (g + 1) * GROUP, :]
            for j in range(PACK):
                code = jnp.bitwise_and(jnp.right_shift(packed, 4 * j), 15).astype(F32)
                cols = slice(j * third, (j + 1) * third)
                w_ref[p, g * GROUP : (g + 1) * GROUP, cols] = (
                    ends[g : g + 1, cols] * code - ends[groups + g : groups + g + 1, cols]
                ).astype(BF16)
    own = pl.ds(pl.multiple_of(dp * depth, depth), depth)
    step, lower = [], []
    for g in range(clip_out.shape[0]):
        upper_end = sigmoid(clip_out[g, 0:1, own]) * range_out[g, 0:1, own]
        lower_end = sigmoid(clip_out[g, 1:2, own]) * range_out[g, 1:2, own]
        step.append((upper_end + lower_end) / 15.0)
        lower.append(lower_end)
    row = lax.broadcasted_iota(jnp.int32, (CHUNK, 1), 0)
    for start in range(0, third, CHUNK):
        packed = codes_out[start : start + CHUNK, :]
        for j in range(PACK):
            first = (PACK * start + j) // GROUP
            last = (PACK * (start + CHUNK - 1) + j) // GROUP
            step_rows, lower_rows = step[first], lower[first]
            for g in range(first + 1, last + 1):
                late = PACK * (row + start) + j >= g * GROUP
                step_rows = jnp.where(late, step[g], step_rows)
                lower_rows = jnp.where(late, lower[g], lower_rows)
            code = jnp.bitwise_and(jnp.right_shift(packed, 4 * j), 15).astype(F32)
            down = (step_rows * code - lower_rows).astype(BF16)
            for q in range(depth // third):
                w_ref[2, q * third + start : q * third + start + CHUNK, j * third : (j + 1) * third] = down[
                    :, q * third : (q + 1) * third
                ]


def set_kernel(experts, first, keep, *refs):
    blocks = refs[0:4]
    sides = refs[4:6]
    earlier = refs[6:10]
    refs = refs[6:] if first == 0 else refs[10:]
    partials = refs[0:4]
    x_ref, s_ref, h_ref, g_ref = refs[4:8]
    rows, width = partials[0].shape
    half = width // 2
    hidden = h_ref.shape[1]
    third = hidden // PACK
    dp, mine = lax.axis_index("dp"), lax.axis_index("expert")
    spans = (
        pl.ds(pl.multiple_of(dp * half, half), half),
        pl.ds(pl.multiple_of((1 - dp) * half, half), half),
    )
    here = slice(first, first + 4 * rows)
    if first and not keep:
        for old, new in zip(earlier, refs[4:8]):
            new[..., :first, :] = old[..., :first, :]
    for i in range(4):
        span = slice(first + i * rows, first + (i + 1) * rows)
        x_ref[span, :] = blocks[i][:, :width]
        beside = blocks[i][:, 2 * width :].astype(F32)
        lane = lax.broadcasted_iota(jnp.int32, beside.shape, 1)
        keep = (lane == mine) | (lane == mine + experts) | (lane == mine + 2 * experts)
        scale = jnp.sum(jnp.where(keep, beside, 0.0), axis=1, keepdims=True)
        s_ref[span, :] = (scale * blocks[i][:, width : 2 * width].astype(F32)).astype(BF16)
    for j in range(PACK):
        cols = slice(j * third, (j + 1) * third)
        gate_pre = dot_nn(x_ref[here, spans[0]], sides[0][0, :, cols]) + dot_nn(
            x_ref[here, spans[1]], sides[1][0, :, cols]
        )
        up_pre = dot_nn(x_ref[here, spans[0]], sides[0][1, :, cols]) + dot_nn(
            x_ref[here, spans[1]], sides[1][1, :, cols]
        )
        grad_hidden = 0.0
        for side in range(2):
            for q in range(half // third):
                tile = pl.ds(pl.multiple_of((dp if side == 0 else 1 - dp) * half + q * third, third), third)
                grad_hidden = grad_hidden + dot_nt(
                    s_ref[here, tile], sides[side][2, q * third : (q + 1) * third, cols]
                )
        sig = sigmoid(gate_pre)
        act = gate_pre * sig
        h_ref[here, cols] = (act * up_pre).astype(BF16)
        g_ref[0, here, cols] = (grad_hidden * up_pre * sig * (1.0 + gate_pre * (1.0 - sig))).astype(BF16)
        g_ref[1, here, cols] = (grad_hidden * act).astype(BF16)
    for side in range(2):
        base = jnp.where(side == 0, dp, 1 - dp) * half

        @pl.loop(0, half // TILE)
        def _(n):
            depth = pl.ds(pl.multiple_of(n * TILE, TILE), TILE)
            part = dot_nt(g_ref[0, here, :], sides[side][0, depth, :]) + dot_nt(
                g_ref[1, here, :], sides[side][1, depth, :]
            )
            cols = pl.ds(pl.multiple_of(base + n * TILE, TILE), TILE)
            for i in range(4):
                partials[i][:, cols] = part[i * rows : (i + 1) * rows, :].astype(BF16)


def run_set(calls, blocks, weights, experts, pair=None, after=()):
    rows, width = blocks[0].shape[0], 2 * weights[0].shape[1]
    hidden = weights[0].shape[2]
    both = 8 * rows
    stored = [((both, width), BF16), ((both, width), BF16), ((both, hidden), BF16), ((2, both, hidden), BF16)]
    out = calls.run(
        functools.partial(set_kernel, experts, 0 if pair is None else 4 * rows, calls.keep),
        "expert_set",
        [*blocks, *weights, *(pair or ())],
        [((rows, width), BF16)] * 4 + stored,
        after=after,
        alias=None if pair is None else {6 + i: 4 + i for i in range(4)},
    )
    return list(out[:4]), list(out[4:])


def group_marks(size, count, span, planes):
    row = lax.broadcasted_iota(jnp.int32, (size, count), 0)
    group = lax.broadcasted_iota(jnp.int32, (size, count), 1)
    if planes > 1:
        third = size // planes
        plane = jnp.zeros_like(row)
        for j in range(1, planes):
            plane = plane + (row >= j * third).astype(jnp.int32)
        row = planes * (row - plane * third) + plane
    return ((row >= group * span) & (row < (group + 1) * span)).astype(F32).astype(BF16)


def two_parts(a):
    high = a.astype(BF16)
    return high, (a - high.astype(F32)).astype(BF16)


def sums_kernel(other, more, x_ref, s_ref, h_ref, g_ref, weights, *refs):
    old_in, old_out = refs[:2] if more else (None, None)
    sums_in, sums_out = refs[-2:]
    width = x_ref.shape[1]
    half = width // 2
    hidden = h_ref.shape[1]
    third = hidden // PACK
    share = sums_in.shape[2]
    groups_out = sums_out.shape[1]
    dp = lax.axis_index("dp")
    base = (1 - dp if other else dp) * half
    span = pl.ds(pl.multiple_of(base, half), half)

    def since(old, found, *where):
        return old[where] + found if more else found

    row_sums = two_parts(dot_nn(x_ref[:, span], group_marks(half, share, GROUP, 1)))
    for p in range(2):
        found = dot_tn(row_sums[0], g_ref[p]) + dot_tn(row_sums[1], g_ref[p])
        sums_in[p, 1] = since(old_in, found, p, 1)
    hidden_sums = two_parts(dot_nn(h_ref[...], group_marks(hidden, groups_out, GROUP, PACK)))
    found = dot_tn(hidden_sums[0], s_ref[:, span]) + dot_tn(hidden_sums[1], s_ref[:, span])
    sums_out[1] = since(old_out, found, 1)

    @pl.loop(0, half // third)
    def _(t):
        rows = pl.ds(pl.multiple_of(t * third, third), third)
        span = pl.ds(pl.multiple_of(base + t * third, third), third)
        x_cols = x_ref[:, span]
        for p in range(2):
            weighted = dot_tn(x_cols, g_ref[p]) * weights[p, rows, :].astype(F32)
            for g in range(third // GROUP):
                spot = pl.ds(t * (third // GROUP) + g, 1)
                found = jnp.sum(weighted[g * GROUP : (g + 1) * GROUP], axis=0, keepdims=True)
                sums_in[p, 0, spot, :] = since(old_in, found, p, 0, spot, slice(None))
        down = jnp.concatenate([weights[2, rows, j * third : (j + 1) * third] for j in range(PACK)], axis=0)
        weighted = dot_tn(h_ref[...], s_ref[:, span]) * down.astype(F32)
        for g in range(groups_out):
            found = None
            for j in range(PACK):
                low = -((j - GROUP * g) // PACK)
                high = -((j - GROUP * (g + 1)) // PACK)
                inner, outer = -(-low // 8) * 8, high // 8 * 8
                part = jnp.sum(weighted[j * third + inner : j * third + outer], axis=0, keepdims=True)
                found = part if found is None else found + part
                for start in sorted(({low // 8 * 8} if low % 8 else set()) | ({outer} if high % 8 else set())):
                    block = weighted[j * third + start : j * third + start + 8]
                    row = lax.broadcasted_iota(jnp.int32, block.shape, 0) + start
                    inside = (row >= low) & (row < high)
                    found = found + jnp.sum(jnp.where(inside, block, 0.0), axis=0, keepdims=True)
            sums_out[0, g : g + 1, rows] = since(old_out, found, 0, slice(g, g + 1), rows)


def run_sums(calls, stored, weights, other, before, shapes, after=()):
    side = weights[1] if other else weights[0]
    return calls.run(
        functools.partial(sums_kernel, other, before is not None),
        "group_sums",
        [*stored, side, *(before or ())],
        [(shape, F32) for shape in shapes],
        after=after,
    )


def clip_kernel(clip_in, range_in, clip_out, range_out, mine_in, got_in, mine_out, got_out, in_ref, out_ref):
    dp = lax.axis_index("dp")
    hidden = clip_in.shape[3]
    groups = in_ref.shape[2]
    share = out_ref.shape[2]
    back = plane_order(hidden, True)

    def finish(weighted, plain, clip, span):
        sig_upper, sig_lower = sigmoid(clip[0]), sigmoid(clip[1])
        upper, lower = sig_upper * span[0], sig_lower * span[1]
        upper_sum = (weighted + lower * plain) / (upper + lower)
        lower_sum = upper_sum - plain
        return (
            upper_sum * span[0] * sig_upper * (1.0 - sig_upper),
            lower_sum * span[1] * sig_lower * (1.0 - sig_lower),
        )

    own = pl.ds(pl.multiple_of(dp * groups, groups), groups)
    for p in range(2):
        sums = jnp.concatenate(
            [mine_in[p, 0] + got_in[p, 0], mine_in[p, 1] + got_in[p, 1]], axis=0
        )
        natural = placed(sums, back)
        in_ref[p, 0], in_ref[p, 1] = finish(
            natural[:groups],
            natural[groups:],
            [clip_in[p, i, own, :] for i in range(2)],
            [range_in[p, i, own, :] for i in range(2)],
        )
    own = pl.ds(pl.multiple_of(dp * share, share), share)
    for g in range(out_ref.shape[0]):
        out_ref[g, 0:1, :], out_ref[g, 1:2, :] = finish(
            mine_out[0, g : g + 1, :] + got_out[0, g : g + 1, :],
            mine_out[1, g : g + 1, :] + got_out[1, g : g + 1, :],
            [clip_out[g, i : i + 1, own] for i in range(2)],
            [range_out[g, i : i + 1, own] for i in range(2)],
        )


def add_kernel(*refs):
    total = refs[0][...].astype(F32)
    for ref in refs[1:-1]:
        total = total + ref[...].astype(F32)
    refs[-1][...] = total.astype(refs[-1].dtype)


def hold_kernel(*refs):
    pass


def body(
    tokens,
    grad_out,
    expert_ids,
    router_weights,
    codes_in,
    codes_out,
    clip_in,
    range_in,
    clip_out,
    range_out,
):
    experts = lax.axis_size("expert")
    rows, width = tokens.shape
    hidden = clip_in.shape[4]
    depth = codes_in.shape[2]
    extra = -(-3 * experts // 128) * 128
    calls = Calls(experts * rows * (3 * width + extra) * 2 < 2**24)

    def swap(array, mask):
        return lax.ppermute(array, "expert", [(i, i ^ mask) for i in range(experts)])

    def swap_core(array):
        return lax.ppermute(array, "dp", [(0, 1), (1, 0)])

    def added(*parts, after=(), free=()):
        return calls.run(
            add_kernel, "add_rows", list(parts), [(parts[0].shape, BF16)], after=after, limit=SMALL, free=free
        )[0]

    def held(array, *after):
        return pl.pallas_call(
            hold_kernel,
            in_specs=[ANYWHERE] * (1 + len(after)),
            out_specs=ANYWHERE,
            out_shape=calls.out(array.shape, array.dtype),
            input_output_aliases={0: 0},
            name="hold",
        )(calls.pin(array), *after)

    packed = calls.run(
        functools.partial(pack_kernel, experts),
        "pack_rows",
        [],
        [((rows, 2 * width + extra), BF16)],
        raw=(tokens, grad_out, expert_ids.T, router_weights.T),
        limit=SMALL,
    )[0]

    clips = (clip_in[0], range_in[0], clip_out[0].transpose(1, 0, 2), range_out[0].transpose(1, 0, 2))
    (own_weights,) = calls.run(
        weight_kernel,
        "make_weights",
        [],
        [((3, depth, hidden), BF16)],
        raw=(codes_in[0], codes_out[0], *clips),
        after=(packed,),
    )
    weights = (own_weights, swap_core(own_weights))

    shapes = ((2, 2, depth // GROUP, hidden), (2, clip_out.shape[2], depth))
    sums = {True: None, False: None}

    def quad(head, after):
        near, far = swap(head, 4), swap(head, 8)
        x0, y0 = swap(head, 1), swap(head, 2)
        d0 = swap(x0, 2)
        last = swap(far, 4)
        ready = held(far, weights[1], x0, y0, d0, near)
        x2, y2 = swap(ready, 1), swap(ready, 2)
        d2 = swap(y2, 1)
        d1, d3 = swap(d0, 4), swap(d2, 4)
        p0, stored = run_set(calls, (head, x0, y0, d0), weights, experts, after=after)
        y3 = swap(held(last, x2, y2), 2)
        x3 = swap(held(last, d2, p0[0]), 1)
        p2, stored = run_set(calls, (far, x2, y2, d2), weights, experts, stored)
        other = run_sums(calls, stored, weights, True, sums[True], shapes)
        y1 = swap(held(near, y3), 2)
        x1 = swap(held(near, x3, p2[0]), 1)
        p3, later = run_set(calls, (last, x3, y3, d3), weights, experts, after=(other[0],))
        x_sum0 = added(p0[1], swap(p0[3], 2))
        x_sum2 = added(p2[1], swap(p2[3], 2))
        mine = run_sums(calls, stored, weights, False, sums[False], shapes, (p3[0],))
        p1, later = run_set(
            calls, (near, x1, y1, d1), weights, experts, later, (x_sum0, x_sum2, mine[0])
        )
        x_sum3 = added(p3[1], swap(p3[3], 2))
        sums[True] = run_sums(calls, later, weights, True, other, shapes, (x_sum3,))
        total3 = added(p3[0], swap(x_sum3, 1), swap(p3[2], 2))
        sums[False] = run_sums(calls, later, weights, False, mine, shapes, (total3,))
        y_sum1 = added(p1[2], swap(p1[3], 1))
        total1 = added(p1[0], swap(p1[1], 1), swap(y_sum1, 2))
        total2 = added(p2[0], swap(x_sum2, 1), swap(p2[2], 2), swap(total3, 4))
        return p0[0], swap(x_sum0, 1), swap(p0[2], 2), swap(total1, 4), swap(total2, 8)

    final, after = [], ()
    for base in range(0, experts, 16):
        parts = quad(swap(packed, base) if base else packed, after)
        final += [swap(added(*parts), base)] if base else parts
        after = (sums[False][0],)
    grad_tokens = added(*final, free=(0,))

    mine_in, mine_out = sums[False]
    got_in, got_out = (swap_core(a) for a in sums[True])
    grad_in, grad_clip_out = calls.run(
        clip_kernel,
        "clip_gradients",
        [mine_in, got_in, mine_out, got_out],
        [((2, 2, depth // GROUP, hidden), F32), ((clip_out.shape[2], 2, depth), F32)],
        raw=clips,
        limit=SMALL,
        free=(0, 1),
    )
    return grad_tokens, grad_in[None], grad_clip_out.transpose(1, 0, 2)[None]


def solution(mesh):
    return jax.shard_map(
        body,
        mesh=mesh,
        in_specs=(
            P(("expert", "dp"), None),
            P(("expert", "dp"), None),
            P(("expert", "dp"), None),
            P(("expert", "dp"), None),
            P("expert", None, "dp", None),
            P("expert", None, "dp"),
            P("expert", None, None, None, None),
            P("expert", None, None, None, None),
            P("expert", None, None, None),
            P("expert", None, None, None),
        ),
        out_specs=(
            P(("expert", "dp"), None),
            P("expert", None, None, "dp", None),
            P("expert", None, None, "dp"),
        ),
        check_vma=False,
    )
```

```python
import functools

import jax
import jax.numpy as jnp
from jax import lax
from jax.experimental import pallas as pl
from jax.experimental.pallas import tpu as pltpu
from jax.sharding import PartitionSpec as P

GROUP = 128
PACK = 3
CHUNK = 16
TILE = 256
LIMIT = 24 * 1024 * 1024
SMALL = 8 * 1024 * 1024
TINY = 1024 * 1024
F32 = jnp.float32
BF16 = jnp.bfloat16


def dot_nn(a, b):
    return lax.dot_general(a, b, (((1,), (0,)), ((), ())), preferred_element_type=F32)


def dot_nt(a, b):
    return lax.dot_general(a, b, (((1,), (1,)), ((), ())), preferred_element_type=F32)


def dot_tn(a, b):
    return lax.dot_general(a, b, (((0,), (0,)), ((), ())), preferred_element_type=F32)


def sigmoid(v):
    return 1.0 / (1.0 + jnp.exp(-v))


def plane_order(size, back=False):
    third = size // PACK
    row = lax.broadcasted_iota(jnp.int32, (size, size), 1 if back else 0)
    col = lax.broadcasted_iota(jnp.int32, (size, size), 0 if back else 1)
    plane = jnp.zeros_like(col)
    for j in range(1, PACK):
        plane = plane + (col >= j * third).astype(jnp.int32)
    return (row == PACK * (col - plane * third) + plane).astype(F32).astype(BF16)


def three_parts(a):
    high = a.astype(BF16)
    rest = a - high.astype(F32)
    middle = rest.astype(BF16)
    low = (rest - middle.astype(F32)).astype(BF16)
    return high, middle, low


def placed(a, order):
    parts = [dot_nn(part, order) for part in three_parts(a)]
    return parts[0] + parts[1] + parts[2]


ANYWHERE = pl.BlockSpec(memory_space=pl.ANY)
INSIDE = pl.BlockSpec(memory_space=pltpu.VMEM)


class Calls:
    def __init__(self, keep):
        self.keep = keep

    def pin(self, array):
        return pltpu.with_memory_space_constraint(array, pltpu.VMEM) if self.keep else array

    def out(self, shape, dtype):
        return pltpu.VMEM(shape, dtype) if self.keep else jax.ShapeDtypeStruct(shape, dtype)

    def run(self, kernel, name, inputs, outputs, after=(), alias=None, limit=LIMIT, raw=(), free=()):
        count, given = len(inputs), len(raw)

        def wrapped(*refs):
            outs = refs[given + count + len(after) : given + count + len(after) + len(outputs)]
            scratch = refs[len(refs) - given - 1 : len(refs) - 1] if raw else ()
            copies = [
                pltpu.make_async_copy(refs[i], scratch[i], refs[-1].at[i]) for i in range(given)
            ]
            for copy in copies:
                copy.start()
            for copy in copies:
                copy.wait()
            kernel(*scratch, *refs[given : given + count], *outs)

        scratch = [pltpu.VMEM(a.shape, a.dtype) for a in raw]
        return pl.pallas_call(
            wrapped,
            in_specs=[ANYWHERE] * given + [INSIDE] * count + [ANYWHERE] * len(after),
            out_specs=[INSIDE] * len(outputs),
            out_shape=[
                jax.ShapeDtypeStruct(shape, dtype) if i in free else self.out(shape, dtype)
                for i, (shape, dtype) in enumerate(outputs)
            ],
            scratch_shapes=scratch + ([pltpu.SemaphoreType.DMA((given,))] if raw else []),
            input_output_aliases=alias or {},
            compiler_params=pltpu.CompilerParams(vmem_limit_bytes=limit),
            cost_estimate=pl.CostEstimate(flops=0, bytes_accessed=0, transcendentals=0),
            name=name,
        )(*[pltpu.with_memory_space_constraint(a, pltpu.HBM) for a in raw], *[self.pin(a) for a in inputs], *after)


def pack_kernel(experts, token_ref, grad_ref, ids_ref, weights_ref, out_ref):
    rows, width = grad_ref.shape
    extra = out_ref.shape[1] - 2 * width
    out_ref[:, :width] = token_ref[...]
    out_ref[:, width : 2 * width] = grad_ref[...]
    line = lax.broadcasted_iota(jnp.int32, (extra, rows), 0)
    part = sum((line >= i * experts).astype(jnp.int32) for i in range(1, 4))
    expert = jnp.where(part < 3, line - part * experts, -1)
    table = jnp.zeros((extra, rows), F32)
    for k in range(ids_ref.shape[0]):
        table = table + jnp.where(ids_ref[k : k + 1, :] == expert, weights_ref[k : k + 1, :], 0.0)
    high, middle, low = three_parts(table)
    split = jnp.where(
        part == 0,
        high.astype(F32),
        jnp.where(part == 1, middle.astype(F32), low.astype(F32)),
    ).astype(BF16)
    same = lax.broadcasted_iota(jnp.int32, (extra, extra), 0) == lax.broadcasted_iota(jnp.int32, (extra, extra), 1)
    out_ref[:, 2 * width :] = dot_tn(split, same.astype(F32).astype(BF16)).astype(BF16)


def weight_kernel(codes_in, codes_out, clip_in, range_in, clip_out, range_out, w_ref):
    dp = lax.axis_index("dp")
    depth, third = codes_in.shape[1:]
    hidden = clip_in.shape[3]
    groups = depth // GROUP
    own = pl.ds(pl.multiple_of(dp * groups, groups), groups)
    order = plane_order(hidden)
    for p in range(2):
        upper = sigmoid(clip_in[p, 0, own, :]) * range_in[p, 0, own, :]
        lower = sigmoid(clip_in[p, 1, own, :]) * range_in[p, 1, own, :]
        ends = placed(jnp.concatenate([(upper + lower) / 15.0, lower], axis=0), order)
        for g in range(groups):
            packed = codes_in[p, g * GROUP : (g + 1) * GROUP, :]
            for j in range(PACK):
                code = jnp.bitwise_and(jnp.right_shift(packed, 4 * j), 15).astype(F32)
                cols = slice(j * third, (j + 1) * third)
                w_ref[p, g * GROUP : (g + 1) * GROUP, cols] = (
                    ends[g : g + 1, cols] * code - ends[groups + g : groups + g + 1, cols]
                ).astype(BF16)
    own = pl.ds(pl.multiple_of(dp * depth, depth), depth)
    step, lower = [], []
    for g in range(clip_out.shape[0]):
        upper_end = sigmoid(clip_out[g, 0:1, own]) * range_out[g, 0:1, own]
        lower_end = sigmoid(clip_out[g, 1:2, own]) * range_out[g, 1:2, own]
        step.append((upper_end + lower_end) / 15.0)
        lower.append(lower_end)
    row = lax.broadcasted_iota(jnp.int32, (CHUNK, 1), 0)
    for start in range(0, third, CHUNK):
        packed = codes_out[start : start + CHUNK, :]
        for j in range(PACK):
            first = (PACK * start + j) // GROUP
            last = (PACK * (start + CHUNK - 1) + j) // GROUP
            step_rows, lower_rows = step[first], lower[first]
            for g in range(first + 1, last + 1):
                late = PACK * (row + start) + j >= g * GROUP
                step_rows = jnp.where(late, step[g], step_rows)
                lower_rows = jnp.where(late, lower[g], lower_rows)
            code = jnp.bitwise_and(jnp.right_shift(packed, 4 * j), 15).astype(F32)
            down = (step_rows * code - lower_rows).astype(BF16)
            for q in range(depth // third):
                w_ref[2, q * third + start : q * third + start + CHUNK, j * third : (j + 1) * third] = down[
                    :, q * third : (q + 1) * third
                ]


def set_kernel(experts, first, keep, *refs):
    blocks = refs[0:4]
    sides = refs[4:6]
    earlier = refs[6:10]
    refs = refs[6:] if first == 0 else refs[10:]
    partials = refs[0:4]
    x_ref, s_ref, h_ref, g_ref = refs[4:8]
    rows, width = partials[0].shape
    half = width // 2
    hidden = h_ref.shape[1]
    third = hidden // PACK
    dp, mine = lax.axis_index("dp"), lax.axis_index("expert")
    spans = (
        pl.ds(pl.multiple_of(dp * half, half), half),
        pl.ds(pl.multiple_of((1 - dp) * half, half), half),
    )
    here = slice(first, first + 4 * rows)
    if first and not keep:
        for old, new in zip(earlier, refs[4:8]):
            new[..., :first, :] = old[..., :first, :]
    for i in range(4):
        span = slice(first + i * rows, first + (i + 1) * rows)
        x_ref[span, :] = blocks[i][:, :width]
        beside = blocks[i][:, 2 * width :].astype(F32)
        lane = lax.broadcasted_iota(jnp.int32, beside.shape, 1)
        keep = (lane == mine) | (lane == mine + experts) | (lane == mine + 2 * experts)
        scale = jnp.sum(jnp.where(keep, beside, 0.0), axis=1, keepdims=True)
        s_ref[span, :] = (scale * blocks[i][:, width : 2 * width].astype(F32)).astype(BF16)
    for j in range(PACK):
        cols = slice(j * third, (j + 1) * third)
        gate_pre = dot_nn(x_ref[here, spans[0]], sides[0][0, :, cols]) + dot_nn(
            x_ref[here, spans[1]], sides[1][0, :, cols]
        )
        up_pre = dot_nn(x_ref[here, spans[0]], sides[0][1, :, cols]) + dot_nn(
            x_ref[here, spans[1]], sides[1][1, :, cols]
        )
        grad_hidden = 0.0
        for side in range(2):
            for q in range(half // third):
                tile = pl.ds(pl.multiple_of((dp if side == 0 else 1 - dp) * half + q * third, third), third)
                grad_hidden = grad_hidden + dot_nt(
                    s_ref[here, tile], sides[side][2, q * third : (q + 1) * third, cols]
                )
        sig = sigmoid(gate_pre)
        act = gate_pre * sig
        h_ref[here, cols] = (act * up_pre).astype(BF16)
        g_ref[0, here, cols] = (grad_hidden * up_pre * sig * (1.0 + gate_pre * (1.0 - sig))).astype(BF16)
        g_ref[1, here, cols] = (grad_hidden * act).astype(BF16)
    for side in range(2):
        base = jnp.where(side == 0, dp, 1 - dp) * half

        @pl.loop(0, half // TILE)
        def _(n):
            depth = pl.ds(pl.multiple_of(n * TILE, TILE), TILE)
            part = dot_nt(g_ref[0, here, :], sides[side][0, depth, :]) + dot_nt(
                g_ref[1, here, :], sides[side][1, depth, :]
            )
            cols = pl.ds(pl.multiple_of(base + n * TILE, TILE), TILE)
            for i in range(4):
                partials[i][:, cols] = part[i * rows : (i + 1) * rows, :].astype(BF16)


def run_set(calls, blocks, weights, experts, pair=None, after=()):
    rows, width = blocks[0].shape[0], 2 * weights[0].shape[1]
    hidden = weights[0].shape[2]
    both = 8 * rows
    stored = [((both, width), BF16), ((both, width), BF16), ((both, hidden), BF16), ((2, both, hidden), BF16)]
    out = calls.run(
        functools.partial(set_kernel, experts, 0 if pair is None else 4 * rows, calls.keep),
        "expert_set",
        [*blocks, *weights, *(pair or ())],
        [((rows, width), BF16)] * 4 + stored,
        after=after,
        alias=None if pair is None else {6 + i: 4 + i for i in range(4)},
    )
    return list(out[:4]), list(out[4:])


def group_marks(size, count, span, planes):
    row = lax.broadcasted_iota(jnp.int32, (size, count), 0)
    group = lax.broadcasted_iota(jnp.int32, (size, count), 1)
    if planes > 1:
        third = size // planes
        plane = jnp.zeros_like(row)
        for j in range(1, planes):
            plane = plane + (row >= j * third).astype(jnp.int32)
        row = planes * (row - plane * third) + plane
    return ((row >= group * span) & (row < (group + 1) * span)).astype(F32).astype(BF16)


def two_parts(a):
    high = a.astype(BF16)
    return high, (a - high.astype(F32)).astype(BF16)


def sums_kernel(other, more, x_ref, s_ref, h_ref, g_ref, weights, *refs):
    old_in, old_out = refs[:2] if more else (None, None)
    sums_in, sums_out = refs[-2:]
    width = x_ref.shape[1]
    half = width // 2
    hidden = h_ref.shape[1]
    third = hidden // PACK
    share = sums_in.shape[2]
    groups_out = sums_out.shape[1]
    dp = lax.axis_index("dp")
    base = (1 - dp if other else dp) * half
    span = pl.ds(pl.multiple_of(base, half), half)

    def since(old, found, *where):
        return old[where] + found if more else found

    row_sums = two_parts(dot_nn(x_ref[:, span], group_marks(half, share, GROUP, 1)))
    for p in range(2):
        found = dot_tn(row_sums[0], g_ref[p]) + dot_tn(row_sums[1], g_ref[p])
        sums_in[p, 1] = since(old_in, found, p, 1)
    hidden_sums = two_parts(dot_nn(h_ref[...], group_marks(hidden, groups_out, GROUP, PACK)))
    found = dot_tn(hidden_sums[0], s_ref[:, span]) + dot_tn(hidden_sums[1], s_ref[:, span])
    sums_out[1] = since(old_out, found, 1)

    @pl.loop(0, half // third)
    def _(t):
        rows = pl.ds(pl.multiple_of(t * third, third), third)
        span = pl.ds(pl.multiple_of(base + t * third, third), third)
        x_cols = x_ref[:, span]
        for p in range(2):
            weighted = dot_tn(x_cols, g_ref[p]) * weights[p, rows, :].astype(F32)
            for g in range(third // GROUP):
                spot = pl.ds(t * (third // GROUP) + g, 1)
                found = jnp.sum(weighted[g * GROUP : (g + 1) * GROUP], axis=0, keepdims=True)
                sums_in[p, 0, spot, :] = since(old_in, found, p, 0, spot, slice(None))
        down = jnp.concatenate([weights[2, rows, j * third : (j + 1) * third] for j in range(PACK)], axis=0)
        weighted = dot_tn(h_ref[...], s_ref[:, span]) * down.astype(F32)
        for g in range(groups_out):
            found = None
            for j in range(PACK):
                low = -((j - GROUP * g) // PACK)
                high = -((j - GROUP * (g + 1)) // PACK)
                inner, outer = -(-low // 8) * 8, high // 8 * 8
                part = jnp.sum(weighted[j * third + inner : j * third + outer], axis=0, keepdims=True)
                found = part if found is None else found + part
                for start in sorted(({low // 8 * 8} if low % 8 else set()) | ({outer} if high % 8 else set())):
                    block = weighted[j * third + start : j * third + start + 8]
                    row = lax.broadcasted_iota(jnp.int32, block.shape, 0) + start
                    inside = (row >= low) & (row < high)
                    found = found + jnp.sum(jnp.where(inside, block, 0.0), axis=0, keepdims=True)
            sums_out[0, g : g + 1, rows] = since(old_out, found, 0, slice(g, g + 1), rows)


def run_sums(calls, stored, weights, other, before, shapes, after=()):
    side = weights[1] if other else weights[0]
    return calls.run(
        functools.partial(sums_kernel, other, before is not None),
        "group_sums",
        [*stored, side, *(before or ())],
        [(shape, F32) for shape in shapes],
        after=after,
    )


def clip_kernel(clip_in, range_in, clip_out, range_out, mine_in, got_in, mine_out, got_out, in_ref, out_ref):
    dp = lax.axis_index("dp")
    hidden = clip_in.shape[3]
    groups = in_ref.shape[2]
    share = out_ref.shape[2]
    back = plane_order(hidden, True)

    def finish(weighted, plain, clip, span):
        sig_upper, sig_lower = sigmoid(clip[0]), sigmoid(clip[1])
        upper, lower = sig_upper * span[0], sig_lower * span[1]
        upper_sum = (weighted + lower * plain) / (upper + lower)
        lower_sum = upper_sum - plain
        return (
            upper_sum * span[0] * sig_upper * (1.0 - sig_upper),
            lower_sum * span[1] * sig_lower * (1.0 - sig_lower),
        )

    own = pl.ds(pl.multiple_of(dp * groups, groups), groups)
    for p in range(2):
        sums = jnp.concatenate(
            [mine_in[p, 0] + got_in[p, 0], mine_in[p, 1] + got_in[p, 1]], axis=0
        )
        natural = placed(sums, back)
        in_ref[p, 0], in_ref[p, 1] = finish(
            natural[:groups],
            natural[groups:],
            [clip_in[p, i, own, :] for i in range(2)],
            [range_in[p, i, own, :] for i in range(2)],
        )
    own = pl.ds(pl.multiple_of(dp * share, share), share)
    for g in range(out_ref.shape[0]):
        out_ref[g, 0:1, :], out_ref[g, 1:2, :] = finish(
            mine_out[0, g : g + 1, :] + got_out[0, g : g + 1, :],
            mine_out[1, g : g + 1, :] + got_out[1, g : g + 1, :],
            [clip_out[g, i : i + 1, own] for i in range(2)],
            [range_out[g, i : i + 1, own] for i in range(2)],
        )


def add_kernel(*refs):
    total = refs[0][...].astype(F32)
    for ref in refs[1:-1]:
        total = total + ref[...].astype(F32)
    refs[-1][...] = total.astype(refs[-1].dtype)


def hold_kernel(*refs):
    pass


def body(
    tokens,
    grad_out,
    expert_ids,
    router_weights,
    codes_in,
    codes_out,
    clip_in,
    range_in,
    clip_out,
    range_out,
):
    experts = lax.axis_size("expert")
    rows, width = tokens.shape
    hidden = clip_in.shape[4]
    depth = codes_in.shape[2]
    extra = -(-3 * experts // 128) * 128
    calls = Calls(experts * rows * (3 * width + extra) * 2 < 2**24)

    def swap(array, mask):
        return lax.ppermute(array, "expert", [(i, i ^ mask) for i in range(experts)])

    def swap_core(array):
        return lax.ppermute(array, "dp", [(0, 1), (1, 0)])

    def added(*parts, after=(), free=()):
        return calls.run(
            add_kernel, "add_rows", list(parts), [(parts[0].shape, BF16)], after=after, limit=SMALL, free=free
        )[0]

    def held(array, *after):
        return pl.pallas_call(
            hold_kernel,
            in_specs=[ANYWHERE] * (1 + len(after)),
            out_specs=ANYWHERE,
            out_shape=calls.out(array.shape, array.dtype),
            input_output_aliases={0: 0},
            compiler_params=pltpu.CompilerParams(vmem_limit_bytes=TINY),
            cost_estimate=pl.CostEstimate(flops=0, bytes_accessed=0, transcendentals=0),
            name="hold",
        )(calls.pin(array), *after)

    packed = calls.run(
        functools.partial(pack_kernel, experts),
        "pack_rows",
        [],
        [((rows, 2 * width + extra), BF16)],
        raw=(tokens, grad_out, expert_ids.T, router_weights.T),
        limit=SMALL,
    )[0]

    clips = (clip_in[0], range_in[0], clip_out[0].transpose(1, 0, 2), range_out[0].transpose(1, 0, 2))
    (own_weights,) = calls.run(
        weight_kernel,
        "make_weights",
        [],
        [((3, depth, hidden), BF16)],
        raw=(codes_in[0], codes_out[0], *clips),
        after=(packed,),
    )
    weights = (own_weights, swap_core(own_weights))

    shapes = ((2, 2, depth // GROUP, hidden), (2, clip_out.shape[2], depth))
    sums = {True: None, False: None}

    def quad(head, after):
        near, far = swap(head, 4), swap(head, 8)
        x0, y0 = swap(head, 1), swap(head, 2)
        d0 = swap(x0, 2)
        last = swap(far, 4)
        ready = held(far, weights[1], x0, y0, d0, near)
        x2, y2 = swap(ready, 1), swap(ready, 2)
        d2 = swap(y2, 1)
        d1, d3 = swap(d0, 4), swap(d2, 4)
        p0, stored = run_set(calls, (head, x0, y0, d0), weights, experts, after=after)
        y3 = swap(held(last, x2, y2), 2)
        x3 = swap(held(last, d2, p0[0]), 1)
        p2, stored = run_set(calls, (far, x2, y2, d2), weights, experts, stored)
        other = run_sums(calls, stored, weights, True, sums[True], shapes)
        y1 = swap(held(near, y3), 2)
        x1 = swap(held(near, x3, p2[0]), 1)
        p3, later = run_set(calls, (last, x3, y3, d3), weights, experts, after=(other[0],))
        x_sum0 = added(p0[1], swap(p0[3], 2))
        x_sum2 = added(p2[1], swap(p2[3], 2))
        mine = run_sums(calls, stored, weights, False, sums[False], shapes, (p3[0],))
        p1, later = run_set(
            calls, (near, x1, y1, d1), weights, experts, later, (x_sum0, x_sum2, mine[0])
        )
        x_sum3 = added(p3[1], swap(p3[3], 2))
        sums[True] = run_sums(calls, later, weights, True, other, shapes, (x_sum3,))
        total3 = added(p3[0], swap(x_sum3, 1), swap(p3[2], 2))
        sums[False] = run_sums(calls, later, weights, False, mine, shapes, (total3,))
        y_sum1 = added(p1[2], swap(p1[3], 1))
        total1 = added(p1[0], swap(p1[1], 1), swap(y_sum1, 2))
        total2 = added(p2[0], swap(x_sum2, 1), swap(p2[2], 2), swap(total3, 4))
        return p0[0], swap(x_sum0, 1), swap(p0[2], 2), swap(total1, 4), swap(total2, 8)

    final, after = [], ()
    for base in range(0, experts, 16):
        parts = quad(swap(packed, base) if base else packed, after)
        final += [swap(added(*parts), base)] if base else parts
        after = (sums[False][0],)
    grad_tokens = added(*final, free=(0,))

    mine_in, mine_out = sums[False]
    got_in, got_out = (swap_core(a) for a in sums[True])
    grad_in, grad_clip_out = calls.run(
        clip_kernel,
        "clip_gradients",
        [mine_in, got_in, mine_out, got_out],
        [((2, 2, depth // GROUP, hidden), F32), ((clip_out.shape[2], 2, depth), F32)],
        raw=clips,
        limit=SMALL,
        free=(0, 1),
    )
    return grad_tokens, grad_in[None], grad_clip_out.transpose(1, 0, 2)[None]


def solution(mesh):
    return jax.shard_map(
        body,
        mesh=mesh,
        in_specs=(
            P(("expert", "dp"), None),
            P(("expert", "dp"), None),
            P(("expert", "dp"), None),
            P(("expert", "dp"), None),
            P("expert", None, "dp", None),
            P("expert", None, "dp"),
            P("expert", None, None, None, None),
            P("expert", None, None, None, None),
            P("expert", None, None, None),
            P("expert", None, None, None),
        ),
        out_specs=(
            P(("expert", "dp"), None),
            P("expert", None, None, "dp", None),
            P("expert", None, None, "dp"),
        ),
        check_vma=False,
    )
```

```python
import functools

import jax
import jax.numpy as jnp
from jax import lax
from jax.experimental import pallas as pl
from jax.experimental.pallas import tpu as pltpu
from jax.sharding import PartitionSpec as P

GROUP = 128
PACK = 3
CHUNK = 16
TILE = 256
LIMIT = 24 * 1024 * 1024
SMALL = 8 * 1024 * 1024
TINY = 1024 * 1024
F32 = jnp.float32
BF16 = jnp.bfloat16


def dot_nn(a, b):
    return lax.dot_general(a, b, (((1,), (0,)), ((), ())), preferred_element_type=F32)


def dot_nt(a, b):
    return lax.dot_general(a, b, (((1,), (1,)), ((), ())), preferred_element_type=F32)


def dot_tn(a, b):
    return lax.dot_general(a, b, (((0,), (0,)), ((), ())), preferred_element_type=F32)


def sigmoid(v):
    return 1.0 / (1.0 + jnp.exp(-v))


def plane_order(size, back=False):
    third = size // PACK
    row = lax.broadcasted_iota(jnp.int32, (size, size), 1 if back else 0)
    col = lax.broadcasted_iota(jnp.int32, (size, size), 0 if back else 1)
    plane = jnp.zeros_like(col)
    for j in range(1, PACK):
        plane = plane + (col >= j * third).astype(jnp.int32)
    return (row == PACK * (col - plane * third) + plane).astype(F32).astype(BF16)


def three_parts(a):
    high = a.astype(BF16)
    rest = a - high.astype(F32)
    middle = rest.astype(BF16)
    low = (rest - middle.astype(F32)).astype(BF16)
    return high, middle, low


def placed(a, order):
    parts = [dot_nn(part, order) for part in three_parts(a)]
    return parts[0] + parts[1] + parts[2]


ANYWHERE = pl.BlockSpec(memory_space=pl.ANY)
INSIDE = pl.BlockSpec(memory_space=pltpu.VMEM)


class Calls:
    def __init__(self, keep):
        self.keep = keep

    def pin(self, array):
        return pltpu.with_memory_space_constraint(array, pltpu.VMEM) if self.keep else array

    def out(self, shape, dtype):
        return pltpu.VMEM(shape, dtype) if self.keep else jax.ShapeDtypeStruct(shape, dtype)

    def run(self, kernel, name, inputs, outputs, after=(), alias=None, limit=LIMIT, raw=(), late=0, free=()):
        count, given = len(inputs), len(raw)

        def wrapped(*refs):
            outs = refs[given + count + len(after) : given + count + len(after) + len(outputs)]
            scratch = refs[len(refs) - given - 1 : len(refs) - 1] if raw else ()
            copies = [
                pltpu.make_async_copy(refs[i], scratch[i], refs[-1].at[i]) for i in range(given)
            ]
            for copy in copies:
                copy.start()
            for copy in copies[late:]:
                copy.wait()
            waits = [copy.wait for copy in copies[:late]]
            kernel(*waits, *scratch, *refs[given : given + count], *outs)

        scratch = [pltpu.VMEM(a.shape, a.dtype) for a in raw]
        return pl.pallas_call(
            wrapped,
            in_specs=[ANYWHERE] * given + [INSIDE] * count + [ANYWHERE] * len(after),
            out_specs=[INSIDE] * len(outputs),
            out_shape=[
                jax.ShapeDtypeStruct(shape, dtype) if i in free else self.out(shape, dtype)
                for i, (shape, dtype) in enumerate(outputs)
            ],
            scratch_shapes=scratch + ([pltpu.SemaphoreType.DMA((given,))] if raw else []),
            input_output_aliases=alias or {},
            compiler_params=pltpu.CompilerParams(vmem_limit_bytes=limit),
            cost_estimate=pl.CostEstimate(flops=0, bytes_accessed=0, transcendentals=0),
            name=name,
        )(*[pltpu.with_memory_space_constraint(a, pltpu.HBM) for a in raw], *[self.pin(a) for a in inputs], *after)


def pack_kernel(experts, token_ref, grad_ref, ids_ref, weights_ref, out_ref):
    rows, width = grad_ref.shape
    extra = out_ref.shape[1] - 2 * width
    out_ref[:, :width] = token_ref[...]
    out_ref[:, width : 2 * width] = grad_ref[...]
    line = lax.broadcasted_iota(jnp.int32, (extra, rows), 0)
    part = sum((line >= i * experts).astype(jnp.int32) for i in range(1, 4))
    expert = jnp.where(part < 3, line - part * experts, -1)
    table = jnp.zeros((extra, rows), F32)
    for k in range(ids_ref.shape[0]):
        table = table + jnp.where(ids_ref[k : k + 1, :] == expert, weights_ref[k : k + 1, :], 0.0)
    high, middle, low = three_parts(table)
    split = jnp.where(
        part == 0,
        high.astype(F32),
        jnp.where(part == 1, middle.astype(F32), low.astype(F32)),
    ).astype(BF16)
    same = lax.broadcasted_iota(jnp.int32, (extra, extra), 0) == lax.broadcasted_iota(jnp.int32, (extra, extra), 1)
    out_ref[:, 2 * width :] = dot_tn(split, same.astype(F32).astype(BF16)).astype(BF16)


def weight_kernel(wait_in, wait_out, codes_in, codes_out, clip_in, range_in, clip_out, range_out, w_ref):
    dp = lax.axis_index("dp")
    depth, third = codes_in.shape[1:]
    hidden = clip_in.shape[3]
    groups = depth // GROUP
    own = pl.ds(pl.multiple_of(dp * groups, groups), groups)
    order = plane_order(hidden)
    for p in range(2):
        upper = sigmoid(clip_in[p, 0, own, :]) * range_in[p, 0, own, :]
        lower = sigmoid(clip_in[p, 1, own, :]) * range_in[p, 1, own, :]
        ends = placed(jnp.concatenate([(upper + lower) / 15.0, lower], axis=0), order)
        if p == 0:
            wait_in()
        for g in range(groups):
            packed = codes_in[p, g * GROUP : (g + 1) * GROUP, :]
            for j in range(PACK):
                code = jnp.bitwise_and(jnp.right_shift(packed, 4 * j), 15).astype(F32)
                cols = slice(j * third, (j + 1) * third)
                w_ref[p, g * GROUP : (g + 1) * GROUP, cols] = (
                    ends[g : g + 1, cols] * code - ends[groups + g : groups + g + 1, cols]
                ).astype(BF16)
    own = pl.ds(pl.multiple_of(dp * depth, depth), depth)
    step, lower = [], []
    for g in range(clip_out.shape[0]):
        upper_end = sigmoid(clip_out[g, 0:1, own]) * range_out[g, 0:1, own]
        lower_end = sigmoid(clip_out[g, 1:2, own]) * range_out[g, 1:2, own]
        step.append((upper_end + lower_end) / 15.0)
        lower.append(lower_end)
    row = lax.broadcasted_iota(jnp.int32, (CHUNK, 1), 0)
    wait_out()
    for start in range(0, third, CHUNK):
        packed = codes_out[start : start + CHUNK, :]
        for j in range(PACK):
            first = (PACK * start + j) // GROUP
            last = (PACK * (start + CHUNK - 1) + j) // GROUP
            step_rows, lower_rows = step[first], lower[first]
            for g in range(first + 1, last + 1):
                late = PACK * (row + start) + j >= g * GROUP
                step_rows = jnp.where(late, step[g], step_rows)
                lower_rows = jnp.where(late, lower[g], lower_rows)
            code = jnp.bitwise_and(jnp.right_shift(packed, 4 * j), 15).astype(F32)
            down = (step_rows * code - lower_rows).astype(BF16)
            for q in range(depth // third):
                w_ref[2, q * third + start : q * third + start + CHUNK, j * third : (j + 1) * third] = down[
                    :, q * third : (q + 1) * third
                ]


def set_kernel(experts, first, keep, count, *refs):
    blocks, sides = refs[:count], refs[count : count + 2]
    earlier = refs[count + 2 : count + 6]
    refs = refs[count + 2 :] if first == 0 else refs[count + 6 :]
    partials = refs[0:4]
    x_ref, s_ref, h_ref, g_ref = refs[4:8]
    rows, width = partials[0].shape
    half = width // 2
    hidden = h_ref.shape[1]
    third = hidden // PACK
    dp, mine = lax.axis_index("dp"), lax.axis_index("expert")
    spans = (
        pl.ds(pl.multiple_of(dp * half, half), half),
        pl.ds(pl.multiple_of((1 - dp) * half, half), half),
    )
    here = slice(first, first + 4 * rows)
    if first and not keep:
        for old, new in zip(earlier, refs[4:8]):
            new[..., :first, :] = old[..., :first, :]
    start = first
    for block in blocks:
        span = slice(start, start + block.shape[0])
        start = span.stop
        x_ref[span, :] = block[:, :width]
        beside = block[:, 2 * width :].astype(F32)
        lane = lax.broadcasted_iota(jnp.int32, beside.shape, 1)
        keep = (lane == mine) | (lane == mine + experts) | (lane == mine + 2 * experts)
        scale = jnp.sum(jnp.where(keep, beside, 0.0), axis=1, keepdims=True)
        s_ref[span, :] = (scale * block[:, width : 2 * width].astype(F32)).astype(BF16)
    for j in range(PACK):
        cols = slice(j * third, (j + 1) * third)
        gate_pre = dot_nn(x_ref[here, spans[0]], sides[0][0, :, cols]) + dot_nn(
            x_ref[here, spans[1]], sides[1][0, :, cols]
        )
        up_pre = dot_nn(x_ref[here, spans[0]], sides[0][1, :, cols]) + dot_nn(
            x_ref[here, spans[1]], sides[1][1, :, cols]
        )
        grad_hidden = 0.0
        for side in range(2):
            for q in range(half // third):
                tile = pl.ds(pl.multiple_of((dp if side == 0 else 1 - dp) * half + q * third, third), third)
                grad_hidden = grad_hidden + dot_nt(
                    s_ref[here, tile], sides[side][2, q * third : (q + 1) * third, cols]
                )
        sig = sigmoid(gate_pre)
        act = gate_pre * sig
        h_ref[here, cols] = (act * up_pre).astype(BF16)
        g_ref[0, here, cols] = (grad_hidden * up_pre * sig * (1.0 + gate_pre * (1.0 - sig))).astype(BF16)
        g_ref[1, here, cols] = (grad_hidden * act).astype(BF16)
    for side in range(2):
        base = jnp.where(side == 0, dp, 1 - dp) * half

        @pl.loop(0, half // TILE)
        def _(n):
            depth = pl.ds(pl.multiple_of(n * TILE, TILE), TILE)
            part = dot_nt(g_ref[0, here, :], sides[side][0, depth, :]) + dot_nt(
                g_ref[1, here, :], sides[side][1, depth, :]
            )
            cols = pl.ds(pl.multiple_of(base + n * TILE, TILE), TILE)
            for i in range(4):
                partials[i][:, cols] = part[i * rows : (i + 1) * rows, :].astype(BF16)


def run_set(calls, blocks, weights, experts, pair=None, after=()):
    rows, width = blocks[0].shape[0], 2 * weights[0].shape[1]
    hidden = weights[0].shape[2]
    both = 8 * rows
    stored = [((both, width), BF16), ((both, width), BF16), ((both, hidden), BF16), ((2, both, hidden), BF16)]
    out = calls.run(
        functools.partial(set_kernel, experts, 0 if pair is None else 4 * rows, calls.keep, len(blocks)),
        "expert_set",
        [*blocks, *weights, *(pair or ())],
        [((rows, width), BF16)] * 4 + stored,
        after=after,
        alias=None if pair is None else {len(blocks) + 2 + i: 4 + i for i in range(4)},
    )
    return list(out[:4]), list(out[4:])


def group_marks(size, count, span, planes):
    row = lax.broadcasted_iota(jnp.int32, (size, count), 0)
    group = lax.broadcasted_iota(jnp.int32, (size, count), 1)
    if planes > 1:
        third = size // planes
        plane = jnp.zeros_like(row)
        for j in range(1, planes):
            plane = plane + (row >= j * third).astype(jnp.int32)
        row = planes * (row - plane * third) + plane
    return ((row >= group * span) & (row < (group + 1) * span)).astype(F32).astype(BF16)


def two_parts(a):
    high = a.astype(BF16)
    return high, (a - high.astype(F32)).astype(BF16)


def sums_kernel(other, more, x_ref, s_ref, h_ref, g_ref, weights, *refs):
    old_in, old_out = refs[:2] if more else (None, None)
    sums_in, sums_out = refs[-2:]
    width = x_ref.shape[1]
    half = width // 2
    hidden = h_ref.shape[1]
    third = hidden // PACK
    share = sums_in.shape[2]
    groups_out = sums_out.shape[1]
    dp = lax.axis_index("dp")
    base = (1 - dp if other else dp) * half
    span = pl.ds(pl.multiple_of(base, half), half)

    def since(old, found, *where):
        return old[where] + found if more else found

    row_sums = two_parts(dot_nn(x_ref[:, span], group_marks(half, share, GROUP, 1)))
    for p in range(2):
        found = dot_tn(row_sums[0], g_ref[p]) + dot_tn(row_sums[1], g_ref[p])
        sums_in[p, 1] = since(old_in, found, p, 1)
    hidden_sums = two_parts(dot_nn(h_ref[...], group_marks(hidden, groups_out, GROUP, PACK)))
    found = dot_tn(hidden_sums[0], s_ref[:, span]) + dot_tn(hidden_sums[1], s_ref[:, span])
    sums_out[1] = since(old_out, found, 1)

    @pl.loop(0, half // third)
    def _(t):
        rows = pl.ds(pl.multiple_of(t * third, third), third)
        span = pl.ds(pl.multiple_of(base + t * third, third), third)
        x_cols = x_ref[:, span]
        for p in range(2):
            weighted = dot_tn(x_cols, g_ref[p]) * weights[p, rows, :].astype(F32)
            for g in range(third // GROUP):
                spot = pl.ds(t * (third // GROUP) + g, 1)
                found = jnp.sum(weighted[g * GROUP : (g + 1) * GROUP], axis=0, keepdims=True)
                sums_in[p, 0, spot, :] = since(old_in, found, p, 0, spot, slice(None))
        down = jnp.concatenate([weights[2, rows, j * third : (j + 1) * third] for j in range(PACK)], axis=0)
        weighted = dot_tn(h_ref[...], s_ref[:, span]) * down.astype(F32)
        for g in range(groups_out):
            found = None
            for j in range(PACK):
                low = -((j - GROUP * g) // PACK)
                high = -((j - GROUP * (g + 1)) // PACK)
                inner, outer = -(-low // 8) * 8, high // 8 * 8
                part = jnp.sum(weighted[j * third + inner : j * third + outer], axis=0, keepdims=True)
                found = part if found is None else found + part
                for start in sorted(({low // 8 * 8} if low % 8 else set()) | ({outer} if high % 8 else set())):
                    block = weighted[j * third + start : j * third + start + 8]
                    row = lax.broadcasted_iota(jnp.int32, block.shape, 0) + start
                    inside = (row >= low) & (row < high)
                    found = found + jnp.sum(jnp.where(inside, block, 0.0), axis=0, keepdims=True)
            sums_out[0, g : g + 1, rows] = since(old_out, found, 0, slice(g, g + 1), rows)


def run_sums(calls, stored, weights, other, before, shapes, after=()):
    side = weights[1] if other else weights[0]
    return calls.run(
        functools.partial(sums_kernel, other, before is not None),
        "group_sums",
        [*stored, side, *(before or ())],
        [(shape, F32) for shape in shapes],
        after=after,
    )


def clip_kernel(clip_in, range_in, clip_out, range_out, mine_in, got_in, mine_out, got_out, in_ref, out_ref):
    dp = lax.axis_index("dp")
    hidden = clip_in.shape[3]
    groups = in_ref.shape[2]
    share = out_ref.shape[2]
    back = plane_order(hidden, True)

    def finish(weighted, plain, clip, span):
        sig_upper, sig_lower = sigmoid(clip[0]), sigmoid(clip[1])
        upper, lower = sig_upper * span[0], sig_lower * span[1]
        upper_sum = (weighted + lower * plain) / (upper + lower)
        lower_sum = upper_sum - plain
        return (
            upper_sum * span[0] * sig_upper * (1.0 - sig_upper),
            lower_sum * span[1] * sig_lower * (1.0 - sig_lower),
        )

    own = pl.ds(pl.multiple_of(dp * groups, groups), groups)
    for p in range(2):
        sums = jnp.concatenate(
            [mine_in[p, 0] + got_in[p, 0], mine_in[p, 1] + got_in[p, 1]], axis=0
        )
        natural = placed(sums, back)
        in_ref[p, 0], in_ref[p, 1] = finish(
            natural[:groups],
            natural[groups:],
            [clip_in[p, i, own, :] for i in range(2)],
            [range_in[p, i, own, :] for i in range(2)],
        )
    own = pl.ds(pl.multiple_of(dp * share, share), share)
    for g in range(out_ref.shape[0]):
        out_ref[g, 0:1, :], out_ref[g, 1:2, :] = finish(
            mine_out[0, g : g + 1, :] + got_out[0, g : g + 1, :],
            mine_out[1, g : g + 1, :] + got_out[1, g : g + 1, :],
            [clip_out[g, i : i + 1, own] for i in range(2)],
            [range_out[g, i : i + 1, own] for i in range(2)],
        )


def add_kernel(*refs):
    total = refs[0][...].astype(F32)
    for ref in refs[1:-1]:
        total = total + ref[...].astype(F32)
    refs[-1][...] = total.astype(refs[-1].dtype)


def hold_kernel(*refs):
    pass


def body(
    tokens,
    grad_out,
    expert_ids,
    router_weights,
    codes_in,
    codes_out,
    clip_in,
    range_in,
    clip_out,
    range_out,
):
    experts = lax.axis_size("expert")
    rows, width = tokens.shape
    hidden = clip_in.shape[4]
    depth = codes_in.shape[2]
    extra = -(-3 * experts // 128) * 128
    calls = Calls(experts * rows * (3 * width + extra) * 2 < 2**24)

    def swap(array, mask):
        return lax.ppermute(array, "expert", [(i, i ^ mask) for i in range(experts)])

    def swap_core(array):
        return lax.ppermute(array, "dp", [(0, 1), (1, 0)])

    def added(*parts, after=(), free=()):
        return calls.run(
            add_kernel, "add_rows", list(parts), [(parts[0].shape, BF16)], after=after, limit=SMALL, free=free
        )[0]

    def held(array, *after):
        return pl.pallas_call(
            hold_kernel,
            in_specs=[ANYWHERE] * (1 + len(after)),
            out_specs=ANYWHERE,
            out_shape=calls.out(array.shape, array.dtype),
            input_output_aliases={0: 0},
            compiler_params=pltpu.CompilerParams(vmem_limit_bytes=TINY),
            cost_estimate=pl.CostEstimate(flops=0, bytes_accessed=0, transcendentals=0),
            name="hold",
        )(calls.pin(array), *after)

    packed = calls.run(
        functools.partial(pack_kernel, experts),
        "pack_rows",
        [],
        [((rows, 2 * width + extra), BF16)],
        raw=(tokens, grad_out, expert_ids.T, router_weights.T),
        limit=SMALL,
    )[0]

    clips = (clip_in[0], range_in[0], clip_out[0].transpose(1, 0, 2), range_out[0].transpose(1, 0, 2))
    shapes = ((2, 2, depth // GROUP, hidden), (2, clip_out.shape[2], depth))
    sums = {True: None, False: None}

    def dequantized(*after):
        (own_weights,) = calls.run(
            weight_kernel,
            "make_weights",
            [],
            [((3, depth, hidden), BF16)],
            raw=(codes_in[0], codes_out[0], *clips),
            late=2,
            after=after,
        )
        return own_weights, swap_core(own_weights)

    cut = rows // 2

    def crossed(over_x, over_y):
        return swap(over_x[:cut], 2), swap(over_y[cut:], 1)

    def quad(head, weights, after):
        near, far = swap(head, 4), swap(head, 8)
        x0, y0 = swap(head, 1), swap(head, 2)
        if weights is None:
            weights = dequantized(head)
        d0 = crossed(x0, y0)
        last = swap(far, 4)
        ready = held(near, x0, y0, weights[1])
        x1, y1 = swap(ready, 1), swap(ready, 2)
        d1 = tuple(swap(part, 4) for part in d0)
        ready = held(far, x1, y1, *d0, *d1)
        x2, y2 = swap(ready, 1), swap(ready, 2)
        d2 = crossed(x2, y2)
        d3 = tuple(swap(part, 4) for part in d2)
        p0, stored = run_set(calls, (head, x0, y0, *d0), weights, experts, after=after)
        p1, stored = run_set(calls, (near, x1, y1, *d1), weights, experts, stored)
        ready = held(last, x2, y2, p0[0], p1[0])
        x3, y3 = swap(ready, 1), swap(ready, 2)
        other = run_sums(calls, stored, weights, True, sums[True], shapes)
        p2, later = run_set(calls, (far, x2, y2, *d2), weights, experts, after=(other[0],))
        p3, later = run_set(calls, (last, x3, y3, *d3), weights, experts, later)
        sums[True] = run_sums(calls, later, weights, True, other, shapes)
        y_sum3 = added(p3[2], swap(p3[3], 1), after=(sums[True][0],))
        mine = run_sums(calls, stored, weights, False, sums[False], shapes, (y_sum3,))
        x_sum2 = added(p2[1], swap(p2[3], 2))
        total2 = added(p2[0], swap(x_sum2, 1), swap(p2[2], 2))
        total3 = added(p3[0], swap(p3[1], 1), swap(y_sum3, 2), after=(mine[0],))
        sums[False] = run_sums(calls, later, weights, False, mine, shapes, (total3,))
        y_sum1 = added(p1[2], swap(p1[3], 1))
        total1 = added(p1[0], swap(p1[1], 1), swap(y_sum1, 2))
        x_sum0 = added(p0[1], swap(p0[3], 2))
        parts = (
            p0[0],
            swap(x_sum0, 1),
            swap(p0[2], 2),
            swap(total1, 4),
            swap(total2, 8),
            swap(total3, 12),
        )
        return parts, weights

    final, after, weights = [], (), None
    for base in range(0, experts, 16):
        parts, weights = quad(swap(packed, base) if base else packed, weights, after)
        final += [swap(added(*parts), base)] if base else parts
        after = (sums[False][0],)
    grad_tokens = added(*final, free=(0,))

    mine_in, mine_out = sums[False]
    got_in, got_out = (swap_core(a) for a in sums[True])
    grad_in, grad_clip_out = calls.run(
        clip_kernel,
        "clip_gradients",
        [mine_in, got_in, mine_out, got_out],
        [((2, 2, depth // GROUP, hidden), F32), ((clip_out.shape[2], 2, depth), F32)],
        raw=clips,
        limit=SMALL,
        free=(0, 1),
    )
    return grad_tokens, grad_in[None], grad_clip_out.transpose(1, 0, 2)[None]


def solution(mesh):
    return jax.shard_map(
        body,
        mesh=mesh,
        in_specs=(
            P(("expert", "dp"), None),
            P(("expert", "dp"), None),
            P(("expert", "dp"), None),
            P(("expert", "dp"), None),
            P("expert", None, "dp", None),
            P("expert", None, "dp"),
            P("expert", None, None, None, None),
            P("expert", None, None, None, None),
            P("expert", None, None, None),
            P("expert", None, None, None),
        ),
        out_specs=(
            P(("expert", "dp"), None),
            P("expert", None, None, "dp", None),
            P("expert", None, None, "dp"),
        ),
        check_vma=False,
    )
```

```python
import functools

import jax
import jax.numpy as jnp
from jax import lax
from jax.experimental import pallas as pl
from jax.experimental.pallas import tpu as pltpu
from jax.sharding import PartitionSpec as P

GROUP = 128
PACK = 3
CHUNK = 16
TILE = 256
LIMIT = 24 * 1024 * 1024
SMALL = 8 * 1024 * 1024
F32 = jnp.float32
BF16 = jnp.bfloat16


def dot_nn(a, b):
    return lax.dot_general(a, b, (((1,), (0,)), ((), ())), preferred_element_type=F32)


def dot_nt(a, b):
    return lax.dot_general(a, b, (((1,), (1,)), ((), ())), preferred_element_type=F32)


def dot_tn(a, b):
    return lax.dot_general(a, b, (((0,), (0,)), ((), ())), preferred_element_type=F32)


def sigmoid(v):
    return 1.0 / (1.0 + jnp.exp(-v))


def plane_order(size, back=False):
    third = size // PACK
    row = lax.broadcasted_iota(jnp.int32, (size, size), 1 if back else 0)
    col = lax.broadcasted_iota(jnp.int32, (size, size), 0 if back else 1)
    plane = jnp.zeros_like(col)
    for j in range(1, PACK):
        plane = plane + (col >= j * third).astype(jnp.int32)
    return (row == PACK * (col - plane * third) + plane).astype(F32).astype(BF16)


def three_parts(a):
    high = a.astype(BF16)
    rest = a - high.astype(F32)
    middle = rest.astype(BF16)
    low = (rest - middle.astype(F32)).astype(BF16)
    return high, middle, low


def placed(a, order):
    parts = [dot_nn(part, order) for part in three_parts(a)]
    return parts[0] + parts[1] + parts[2]


ANYWHERE = pl.BlockSpec(memory_space=pl.ANY)
INSIDE = pl.BlockSpec(memory_space=pltpu.VMEM)


class Calls:
    def __init__(self, keep):
        self.keep = keep

    def pin(self, array):
        return pltpu.with_memory_space_constraint(array, pltpu.VMEM) if self.keep else array

    def out(self, shape, dtype):
        return pltpu.VMEM(shape, dtype) if self.keep else jax.ShapeDtypeStruct(shape, dtype)

    def run(self, kernel, name, inputs, outputs, after=(), alias=None, limit=LIMIT, raw=(), free=(), flops=0):
        count, given = len(inputs), len(raw)

        def wrapped(*refs):
            outs = refs[given + count + len(after) : given + count + len(after) + len(outputs)]
            scratch = refs[len(refs) - given - 1 : len(refs) - 1] if raw else ()
            copies = [
                pltpu.make_async_copy(refs[i], scratch[i], refs[-1].at[i]) for i in range(given)
            ]
            for copy in copies:
                copy.start()
            for copy in copies:
                copy.wait()
            kernel(*scratch, *refs[given : given + count], *outs)

        scratch = [pltpu.VMEM(a.shape, a.dtype) for a in raw]
        return pl.pallas_call(
            wrapped,
            in_specs=[ANYWHERE] * given + [INSIDE] * count + [ANYWHERE] * len(after),
            out_specs=[INSIDE] * len(outputs),
            out_shape=[
                jax.ShapeDtypeStruct(shape, dtype) if i in free else self.out(shape, dtype)
                for i, (shape, dtype) in enumerate(outputs)
            ],
            scratch_shapes=scratch + ([pltpu.SemaphoreType.DMA((given,))] if raw else []),
            input_output_aliases=alias or {},
            compiler_params=pltpu.CompilerParams(vmem_limit_bytes=limit),
            cost_estimate=pl.CostEstimate(flops=int(flops), bytes_accessed=0, transcendentals=0),
            name=name,
        )(*[pltpu.with_memory_space_constraint(a, pltpu.HBM) for a in raw], *[self.pin(a) for a in inputs], *after)


def pack_kernel(experts, token_ref, grad_ref, ids_ref, weights_ref, out_ref):
    rows, width = grad_ref.shape
    extra = out_ref.shape[1] - 2 * width
    out_ref[:, :width] = token_ref[...]
    out_ref[:, width : 2 * width] = grad_ref[...]
    line = lax.broadcasted_iota(jnp.int32, (extra, rows), 0)
    part = sum((line >= i * experts).astype(jnp.int32) for i in range(1, 4))
    expert = jnp.where(part < 3, line - part * experts, -1)
    table = jnp.zeros((extra, rows), F32)
    for k in range(ids_ref.shape[0]):
        table = table + jnp.where(ids_ref[k : k + 1, :] == expert, weights_ref[k : k + 1, :], 0.0)
    high, middle, low = three_parts(table)
    split = jnp.where(
        part == 0,
        high.astype(F32),
        jnp.where(part == 1, middle.astype(F32), low.astype(F32)),
    ).astype(BF16)
    same = lax.broadcasted_iota(jnp.int32, (extra, extra), 0) == lax.broadcasted_iota(jnp.int32, (extra, extra), 1)
    out_ref[:, 2 * width :] = dot_tn(split, same.astype(F32).astype(BF16)).astype(BF16)


def weight_kernel(codes_in, codes_out, clip_in, range_in, clip_out, range_out, w_ref):
    dp = lax.axis_index("dp")
    depth, third = codes_in.shape[1:]
    hidden = clip_in.shape[3]
    groups = depth // GROUP
    own = pl.ds(pl.multiple_of(dp * groups, groups), groups)
    order = plane_order(hidden)
    for p in range(2):
        upper = sigmoid(clip_in[p, 0, own, :]) * range_in[p, 0, own, :]
        lower = sigmoid(clip_in[p, 1, own, :]) * range_in[p, 1, own, :]
        ends = placed(jnp.concatenate([(upper + lower) / 15.0, lower], axis=0), order)
        for g in range(groups):
            packed = codes_in[p, g * GROUP : (g + 1) * GROUP, :]
            for j in range(PACK):
                code = jnp.bitwise_and(jnp.right_shift(packed, 4 * j), 15).astype(F32)
                cols = slice(j * third, (j + 1) * third)
                w_ref[p, g * GROUP : (g + 1) * GROUP, cols] = (
                    ends[g : g + 1, cols] * code - ends[groups + g : groups + g + 1, cols]
                ).astype(BF16)
    own = pl.ds(pl.multiple_of(dp * depth, depth), depth)
    step, lower = [], []
    for g in range(clip_out.shape[0]):
        upper_end = sigmoid(clip_out[g, 0:1, own]) * range_out[g, 0:1, own]
        lower_end = sigmoid(clip_out[g, 1:2, own]) * range_out[g, 1:2, own]
        step.append((upper_end + lower_end) / 15.0)
        lower.append(lower_end)
    row = lax.broadcasted_iota(jnp.int32, (CHUNK, 1), 0)
    for start in range(0, third, CHUNK):
        packed = codes_out[start : start + CHUNK, :]
        for j in range(PACK):
            first = (PACK * start + j) // GROUP
            last = (PACK * (start + CHUNK - 1) + j) // GROUP
            step_rows, lower_rows = step[first], lower[first]
            for g in range(first + 1, last + 1):
                late = PACK * (row + start) + j >= g * GROUP
                step_rows = jnp.where(late, step[g], step_rows)
                lower_rows = jnp.where(late, lower[g], lower_rows)
            code = jnp.bitwise_and(jnp.right_shift(packed, 4 * j), 15).astype(F32)
            down = (step_rows * code - lower_rows).astype(BF16)
            for q in range(depth // third):
                w_ref[2, q * third + start : q * third + start + CHUNK, j * third : (j + 1) * third] = down[
                    :, q * third : (q + 1) * third
                ]


def set_kernel(experts, first, keep, count, *refs):
    blocks, sides = refs[:count], refs[count : count + 2]
    earlier = refs[count + 2 : count + 6]
    refs = refs[count + 2 :] if first == 0 else refs[count + 6 :]
    partials = refs[0:4]
    x_ref, s_ref, h_ref, g_ref = refs[4:8]
    rows, width = partials[0].shape
    half = width // 2
    hidden = h_ref.shape[1]
    third = hidden // PACK
    dp, mine = lax.axis_index("dp"), lax.axis_index("expert")
    spans = (
        pl.ds(pl.multiple_of(dp * half, half), half),
        pl.ds(pl.multiple_of((1 - dp) * half, half), half),
    )
    here = slice(first, first + 4 * rows)
    if first and not keep:
        for old, new in zip(earlier, refs[4:8]):
            new[..., :first, :] = old[..., :first, :]
    start = first
    for block in blocks:
        span = slice(start, start + block.shape[0])
        start = span.stop
        x_ref[span, :] = block[:, :width]
        beside = block[:, 2 * width :].astype(F32)
        lane = lax.broadcasted_iota(jnp.int32, beside.shape, 1)
        keep = (lane == mine) | (lane == mine + experts) | (lane == mine + 2 * experts)
        scale = jnp.sum(jnp.where(keep, beside, 0.0), axis=1, keepdims=True)
        s_ref[span, :] = (scale * block[:, width : 2 * width].astype(F32)).astype(BF16)
    for j in range(PACK):
        cols = slice(j * third, (j + 1) * third)
        gate_pre = dot_nn(x_ref[here, spans[0]], sides[0][0, :, cols]) + dot_nn(
            x_ref[here, spans[1]], sides[1][0, :, cols]
        )
        up_pre = dot_nn(x_ref[here, spans[0]], sides[0][1, :, cols]) + dot_nn(
            x_ref[here, spans[1]], sides[1][1, :, cols]
        )
        grad_hidden = 0.0
        for side in range(2):
            for q in range(half // third):
                tile = pl.ds(pl.multiple_of((dp if side == 0 else 1 - dp) * half + q * third, third), third)
                grad_hidden = grad_hidden + dot_nt(
                    s_ref[here, tile], sides[side][2, q * third : (q + 1) * third, cols]
                )
        sig = sigmoid(gate_pre)
        act = gate_pre * sig
        h_ref[here, cols] = (act * up_pre).astype(BF16)
        g_ref[0, here, cols] = (grad_hidden * up_pre * sig * (1.0 + gate_pre * (1.0 - sig))).astype(BF16)
        g_ref[1, here, cols] = (grad_hidden * act).astype(BF16)
    for side in range(2):
        base = jnp.where(side == 0, dp, 1 - dp) * half

        @pl.loop(0, half // TILE)
        def _(n):
            depth = pl.ds(pl.multiple_of(n * TILE, TILE), TILE)
            part = dot_nt(g_ref[0, here, :], sides[side][0, depth, :]) + dot_nt(
                g_ref[1, here, :], sides[side][1, depth, :]
            )
            cols = pl.ds(pl.multiple_of(base + n * TILE, TILE), TILE)
            for i in range(4):
                partials[i][:, cols] = part[i * rows : (i + 1) * rows, :].astype(BF16)


def run_set(calls, blocks, weights, experts, pair=None, after=()):
    rows, width = blocks[0].shape[0], 2 * weights[0].shape[1]
    hidden = weights[0].shape[2]
    both = 8 * rows
    stored = [((both, width), BF16), ((both, width), BF16), ((both, hidden), BF16), ((2, both, hidden), BF16)]
    out = calls.run(
        functools.partial(set_kernel, experts, 0 if pair is None else 4 * rows, calls.keep, len(blocks)),
        "expert_set",
        [*blocks, *weights, *(pair or ())],
        [((rows, width), BF16)] * 4 + stored,
        after=after,
        flops=40 * rows * width * hidden,
        alias=None if pair is None else {len(blocks) + 2 + i: 4 + i for i in range(4)},
    )
    return list(out[:4]), list(out[4:])


def group_marks(size, count, span, planes):
    row = lax.broadcasted_iota(jnp.int32, (size, count), 0)
    group = lax.broadcasted_iota(jnp.int32, (size, count), 1)
    if planes > 1:
        third = size // planes
        plane = jnp.zeros_like(row)
        for j in range(1, planes):
            plane = plane + (row >= j * third).astype(jnp.int32)
        row = planes * (row - plane * third) + plane
    return ((row >= group * span) & (row < (group + 1) * span)).astype(F32).astype(BF16)


def two_parts(a):
    high = a.astype(BF16)
    return high, (a - high.astype(F32)).astype(BF16)


def sums_kernel(other, more, x_ref, s_ref, h_ref, g_ref, weights, *refs):
    old_in, old_out = refs[:2] if more else (None, None)
    sums_in, sums_out = refs[-2:]
    width = x_ref.shape[1]
    half = width // 2
    hidden = h_ref.shape[1]
    third = hidden // PACK
    share = sums_in.shape[2]
    groups_out = sums_out.shape[1]
    dp = lax.axis_index("dp")
    base = (1 - dp if other else dp) * half
    span = pl.ds(pl.multiple_of(base, half), half)

    def since(old, found, *where):
        return old[where] + found if more else found

    row_sums = two_parts(dot_nn(x_ref[:, span], group_marks(half, share, GROUP, 1)))
    for p in range(2):
        found = dot_tn(row_sums[0], g_ref[p]) + dot_tn(row_sums[1], g_ref[p])
        sums_in[p, 1] = since(old_in, found, p, 1)
    hidden_sums = two_parts(dot_nn(h_ref[...], group_marks(hidden, groups_out, GROUP, PACK)))
    found = dot_tn(hidden_sums[0], s_ref[:, span]) + dot_tn(hidden_sums[1], s_ref[:, span])
    sums_out[1] = since(old_out, found, 1)

    @pl.loop(0, half // third)
    def _(t):
        rows = pl.ds(pl.multiple_of(t * third, third), third)
        span = pl.ds(pl.multiple_of(base + t * third, third), third)
        x_cols = x_ref[:, span]
        for p in range(2):
            weighted = dot_tn(x_cols, g_ref[p]) * weights[p, rows, :].astype(F32)
            for g in range(third // GROUP):
                spot = pl.ds(t * (third // GROUP) + g, 1)
                found = jnp.sum(weighted[g * GROUP : (g + 1) * GROUP], axis=0, keepdims=True)
                sums_in[p, 0, spot, :] = since(old_in, found, p, 0, spot, slice(None))
        down = jnp.concatenate([weights[2, rows, j * third : (j + 1) * third] for j in range(PACK)], axis=0)
        weighted = dot_tn(h_ref[...], s_ref[:, span]) * down.astype(F32)
        for g in range(groups_out):
            found = None
            for j in range(PACK):
                low = -((j - GROUP * g) // PACK)
                high = -((j - GROUP * (g + 1)) // PACK)
                inner, outer = -(-low // 8) * 8, high // 8 * 8
                part = jnp.sum(weighted[j * third + inner : j * third + outer], axis=0, keepdims=True)
                found = part if found is None else found + part
                for start in sorted(({low // 8 * 8} if low % 8 else set()) | ({outer} if high % 8 else set())):
                    block = weighted[j * third + start : j * third + start + 8]
                    row = lax.broadcasted_iota(jnp.int32, block.shape, 0) + start
                    inside = (row >= low) & (row < high)
                    found = found + jnp.sum(jnp.where(inside, block, 0.0), axis=0, keepdims=True)
            sums_out[0, g : g + 1, rows] = since(old_out, found, 0, slice(g, g + 1), rows)


def run_sums(calls, stored, weights, other, before, shapes, after=()):
    side = weights[1] if other else weights[0]
    return calls.run(
        functools.partial(sums_kernel, other, before is not None),
        "group_sums",
        [*stored, side, *(before or ())],
        [(shape, F32) for shape in shapes],
        after=after,
        flops=24 * stored[0].shape[0] * weights[0].size // 8,
    )


def clip_kernel(clip_in, range_in, clip_out, range_out, mine_in, got_in, mine_out, got_out, in_ref, out_ref):
    dp = lax.axis_index("dp")
    hidden = clip_in.shape[3]
    groups = in_ref.shape[2]
    share = out_ref.shape[2]
    back = plane_order(hidden, True)

    def finish(weighted, plain, clip, span):
        sig_upper, sig_lower = sigmoid(clip[0]), sigmoid(clip[1])
        upper, lower = sig_upper * span[0], sig_lower * span[1]
        upper_sum = (weighted + lower * plain) / (upper + lower)
        lower_sum = upper_sum - plain
        return (
            upper_sum * span[0] * sig_upper * (1.0 - sig_upper),
            lower_sum * span[1] * sig_lower * (1.0 - sig_lower),
        )

    own = pl.ds(pl.multiple_of(dp * groups, groups), groups)
    for p in range(2):
        sums = jnp.concatenate(
            [mine_in[p, 0] + got_in[p, 0], mine_in[p, 1] + got_in[p, 1]], axis=0
        )
        natural = placed(sums, back)
        in_ref[p, 0], in_ref[p, 1] = finish(
            natural[:groups],
            natural[groups:],
            [clip_in[p, i, own, :] for i in range(2)],
            [range_in[p, i, own, :] for i in range(2)],
        )
    own = pl.ds(pl.multiple_of(dp * share, share), share)
    for g in range(out_ref.shape[0]):
        out_ref[g, 0:1, :], out_ref[g, 1:2, :] = finish(
            mine_out[0, g : g + 1, :] + got_out[0, g : g + 1, :],
            mine_out[1, g : g + 1, :] + got_out[1, g : g + 1, :],
            [clip_out[g, i : i + 1, own] for i in range(2)],
            [range_out[g, i : i + 1, own] for i in range(2)],
        )


def add_kernel(*refs):
    total = refs[0][...].astype(F32)
    for ref in refs[1:-1]:
        total = total + ref[...].astype(F32)
    refs[-1][...] = total.astype(refs[-1].dtype)


def part_kernel(first, old, new):
    new[...] = old[first : first + new.shape[0], :]


def hold_kernel(old, new):
    new[...] = old[...]


def body(
    tokens,
    grad_out,
    expert_ids,
    router_weights,
    codes_in,
    codes_out,
    clip_in,
    range_in,
    clip_out,
    range_out,
):
    experts = lax.axis_size("expert")
    rows, width = tokens.shape
    hidden = clip_in.shape[4]
    depth = codes_in.shape[2]
    extra = -(-3 * experts // 128) * 128
    calls = Calls(experts * rows * (3 * width + extra) * 2 < 2**24)

    def swap(array, mask):
        return lax.ppermute(array, "expert", [(i, i ^ mask) for i in range(experts)])

    def swap_core(array):
        return lax.ppermute(array, "dp", [(0, 1), (1, 0)])

    def added(*parts, after=(), free=()):
        return calls.run(
            add_kernel, "add_rows", list(parts), [(parts[0].shape, BF16)], after=after, limit=SMALL, free=free
        )[0]

    def held(array, *after):
        return calls.run(hold_kernel, "hold", [array], [(array.shape, array.dtype)], after, limit=SMALL)[0]

    packed = calls.run(
        functools.partial(pack_kernel, experts),
        "pack_rows",
        [],
        [((rows, 2 * width + extra), BF16)],
        raw=(tokens, grad_out, expert_ids.T, router_weights.T),
        limit=SMALL,
    )[0]

    clips = (clip_in[0], range_in[0], clip_out[0].transpose(1, 0, 2), range_out[0].transpose(1, 0, 2))
    shapes = ((2, 2, depth // GROUP, hidden), (2, clip_out.shape[2], depth))
    sums = {True: None, False: None}

    def dequantized(*after):
        (own_weights,) = calls.run(
            weight_kernel,
            "make_weights",
            [],
            [((3, depth, hidden), BF16)],
            raw=(codes_in[0], codes_out[0], *clips),
            after=after,
        )
        return own_weights, swap_core(own_weights)

    cut = rows // 2

    def part(array, first, after):
        shape = (rows - cut if first else cut, array.shape[1])
        return calls.run(
            functools.partial(part_kernel, first), "part", [array], [(shape, array.dtype)], after, limit=SMALL
        )[0]

    def crossed(over_x, over_y, *after):
        return swap(part(over_x, 0, after), 2), swap(part(over_y, cut, after), 1)

    def quad(head, weights, after):
        near = swap(head, 4)
        x0, y0 = swap(head, 1), swap(head, 2)
        far = swap(near, 12)
        if weights is None:
            weights = dequantized(head)
        d0 = crossed(x0, y0)
        ready = held(near, x0, y0, weights[1])
        x1, y1 = swap(ready, 1), swap(ready, 2)
        d1 = tuple(swap(half, 4) for half in d0)
        p0, stored = run_set(calls, (head, x0, y0, *d0), weights, experts, after=after)
        ready = held(far, x1, y1, *d1, p0[0])
        x2, y2, last = swap(ready, 1), swap(ready, 2), swap(ready, 4)
        p1, stored = run_set(calls, (near, x1, y1, *d1), weights, experts, stored)
        ready = held(last, x2, y2)
        x3, y3 = swap(ready, 1), swap(ready, 2)
        other = run_sums(calls, stored, weights, True, sums[True], shapes)
        d2 = crossed(x2, y2, other[0])
        d3 = tuple(swap(half, 4) for half in d2)
        p2, later = run_set(calls, (far, x2, y2, *d2), weights, experts)
        mine = run_sums(calls, stored, weights, False, sums[False], shapes, (p2[0],))
        x_sum2 = added(p2[1], swap(p2[3], 2))
        p3, later = run_set(calls, (last, x3, y3, *d3), weights, experts, later, (x_sum2,))
        total2 = added(p2[0], swap(x_sum2, 1), swap(p2[2], 2))
        sums[True] = run_sums(calls, later, weights, True, other, shapes, (total2,))
        y_sum3 = added(p3[2], swap(p3[3], 1), after=(sums[True][0],))
        far_sum = swap(total2, 8)
        total3 = added(p3[0], swap(p3[1], 1), swap(y_sum3, 2), after=(far_sum,))
        sums[False] = run_sums(calls, later, weights, False, mine, shapes, (total3,))
        y_sum1 = added(p1[2], swap(held(p1[3], x3, y3), 1))
        total1 = added(p1[0], swap(p1[1], 1), swap(y_sum1, 2))
        x_sum0 = added(p0[1], swap(held(p0[3], x3, y3), 2))
        parts = (
            p0[0],
            swap(x_sum0, 1),
            swap(p0[2], 2),
            swap(total1, 4),
            far_sum,
            swap(total3, 12),
        )
        return parts, weights

    final, after, weights = [], (), None
    for base in range(0, experts, 16):
        parts, weights = quad(swap(packed, base) if base else packed, weights, after)
        final += [swap(added(*parts), base)] if base else parts
        after = (sums[False][0],)
    grad_tokens = added(*final, free=(0,))

    mine_in, mine_out = sums[False]
    got_in, got_out = (swap_core(a) for a in sums[True])
    grad_in, grad_clip_out = calls.run(
        clip_kernel,
        "clip_gradients",
        [mine_in, got_in, mine_out, got_out],
        [((2, 2, depth // GROUP, hidden), F32), ((clip_out.shape[2], 2, depth), F32)],
        raw=clips,
        limit=SMALL,
        free=(0, 1),
    )
    return grad_tokens, grad_in[None], grad_clip_out.transpose(1, 0, 2)[None]


def solution(mesh):
    return jax.shard_map(
        body,
        mesh=mesh,
        in_specs=(
            P(("expert", "dp"), None),
            P(("expert", "dp"), None),
            P(("expert", "dp"), None),
            P(("expert", "dp"), None),
            P("expert", None, "dp", None),
            P("expert", None, "dp"),
            P("expert", None, None, None, None),
            P("expert", None, None, None, None),
            P("expert", None, None, None),
            P("expert", None, None, None),
        ),
        out_specs=(
            P(("expert", "dp"), None),
            P("expert", None, None, "dp", None),
            P("expert", None, None, "dp"),
        ),
        check_vma=False,
    )
```

```python
import functools

import jax
import jax.numpy as jnp
from jax import lax
from jax.experimental import pallas as pl
from jax.experimental.pallas import tpu as pltpu
from jax.sharding import PartitionSpec as P

GROUP = 128
PACK = 3
CHUNK = 16
TILE = 256
LIMIT = 24 * 1024 * 1024
SMALL = 8 * 1024 * 1024
F32 = jnp.float32
BF16 = jnp.bfloat16


def dot_nn(a, b):
    return lax.dot_general(a, b, (((1,), (0,)), ((), ())), preferred_element_type=F32)


def dot_nt(a, b):
    return lax.dot_general(a, b, (((1,), (1,)), ((), ())), preferred_element_type=F32)


def dot_tn(a, b):
    return lax.dot_general(a, b, (((0,), (0,)), ((), ())), preferred_element_type=F32)


def sigmoid(v):
    return 1.0 / (1.0 + jnp.exp(-v))


def plane_order(size, back=False):
    third = size // PACK
    row = lax.broadcasted_iota(jnp.int32, (size, size), 1 if back else 0)
    col = lax.broadcasted_iota(jnp.int32, (size, size), 0 if back else 1)
    plane = jnp.zeros_like(col)
    for j in range(1, PACK):
        plane = plane + (col >= j * third).astype(jnp.int32)
    return (row == PACK * (col - plane * third) + plane).astype(F32).astype(BF16)


def three_parts(a):
    high = a.astype(BF16)
    rest = a - high.astype(F32)
    middle = rest.astype(BF16)
    low = (rest - middle.astype(F32)).astype(BF16)
    return high, middle, low


def placed(a, order):
    parts = [dot_nn(part, order) for part in three_parts(a)]
    return parts[0] + parts[1] + parts[2]


ANYWHERE = pl.BlockSpec(memory_space=pl.ANY)
INSIDE = pl.BlockSpec(memory_space=pltpu.VMEM)


class Calls:
    def __init__(self, keep):
        self.keep = keep

    def pin(self, array):
        return pltpu.with_memory_space_constraint(array, pltpu.VMEM) if self.keep else array

    def out(self, shape, dtype):
        return pltpu.VMEM(shape, dtype) if self.keep else jax.ShapeDtypeStruct(shape, dtype)

    def run(self, kernel, name, inputs, outputs, after=(), alias=None, limit=LIMIT, raw=(), free=(), flops=0):
        count, given = len(inputs), len(raw)

        def wrapped(*refs):
            outs = refs[given + count + len(after) : given + count + len(after) + len(outputs)]
            scratch = refs[len(refs) - given - 1 : len(refs) - 1] if raw else ()
            copies = [
                pltpu.make_async_copy(refs[i], scratch[i], refs[-1].at[i]) for i in range(given)
            ]
            for copy in copies:
                copy.start()
            for copy in copies:
                copy.wait()
            kernel(*scratch, *refs[given : given + count], *outs)

        scratch = [pltpu.VMEM(a.shape, a.dtype) for a in raw]
        return pl.pallas_call(
            wrapped,
            in_specs=[ANYWHERE] * given + [INSIDE] * count + [ANYWHERE] * len(after),
            out_specs=[INSIDE] * len(outputs),
            out_shape=[
                jax.ShapeDtypeStruct(shape, dtype) if i in free else self.out(shape, dtype)
                for i, (shape, dtype) in enumerate(outputs)
            ],
            scratch_shapes=scratch + ([pltpu.SemaphoreType.DMA((given,))] if raw else []),
            input_output_aliases=alias or {},
            compiler_params=pltpu.CompilerParams(vmem_limit_bytes=limit),
            cost_estimate=pl.CostEstimate(flops=int(flops), bytes_accessed=0, transcendentals=0),
            name=name,
        )(*[pltpu.with_memory_space_constraint(a, pltpu.HBM) for a in raw], *[self.pin(a) for a in inputs], *after)


def pack_kernel(experts, token_ref, grad_ref, ids_ref, weights_ref, out_ref):
    rows, width = grad_ref.shape
    extra = out_ref.shape[1] - 2 * width
    out_ref[:, :width] = token_ref[...]
    out_ref[:, width : 2 * width] = grad_ref[...]
    line = lax.broadcasted_iota(jnp.int32, (extra, rows), 0)
    part = sum((line >= i * experts).astype(jnp.int32) for i in range(1, 4))
    expert = jnp.where(part < 3, line - part * experts, -1)
    table = jnp.zeros((extra, rows), F32)
    for k in range(ids_ref.shape[0]):
        table = table + jnp.where(ids_ref[k : k + 1, :] == expert, weights_ref[k : k + 1, :], 0.0)
    high, middle, low = three_parts(table)
    split = jnp.where(
        part == 0,
        high.astype(F32),
        jnp.where(part == 1, middle.astype(F32), low.astype(F32)),
    ).astype(BF16)
    same = lax.broadcasted_iota(jnp.int32, (extra, extra), 0) == lax.broadcasted_iota(jnp.int32, (extra, extra), 1)
    out_ref[:, 2 * width :] = dot_tn(split, same.astype(F32).astype(BF16)).astype(BF16)


def weight_kernel(codes_in, codes_out, clip_in, range_in, clip_out, range_out, w_ref):
    dp = lax.axis_index("dp")
    depth, third = codes_in.shape[1:]
    hidden = clip_in.shape[3]
    groups = depth // GROUP
    own = pl.ds(pl.multiple_of(dp * groups, groups), groups)
    order = plane_order(hidden)
    for p in range(2):
        upper = sigmoid(clip_in[p, 0, own, :]) * range_in[p, 0, own, :]
        lower = sigmoid(clip_in[p, 1, own, :]) * range_in[p, 1, own, :]
        ends = placed(jnp.concatenate([(upper + lower) / 15.0, lower], axis=0), order)
        for g in range(groups):
            packed = codes_in[p, g * GROUP : (g + 1) * GROUP, :]
            for j in range(PACK):
                code = jnp.bitwise_and(jnp.right_shift(packed, 4 * j), 15).astype(F32)
                cols = slice(j * third, (j + 1) * third)
                w_ref[p, g * GROUP : (g + 1) * GROUP, cols] = (
                    ends[g : g + 1, cols] * code - ends[groups + g : groups + g + 1, cols]
                ).astype(BF16)
    own = pl.ds(pl.multiple_of(dp * depth, depth), depth)
    step, lower = [], []
    for g in range(clip_out.shape[0]):
        upper_end = sigmoid(clip_out[g, 0:1, own]) * range_out[g, 0:1, own]
        lower_end = sigmoid(clip_out[g, 1:2, own]) * range_out[g, 1:2, own]
        step.append((upper_end + lower_end) / 15.0)
        lower.append(lower_end)
    row = lax.broadcasted_iota(jnp.int32, (CHUNK, 1), 0)
    for start in range(0, third, CHUNK):
        packed = codes_out[start : start + CHUNK, :]
        for j in range(PACK):
            first = (PACK * start + j) // GROUP
            last = (PACK * (start + CHUNK - 1) + j) // GROUP
            step_rows, lower_rows = step[first], lower[first]
            for g in range(first + 1, last + 1):
                late = PACK * (row + start) + j >= g * GROUP
                step_rows = jnp.where(late, step[g], step_rows)
                lower_rows = jnp.where(late, lower[g], lower_rows)
            code = jnp.bitwise_and(jnp.right_shift(packed, 4 * j), 15).astype(F32)
            down = (step_rows * code - lower_rows).astype(BF16)
            for q in range(depth // third):
                w_ref[2, q * third + start : q * third + start + CHUNK, j * third : (j + 1) * third] = down[
                    :, q * third : (q + 1) * third
                ]


def set_kernel(experts, first, keep, count, *refs):
    blocks, sides = refs[:count], refs[count : count + 2]
    earlier = refs[count + 2 : count + 6]
    refs = refs[count + 2 :] if first == 0 else refs[count + 6 :]
    partials = refs[0:4]
    x_ref, s_ref, h_ref, g_ref = refs[4:8]
    rows, width = partials[0].shape
    half = width // 2
    hidden = h_ref.shape[1]
    third = hidden // PACK
    dp, mine = lax.axis_index("dp"), lax.axis_index("expert")
    spans = (
        pl.ds(pl.multiple_of(dp * half, half), half),
        pl.ds(pl.multiple_of((1 - dp) * half, half), half),
    )
    here = slice(first, first + 4 * rows)
    if first and not keep:
        for old, new in zip(earlier, refs[4:8]):
            new[..., :first, :] = old[..., :first, :]
    start = first
    for block in blocks:
        span = slice(start, start + block.shape[0])
        start = span.stop
        x_ref[span, :] = block[:, :width]
        beside = block[:, 2 * width :].astype(F32)
        lane = lax.broadcasted_iota(jnp.int32, beside.shape, 1)
        keep = (lane == mine) | (lane == mine + experts) | (lane == mine + 2 * experts)
        scale = jnp.sum(jnp.where(keep, beside, 0.0), axis=1, keepdims=True)
        s_ref[span, :] = (scale * block[:, width : 2 * width].astype(F32)).astype(BF16)
    for j in range(PACK):
        cols = slice(j * third, (j + 1) * third)
        gate_pre = dot_nn(x_ref[here, spans[0]], sides[0][0, :, cols]) + dot_nn(
            x_ref[here, spans[1]], sides[1][0, :, cols]
        )
        up_pre = dot_nn(x_ref[here, spans[0]], sides[0][1, :, cols]) + dot_nn(
            x_ref[here, spans[1]], sides[1][1, :, cols]
        )
        grad_hidden = 0.0
        for side in range(2):
            for q in range(half // third):
                tile = pl.ds(pl.multiple_of((dp if side == 0 else 1 - dp) * half + q * third, third), third)
                grad_hidden = grad_hidden + dot_nt(
                    s_ref[here, tile], sides[side][2, q * third : (q + 1) * third, cols]
                )
        sig = sigmoid(gate_pre)
        act = gate_pre * sig
        h_ref[here, cols] = (act * up_pre).astype(BF16)
        g_ref[0, here, cols] = (grad_hidden * up_pre * sig * (1.0 + gate_pre * (1.0 - sig))).astype(BF16)
        g_ref[1, here, cols] = (grad_hidden * act).astype(BF16)
    for side in range(2):
        base = jnp.where(side == 0, dp, 1 - dp) * half

        @pl.loop(0, half // TILE)
        def _(n):
            depth = pl.ds(pl.multiple_of(n * TILE, TILE), TILE)
            part = dot_nt(g_ref[0, here, :], sides[side][0, depth, :]) + dot_nt(
                g_ref[1, here, :], sides[side][1, depth, :]
            )
            cols = pl.ds(pl.multiple_of(base + n * TILE, TILE), TILE)
            for i in range(4):
                partials[i][:, cols] = part[i * rows : (i + 1) * rows, :].astype(BF16)


def run_set(calls, blocks, weights, experts, pair=None, after=()):
    rows, width = blocks[0].shape[0], 2 * weights[0].shape[1]
    hidden = weights[0].shape[2]
    both = 8 * rows
    stored = [((both, width), BF16), ((both, width), BF16), ((both, hidden), BF16), ((2, both, hidden), BF16)]
    out = calls.run(
        functools.partial(set_kernel, experts, 0 if pair is None else 4 * rows, calls.keep, len(blocks)),
        "expert_set",
        [*blocks, *weights, *(pair or ())],
        [((rows, width), BF16)] * 4 + stored,
        after=after,
        flops=40 * rows * width * hidden,
        alias=None if pair is None else {len(blocks) + 2 + i: 4 + i for i in range(4)},
    )
    return list(out[:4]), list(out[4:])


def group_marks(size, count, span, planes):
    row = lax.broadcasted_iota(jnp.int32, (size, count), 0)
    group = lax.broadcasted_iota(jnp.int32, (size, count), 1)
    if planes > 1:
        third = size // planes
        plane = jnp.zeros_like(row)
        for j in range(1, planes):
            plane = plane + (row >= j * third).astype(jnp.int32)
        row = planes * (row - plane * third) + plane
    return ((row >= group * span) & (row < (group + 1) * span)).astype(F32).astype(BF16)


def two_parts(a):
    high = a.astype(BF16)
    return high, (a - high.astype(F32)).astype(BF16)


def sums_kernel(other, more, x_ref, s_ref, h_ref, g_ref, weights, *refs):
    old_in, old_out = refs[:2] if more else (None, None)
    sums_in, sums_out = refs[-2:]
    width = x_ref.shape[1]
    half = width // 2
    hidden = h_ref.shape[1]
    third = hidden // PACK
    share = sums_in.shape[2]
    groups_out = sums_out.shape[1]
    dp = lax.axis_index("dp")
    base = (1 - dp if other else dp) * half
    span = pl.ds(pl.multiple_of(base, half), half)

    def since(old, found, *where):
        return old[where] + found if more else found

    row_sums = two_parts(dot_nn(x_ref[:, span], group_marks(half, share, GROUP, 1)))
    for p in range(2):
        found = dot_tn(row_sums[0], g_ref[p]) + dot_tn(row_sums[1], g_ref[p])
        sums_in[p, 1] = since(old_in, found, p, 1)
    hidden_sums = two_parts(dot_nn(h_ref[...], group_marks(hidden, groups_out, GROUP, PACK)))
    found = dot_tn(hidden_sums[0], s_ref[:, span]) + dot_tn(hidden_sums[1], s_ref[:, span])
    sums_out[1] = since(old_out, found, 1)

    @pl.loop(0, half // third)
    def _(t):
        rows = pl.ds(pl.multiple_of(t * third, third), third)
        span = pl.ds(pl.multiple_of(base + t * third, third), third)
        x_cols = x_ref[:, span]
        for p in range(2):
            weighted = dot_tn(x_cols, g_ref[p]) * weights[p, rows, :].astype(F32)
            for g in range(third // GROUP):
                spot = pl.ds(t * (third // GROUP) + g, 1)
                found = jnp.sum(weighted[g * GROUP : (g + 1) * GROUP], axis=0, keepdims=True)
                sums_in[p, 0, spot, :] = since(old_in, found, p, 0, spot, slice(None))
        down = jnp.concatenate([weights[2, rows, j * third : (j + 1) * third] for j in range(PACK)], axis=0)
        weighted = dot_tn(h_ref[...], s_ref[:, span]) * down.astype(F32)
        for g in range(groups_out):
            found = None
            for j in range(PACK):
                low = -((j - GROUP * g) // PACK)
                high = -((j - GROUP * (g + 1)) // PACK)
                inner, outer = -(-low // 8) * 8, high // 8 * 8
                part = jnp.sum(weighted[j * third + inner : j * third + outer], axis=0, keepdims=True)
                found = part if found is None else found + part
                for start in sorted(({low // 8 * 8} if low % 8 else set()) | ({outer} if high % 8 else set())):
                    block = weighted[j * third + start : j * third + start + 8]
                    row = lax.broadcasted_iota(jnp.int32, block.shape, 0) + start
                    inside = (row >= low) & (row < high)
                    found = found + jnp.sum(jnp.where(inside, block, 0.0), axis=0, keepdims=True)
            sums_out[0, g : g + 1, rows] = since(old_out, found, 0, slice(g, g + 1), rows)


def run_sums(calls, stored, weights, other, before, shapes, after=()):
    side = weights[1] if other else weights[0]
    return calls.run(
        functools.partial(sums_kernel, other, before is not None),
        "group_sums",
        [*stored, side, *(before or ())],
        [(shape, F32) for shape in shapes],
        after=after,
        flops=24 * stored[0].shape[0] * weights[0].size // 8,
    )


def clip_kernel(clip_in, range_in, clip_out, range_out, mine_in, got_in, mine_out, got_out, in_ref, out_ref):
    dp = lax.axis_index("dp")
    hidden = clip_in.shape[3]
    groups = in_ref.shape[2]
    share = out_ref.shape[2]
    back = plane_order(hidden, True)

    def finish(weighted, plain, clip, span):
        sig_upper, sig_lower = sigmoid(clip[0]), sigmoid(clip[1])
        upper, lower = sig_upper * span[0], sig_lower * span[1]
        upper_sum = (weighted + lower * plain) / (upper + lower)
        lower_sum = upper_sum - plain
        return (
            upper_sum * span[0] * sig_upper * (1.0 - sig_upper),
            lower_sum * span[1] * sig_lower * (1.0 - sig_lower),
        )

    own = pl.ds(pl.multiple_of(dp * groups, groups), groups)
    for p in range(2):
        sums = jnp.concatenate(
            [mine_in[p, 0] + got_in[p, 0], mine_in[p, 1] + got_in[p, 1]], axis=0
        )
        natural = placed(sums, back)
        in_ref[p, 0], in_ref[p, 1] = finish(
            natural[:groups],
            natural[groups:],
            [clip_in[p, i, own, :] for i in range(2)],
            [range_in[p, i, own, :] for i in range(2)],
        )
    own = pl.ds(pl.multiple_of(dp * share, share), share)
    for g in range(out_ref.shape[0]):
        out_ref[g, 0:1, :], out_ref[g, 1:2, :] = finish(
            mine_out[0, g : g + 1, :] + got_out[0, g : g + 1, :],
            mine_out[1, g : g + 1, :] + got_out[1, g : g + 1, :],
            [clip_out[g, i : i + 1, own] for i in range(2)],
            [range_out[g, i : i + 1, own] for i in range(2)],
        )


def add_kernel(*refs):
    total = refs[0][...].astype(F32)
    for ref in refs[1:-1]:
        total = total + ref[...].astype(F32)
    refs[-1][...] = total.astype(refs[-1].dtype)


def part_kernel(first, old, new):
    new[...] = old[first : first + new.shape[0], :]


def hold_kernel(old, new):
    new[...] = old[...]


def body(
    tokens,
    grad_out,
    expert_ids,
    router_weights,
    codes_in,
    codes_out,
    clip_in,
    range_in,
    clip_out,
    range_out,
):
    experts = lax.axis_size("expert")
    rows, width = tokens.shape
    hidden = clip_in.shape[4]
    depth = codes_in.shape[2]
    extra = -(-3 * experts // 128) * 128
    calls = Calls(experts * rows * (3 * width + extra) * 2 < 2**24)

    def swap(array, mask):
        return lax.ppermute(array, "expert", [(i, i ^ mask) for i in range(experts)])

    def swap_core(array):
        return lax.ppermute(array, "dp", [(0, 1), (1, 0)])

    def added(*parts, after=(), free=()):
        return calls.run(
            add_kernel, "add_rows", list(parts), [(parts[0].shape, BF16)], after=after, limit=SMALL, free=free
        )[0]

    def held(array, *after):
        return calls.run(hold_kernel, "hold", [array], [(array.shape, array.dtype)], after, limit=SMALL)[0]

    packed = calls.run(
        functools.partial(pack_kernel, experts),
        "pack_rows",
        [],
        [((rows, 2 * width + extra), BF16)],
        raw=(tokens, grad_out, expert_ids.T, router_weights.T),
        limit=SMALL,
    )[0]

    clips = (clip_in[0], range_in[0], clip_out[0].transpose(1, 0, 2), range_out[0].transpose(1, 0, 2))
    shapes = ((2, 2, depth // GROUP, hidden), (2, clip_out.shape[2], depth))
    sums = {True: None, False: None}

    def dequantized(*after):
        (own_weights,) = calls.run(
            weight_kernel,
            "make_weights",
            [],
            [((3, depth, hidden), BF16)],
            raw=(codes_in[0], codes_out[0], *clips),
            after=after,
        )
        return own_weights, swap_core(own_weights)

    cut = rows // 2

    def part(array, first, after):
        shape = (rows - cut if first else cut, array.shape[1])
        return calls.run(
            functools.partial(part_kernel, first), "part", [array], [(shape, array.dtype)], after, limit=SMALL
        )[0]

    def crossed(over_x, over_y, *after):
        return swap(part(over_x, 0, after), 2), swap(part(over_y, cut, after), 1)

    def quad(head, weights, after):
        near = swap(head, 4)
        x0, y0 = swap(head, 1), swap(head, 2)
        far = swap(near, 12)
        if weights is None:
            weights = dequantized(head)
        d0 = crossed(x0, y0)
        ready = held(near, x0, y0, weights[1])
        x1, y1 = swap(ready, 1), swap(ready, 2)
        d1 = tuple(swap(half, 4) for half in d0)
        p0, stored = run_set(calls, (head, x0, y0, *d0), weights, experts, after=after)
        ready = held(far, x1, y1, *d1, p0[0])
        x2, y2, last = swap(ready, 1), swap(ready, 2), swap(ready, 4)
        p1, stored = run_set(calls, (near, x1, y1, *d1), weights, experts, stored)
        ready = held(last, x2, y2)
        x3, y3 = swap(ready, 1), swap(ready, 2)
        other = run_sums(calls, stored, weights, True, sums[True], shapes)
        d2 = crossed(x2, y2, other[0])
        d3 = tuple(swap(half, 4) for half in d2)
        p2, later = run_set(calls, (far, x2, y2, *d2), weights, experts)
        p3, later = run_set(calls, (last, x3, y3, *d3), weights, experts, later)
        x_sum0 = added(p0[1], swap(held(p0[3], x3, y3), 2))
        y_sum1 = added(p1[2], swap(held(p1[3], x3, y3), 1))
        x_sum2 = added(p2[1], swap(p2[3], 2), after=(p3[0],))
        sums[True] = run_sums(calls, later, weights, True, other, shapes, (x_sum2,))
        total2 = added(p2[0], swap(x_sum2, 1), swap(p2[2], 2), after=(sums[True][0],))
        far_sum = swap(total2, 8)
        y_sum3 = added(p3[2], swap(p3[3], 1), after=(sums[True][0],))
        mine = run_sums(calls, stored, weights, False, sums[False], shapes, (y_sum3, total2))
        total3 = added(p3[0], swap(p3[1], 1), swap(y_sum3, 2), after=(mine[0], far_sum))
        late0, late1 = held(p0[2], total2), held(p1[1], total2)
        total1 = added(p1[0], swap(late1, 1), swap(held(y_sum1, total2), 2))
        sums[False] = run_sums(calls, later, weights, False, mine, shapes, (total3,))
        parts = (
            p0[0],
            swap(held(x_sum0, total2), 1),
            swap(late0, 2),
            swap(total1, 4),
            far_sum,
            swap(total3, 12),
        )
        return parts, weights, total3

    final, after, weights = [], (), None
    for base in range(0, experts, 16):
        parts, weights, last_sum = quad(swap(packed, base) if base else packed, weights, after)
        final += [swap(added(*parts), base)] if base else parts
        after = (sums[False][0],)
    grad_tokens = added(*final, free=(0,))

    mine_in, mine_out = sums[False]
    got_in, got_out = (swap_core(held(a, last_sum)) for a in sums[True])
    grad_in, grad_clip_out = calls.run(
        clip_kernel,
        "clip_gradients",
        [mine_in, got_in, mine_out, got_out],
        [((2, 2, depth // GROUP, hidden), F32), ((clip_out.shape[2], 2, depth), F32)],
        raw=clips,
        limit=SMALL,
        free=(0, 1),
    )
    return grad_tokens, grad_in[None], grad_clip_out.transpose(1, 0, 2)[None]


def solution(mesh):
    return jax.shard_map(
        body,
        mesh=mesh,
        in_specs=(
            P(("expert", "dp"), None),
            P(("expert", "dp"), None),
            P(("expert", "dp"), None),
            P(("expert", "dp"), None),
            P("expert", None, "dp", None),
            P("expert", None, "dp"),
            P("expert", None, None, None, None),
            P("expert", None, None, None, None),
            P("expert", None, None, None),
            P("expert", None, None, None),
        ),
        out_specs=(
            P(("expert", "dp"), None),
            P("expert", None, None, "dp", None),
            P("expert", None, None, "dp"),
        ),
        check_vma=False,
    )
```

```python
import functools

import jax
import jax.numpy as jnp
from jax import lax
from jax.experimental import pallas as pl
from jax.experimental.pallas import tpu as pltpu
from jax.sharding import PartitionSpec as P

GROUP = 128
PACK = 3
CHUNK = 16
TILE = 256
LIMIT = 24 * 1024 * 1024
SMALL = 8 * 1024 * 1024
F32 = jnp.float32
BF16 = jnp.bfloat16


def dot_nn(a, b):
    return lax.dot_general(a, b, (((1,), (0,)), ((), ())), preferred_element_type=F32)


def dot_nt(a, b):
    return lax.dot_general(a, b, (((1,), (1,)), ((), ())), preferred_element_type=F32)


def dot_tn(a, b):
    return lax.dot_general(a, b, (((0,), (0,)), ((), ())), preferred_element_type=F32)


def sigmoid(v):
    return 1.0 / (1.0 + jnp.exp(-v))


def plane_order(size, back=False):
    third = size // PACK
    row = lax.broadcasted_iota(jnp.int32, (size, size), 1 if back else 0)
    col = lax.broadcasted_iota(jnp.int32, (size, size), 0 if back else 1)
    plane = jnp.zeros_like(col)
    for j in range(1, PACK):
        plane = plane + (col >= j * third).astype(jnp.int32)
    return (row == PACK * (col - plane * third) + plane).astype(F32).astype(BF16)


def three_parts(a):
    high = a.astype(BF16)
    rest = a - high.astype(F32)
    middle = rest.astype(BF16)
    low = (rest - middle.astype(F32)).astype(BF16)
    return high, middle, low


def placed(a, order):
    parts = [dot_nn(part, order) for part in three_parts(a)]
    return parts[0] + parts[1] + parts[2]


ANYWHERE = pl.BlockSpec(memory_space=pl.ANY)
INSIDE = pl.BlockSpec(memory_space=pltpu.VMEM)


class Calls:
    def __init__(self, keep):
        self.keep = keep

    def pin(self, array):
        return pltpu.with_memory_space_constraint(array, pltpu.VMEM) if self.keep else array

    def out(self, shape, dtype):
        return pltpu.VMEM(shape, dtype) if self.keep else jax.ShapeDtypeStruct(shape, dtype)

    def run(self, kernel, name, inputs, outputs, after=(), alias=None, limit=LIMIT, raw=(), free=(), flops=0):
        count, given = len(inputs), len(raw)

        def wrapped(*refs):
            outs = refs[given + count + len(after) : given + count + len(after) + len(outputs)]
            scratch = refs[len(refs) - given - 1 : len(refs) - 1] if raw else ()
            copies = [
                pltpu.make_async_copy(refs[i], scratch[i], refs[-1].at[i]) for i in range(given)
            ]
            for copy in copies:
                copy.start()
            for copy in copies:
                copy.wait()
            kernel(*scratch, *refs[given : given + count], *outs)

        scratch = [pltpu.VMEM(a.shape, a.dtype) for a in raw]
        return pl.pallas_call(
            wrapped,
            in_specs=[ANYWHERE] * given + [INSIDE] * count + [ANYWHERE] * len(after),
            out_specs=[INSIDE] * len(outputs),
            out_shape=[
                jax.ShapeDtypeStruct(shape, dtype) if i in free else self.out(shape, dtype)
                for i, (shape, dtype) in enumerate(outputs)
            ],
            scratch_shapes=scratch + ([pltpu.SemaphoreType.DMA((given,))] if raw else []),
            input_output_aliases=alias or {},
            compiler_params=pltpu.CompilerParams(vmem_limit_bytes=limit),
            cost_estimate=pl.CostEstimate(flops=int(flops), bytes_accessed=0, transcendentals=0),
            name=name,
        )(*[pltpu.with_memory_space_constraint(a, pltpu.HBM) for a in raw], *[self.pin(a) for a in inputs], *after)


def pack_kernel(experts, token_ref, grad_ref, ids_ref, weights_ref, out_ref):
    rows, width = grad_ref.shape
    extra = out_ref.shape[1] - 2 * width
    out_ref[:, :width] = token_ref[...]
    out_ref[:, width : 2 * width] = grad_ref[...]
    line = lax.broadcasted_iota(jnp.int32, (extra, rows), 0)
    part = sum((line >= i * experts).astype(jnp.int32) for i in range(1, 4))
    expert = jnp.where(part < 3, line - part * experts, -1)
    table = jnp.zeros((extra, rows), F32)
    for k in range(ids_ref.shape[0]):
        table = table + jnp.where(ids_ref[k : k + 1, :] == expert, weights_ref[k : k + 1, :], 0.0)
    high, middle, low = three_parts(table)
    split = jnp.where(
        part == 0,
        high.astype(F32),
        jnp.where(part == 1, middle.astype(F32), low.astype(F32)),
    ).astype(BF16)
    same = lax.broadcasted_iota(jnp.int32, (extra, extra), 0) == lax.broadcasted_iota(jnp.int32, (extra, extra), 1)
    out_ref[:, 2 * width :] = dot_tn(split, same.astype(F32).astype(BF16)).astype(BF16)


def weight_kernel(codes_in, codes_out, clip_in, range_in, clip_out, range_out, w_ref):
    dp = lax.axis_index("dp")
    depth, third = codes_in.shape[1:]
    hidden = clip_in.shape[3]
    groups = depth // GROUP
    own = pl.ds(pl.multiple_of(dp * groups, groups), groups)
    order = plane_order(hidden)
    for p in range(2):
        upper = sigmoid(clip_in[p, 0, own, :]) * range_in[p, 0, own, :]
        lower = sigmoid(clip_in[p, 1, own, :]) * range_in[p, 1, own, :]
        ends = placed(jnp.concatenate([(upper + lower) / 15.0, lower], axis=0), order)
        for g in range(groups):
            packed = codes_in[p, g * GROUP : (g + 1) * GROUP, :]
            for j in range(PACK):
                code = jnp.bitwise_and(jnp.right_shift(packed, 4 * j), 15).astype(F32)
                cols = slice(j * third, (j + 1) * third)
                w_ref[p, g * GROUP : (g + 1) * GROUP, cols] = (
                    ends[g : g + 1, cols] * code - ends[groups + g : groups + g + 1, cols]
                ).astype(BF16)
    own = pl.ds(pl.multiple_of(dp * depth, depth), depth)
    step, lower = [], []
    for g in range(clip_out.shape[0]):
        upper_end = sigmoid(clip_out[g, 0:1, own]) * range_out[g, 0:1, own]
        lower_end = sigmoid(clip_out[g, 1:2, own]) * range_out[g, 1:2, own]
        step.append((upper_end + lower_end) / 15.0)
        lower.append(lower_end)
    row = lax.broadcasted_iota(jnp.int32, (CHUNK, 1), 0)
    for start in range(0, third, CHUNK):
        packed = codes_out[start : start + CHUNK, :]
        for j in range(PACK):
            first = (PACK * start + j) // GROUP
            last = (PACK * (start + CHUNK - 1) + j) // GROUP
            step_rows, lower_rows = step[first], lower[first]
            for g in range(first + 1, last + 1):
                late = PACK * (row + start) + j >= g * GROUP
                step_rows = jnp.where(late, step[g], step_rows)
                lower_rows = jnp.where(late, lower[g], lower_rows)
            code = jnp.bitwise_and(jnp.right_shift(packed, 4 * j), 15).astype(F32)
            down = (step_rows * code - lower_rows).astype(BF16)
            for q in range(depth // third):
                w_ref[2, q * third + start : q * third + start + CHUNK, j * third : (j + 1) * third] = down[
                    :, q * third : (q + 1) * third
                ]


def set_kernel(experts, first, keep, count, *refs):
    blocks, sides = refs[:count], refs[count : count + 2]
    earlier = refs[count + 2 : count + 6]
    refs = refs[count + 2 :] if first == 0 else refs[count + 6 :]
    partials = refs[0:4]
    x_ref, s_ref, h_ref, g_ref = refs[4:8]
    rows, width = partials[0].shape
    half = width // 2
    hidden = h_ref.shape[1]
    third = hidden // PACK
    dp, mine = lax.axis_index("dp"), lax.axis_index("expert")
    spans = (
        pl.ds(pl.multiple_of(dp * half, half), half),
        pl.ds(pl.multiple_of((1 - dp) * half, half), half),
    )
    here = slice(first, first + 4 * rows)
    if first and not keep:
        for old, new in zip(earlier, refs[4:8]):
            new[..., :first, :] = old[..., :first, :]
    start = first
    for block in blocks:
        span = slice(start, start + block.shape[0])
        start = span.stop
        x_ref[span, :] = block[:, :width]
        beside = block[:, 2 * width :].astype(F32)
        lane = lax.broadcasted_iota(jnp.int32, beside.shape, 1)
        keep = (lane == mine) | (lane == mine + experts) | (lane == mine + 2 * experts)
        scale = jnp.sum(jnp.where(keep, beside, 0.0), axis=1, keepdims=True)
        s_ref[span, :] = (scale * block[:, width : 2 * width].astype(F32)).astype(BF16)
    for j in range(PACK):
        cols = slice(j * third, (j + 1) * third)
        gate_pre = dot_nn(x_ref[here, spans[0]], sides[0][0, :, cols]) + dot_nn(
            x_ref[here, spans[1]], sides[1][0, :, cols]
        )
        up_pre = dot_nn(x_ref[here, spans[0]], sides[0][1, :, cols]) + dot_nn(
            x_ref[here, spans[1]], sides[1][1, :, cols]
        )
        grad_hidden = 0.0
        for side in range(2):
            for q in range(half // third):
                tile = pl.ds(pl.multiple_of((dp if side == 0 else 1 - dp) * half + q * third, third), third)
                grad_hidden = grad_hidden + dot_nt(
                    s_ref[here, tile], sides[side][2, q * third : (q + 1) * third, cols]
                )
        sig = sigmoid(gate_pre)
        act = gate_pre * sig
        h_ref[here, cols] = (act * up_pre).astype(BF16)
        g_ref[0, here, cols] = (grad_hidden * up_pre * sig * (1.0 + gate_pre * (1.0 - sig))).astype(BF16)
        g_ref[1, here, cols] = (grad_hidden * act).astype(BF16)
    for side in range(2):
        base = jnp.where(side == 0, dp, 1 - dp) * half

        @pl.loop(0, half // TILE)
        def _(n):
            depth = pl.ds(pl.multiple_of(n * TILE, TILE), TILE)
            part = dot_nt(g_ref[0, here, :], sides[side][0, depth, :]) + dot_nt(
                g_ref[1, here, :], sides[side][1, depth, :]
            )
            cols = pl.ds(pl.multiple_of(base + n * TILE, TILE), TILE)
            for i in range(4):
                partials[i][:, cols] = part[i * rows : (i + 1) * rows, :].astype(BF16)


def run_set(calls, blocks, weights, experts, pair=None, after=()):
    rows, width = blocks[0].shape[0], 2 * weights[0].shape[1]
    hidden = weights[0].shape[2]
    both = 8 * rows
    stored = [((both, width), BF16), ((both, width), BF16), ((both, hidden), BF16), ((2, both, hidden), BF16)]
    out = calls.run(
        functools.partial(set_kernel, experts, 0 if pair is None else 4 * rows, calls.keep, len(blocks)),
        "expert_set",
        [*blocks, *weights, *(pair or ())],
        [((rows, width), BF16)] * 4 + stored,
        after=after,
        flops=40 * rows * width * hidden,
        alias=None if pair is None else {len(blocks) + 2 + i: 4 + i for i in range(4)},
    )
    return list(out[:4]), list(out[4:])


def group_marks(size, count, span, planes):
    row = lax.broadcasted_iota(jnp.int32, (size, count), 0)
    group = lax.broadcasted_iota(jnp.int32, (size, count), 1)
    if planes > 1:
        third = size // planes
        plane = jnp.zeros_like(row)
        for j in range(1, planes):
            plane = plane + (row >= j * third).astype(jnp.int32)
        row = planes * (row - plane * third) + plane
    return ((row >= group * span) & (row < (group + 1) * span)).astype(F32).astype(BF16)


def two_parts(a):
    high = a.astype(BF16)
    return high, (a - high.astype(F32)).astype(BF16)


def sums_kernel(other, more, x_ref, s_ref, h_ref, g_ref, weights, *refs):
    old_in, old_out = refs[:2] if more else (None, None)
    sums_in, sums_out = refs[-2:]
    width = x_ref.shape[1]
    half = width // 2
    hidden = h_ref.shape[1]
    third = hidden // PACK
    share = sums_in.shape[2]
    groups_out = sums_out.shape[1]
    dp = lax.axis_index("dp")
    base = (1 - dp if other else dp) * half
    span = pl.ds(pl.multiple_of(base, half), half)

    def since(old, found, *where):
        return old[where] + found if more else found

    row_sums = two_parts(dot_nn(x_ref[:, span], group_marks(half, share, GROUP, 1)))
    for p in range(2):
        found = dot_tn(row_sums[0], g_ref[p]) + dot_tn(row_sums[1], g_ref[p])
        sums_in[p, 1] = since(old_in, found, p, 1)
    hidden_sums = two_parts(dot_nn(h_ref[...], group_marks(hidden, groups_out, GROUP, PACK)))
    found = dot_tn(hidden_sums[0], s_ref[:, span]) + dot_tn(hidden_sums[1], s_ref[:, span])
    sums_out[1] = since(old_out, found, 1)

    @pl.loop(0, half // third)
    def _(t):
        rows = pl.ds(pl.multiple_of(t * third, third), third)
        span = pl.ds(pl.multiple_of(base + t * third, third), third)
        x_cols = x_ref[:, span]
        for p in range(2):
            weighted = dot_tn(x_cols, g_ref[p]) * weights[p, rows, :].astype(F32)
            for g in range(third // GROUP):
                spot = pl.ds(t * (third // GROUP) + g, 1)
                found = jnp.sum(weighted[g * GROUP : (g + 1) * GROUP], axis=0, keepdims=True)
                sums_in[p, 0, spot, :] = since(old_in, found, p, 0, spot, slice(None))
        down = jnp.concatenate([weights[2, rows, j * third : (j + 1) * third] for j in range(PACK)], axis=0)
        weighted = dot_tn(h_ref[...], s_ref[:, span]) * down.astype(F32)
        for g in range(groups_out):
            found = None
            for j in range(PACK):
                low = -((j - GROUP * g) // PACK)
                high = -((j - GROUP * (g + 1)) // PACK)
                inner, outer = -(-low // 8) * 8, high // 8 * 8
                part = jnp.sum(weighted[j * third + inner : j * third + outer], axis=0, keepdims=True)
                found = part if found is None else found + part
                for start in sorted(({low // 8 * 8} if low % 8 else set()) | ({outer} if high % 8 else set())):
                    block = weighted[j * third + start : j * third + start + 8]
                    row = lax.broadcasted_iota(jnp.int32, block.shape, 0) + start
                    inside = (row >= low) & (row < high)
                    found = found + jnp.sum(jnp.where(inside, block, 0.0), axis=0, keepdims=True)
            sums_out[0, g : g + 1, rows] = since(old_out, found, 0, slice(g, g + 1), rows)


def run_sums(calls, stored, weights, other, before, shapes, after=()):
    side = weights[1] if other else weights[0]
    return calls.run(
        functools.partial(sums_kernel, other, before is not None),
        "group_sums",
        [*stored, side, *(before or ())],
        [(shape, F32) for shape in shapes],
        after=after,
        flops=24 * stored[0].shape[0] * weights[0].size // 8,
    )


def clip_kernel(clip_in, range_in, clip_out, range_out, mine_in, got_in, mine_out, got_out, in_ref, out_ref):
    dp = lax.axis_index("dp")
    hidden = clip_in.shape[3]
    groups = in_ref.shape[2]
    share = out_ref.shape[2]
    back = plane_order(hidden, True)

    def finish(weighted, plain, clip, span):
        sig_upper, sig_lower = sigmoid(clip[0]), sigmoid(clip[1])
        upper, lower = sig_upper * span[0], sig_lower * span[1]
        upper_sum = (weighted + lower * plain) / (upper + lower)
        lower_sum = upper_sum - plain
        return (
            upper_sum * span[0] * sig_upper * (1.0 - sig_upper),
            lower_sum * span[1] * sig_lower * (1.0 - sig_lower),
        )

    own = pl.ds(pl.multiple_of(dp * groups, groups), groups)
    for p in range(2):
        sums = jnp.concatenate(
            [mine_in[p, 0] + got_in[p, 0], mine_in[p, 1] + got_in[p, 1]], axis=0
        )
        natural = placed(sums, back)
        in_ref[p, 0], in_ref[p, 1] = finish(
            natural[:groups],
            natural[groups:],
            [clip_in[p, i, own, :] for i in range(2)],
            [range_in[p, i, own, :] for i in range(2)],
        )
    own = pl.ds(pl.multiple_of(dp * share, share), share)
    for g in range(out_ref.shape[0]):
        out_ref[g, 0:1, :], out_ref[g, 1:2, :] = finish(
            mine_out[0, g : g + 1, :] + got_out[0, g : g + 1, :],
            mine_out[1, g : g + 1, :] + got_out[1, g : g + 1, :],
            [clip_out[g, i : i + 1, own] for i in range(2)],
            [range_out[g, i : i + 1, own] for i in range(2)],
        )


def add_kernel(*refs):
    total = refs[0][...].astype(F32)
    for ref in refs[1:-1]:
        total = total + ref[...].astype(F32)
    refs[-1][...] = total.astype(refs[-1].dtype)


def part_kernel(first, old, new):
    new[...] = old[first : first + new.shape[0], :]


def hold_kernel(old, new):
    new[...] = old[...]


def body(
    tokens,
    grad_out,
    expert_ids,
    router_weights,
    codes_in,
    codes_out,
    clip_in,
    range_in,
    clip_out,
    range_out,
):
    experts = lax.axis_size("expert")
    rows, width = tokens.shape
    hidden = clip_in.shape[4]
    depth = codes_in.shape[2]
    extra = -(-3 * experts // 128) * 128
    calls = Calls(experts * rows * (3 * width + extra) * 2 < 2**24)

    def swap(array, mask):
        return lax.ppermute(array, "expert", [(i, i ^ mask) for i in range(experts)])

    def swap_core(array):
        return lax.ppermute(array, "dp", [(0, 1), (1, 0)])

    def added(*parts, after=(), free=()):
        return calls.run(
            add_kernel, "add_rows", list(parts), [(parts[0].shape, BF16)], after=after, limit=SMALL, free=free
        )[0]

    def held(array, *after):
        return calls.run(hold_kernel, "hold", [array], [(array.shape, array.dtype)], after, limit=SMALL)[0]

    packed = calls.run(
        functools.partial(pack_kernel, experts),
        "pack_rows",
        [],
        [((rows, 2 * width + extra), BF16)],
        raw=(tokens, grad_out, expert_ids.T, router_weights.T),
        limit=SMALL,
    )[0]

    clips = (clip_in[0], range_in[0], clip_out[0].transpose(1, 0, 2), range_out[0].transpose(1, 0, 2))
    shapes = ((2, 2, depth // GROUP, hidden), (2, clip_out.shape[2], depth))
    sums = {True: None, False: None}

    def dequantized(*after):
        (own_weights,) = calls.run(
            weight_kernel,
            "make_weights",
            [],
            [((3, depth, hidden), BF16)],
            raw=(codes_in[0], codes_out[0], *clips),
            after=after,
        )
        return own_weights, swap_core(own_weights)

    cut = rows // 2

    def part(array, first, after):
        shape = (rows - cut if first else cut, array.shape[1])
        return calls.run(
            functools.partial(part_kernel, first), "part", [array], [(shape, array.dtype)], after, limit=SMALL
        )[0]

    def crossed(over_x, over_y):
        return swap(part(over_x, 0, ()), 2), swap(part(over_y, cut, ()), 1)

    def quad(head, weights, after):
        near = swap(head, 4)
        x0, y0 = swap(head, 1), swap(head, 2)
        far = swap(near, 12)
        if weights is None:
            weights = dequantized(head)
        d0 = crossed(x0, y0)
        ready = held(near, x0, y0, weights[1])
        x1, y1 = swap(ready, 1), swap(ready, 2)
        d1 = tuple(swap(half, 4) for half in d0)
        p0, stored = run_set(calls, (head, x0, y0, *d0), weights, experts, after=after)
        ready = held(far, x1, y1, p0[0])
        x2, y2, last = swap(ready, 1), swap(ready, 2), swap(ready, 4)
        p1, stored = run_set(calls, (near, x1, y1, *d1), weights, experts, stored)
        halves = part(x2, 0, (p1[0],)), part(y2, cut, (p1[0],))
        d2 = swap(halves[0], 2), swap(halves[1], 1)
        ready = held(last, *halves)
        x3, y3 = swap(ready, 1), swap(ready, 2)
        other = run_sums(calls, stored, weights, True, sums[True], shapes, (ready,))
        d3 = tuple(swap(half, 4) for half in d2)
        p2, later = run_set(calls, (far, x2, y2, *d2), weights, experts, after=(other[0],))
        mine = run_sums(calls, stored, weights, False, sums[False], shapes, (p2[0],))
        p3, later = run_set(calls, (last, x3, y3, *d3), weights, experts, later, (mine[0],))
        x_sum0 = added(p0[1], swap(held(p0[3], x3, y3), 2))
        y_sum1 = added(p1[2], swap(held(p1[3], x3, y3), 1))
        x_sum2 = added(p2[1], swap(p2[3], 2), after=(p3[0],))
        sums[True] = run_sums(calls, later, weights, True, other, shapes, (x_sum2,))
        total2 = added(p2[0], swap(x_sum2, 1), swap(p2[2], 2), after=(sums[True][0],))
        far_sum = swap(total2, 8)
        y_sum3 = added(p3[2], swap(p3[3], 1), after=(sums[True][0],))
        sums[False] = run_sums(calls, later, weights, False, mine, shapes, (y_sum3, total2))
        total3 = added(p3[0], swap(p3[1], 1), swap(y_sum3, 2), after=(sums[False][0], far_sum))
        late0, late1 = held(p0[2], total2), held(p1[1], total2)
        total1 = added(p1[0], swap(late1, 1), swap(held(y_sum1, total2), 2))
        parts = (
            p0[0],
            swap(held(x_sum0, total2), 1),
            swap(late0, 2),
            swap(total1, 4),
            far_sum,
            swap(total3, 12),
        )
        return parts, weights, total3

    final, after, weights = [], (), None
    for base in range(0, experts, 16):
        parts, weights, last_sum = quad(swap(packed, base) if base else packed, weights, after)
        final += [swap(added(*parts), base)] if base else parts
        after = (sums[False][0],)
    grad_tokens = added(*final, free=(0,))

    mine_in, mine_out = sums[False]
    got_in, got_out = (swap_core(held(a, last_sum)) for a in sums[True])
    grad_in, grad_clip_out = calls.run(
        clip_kernel,
        "clip_gradients",
        [mine_in, got_in, mine_out, got_out],
        [((2, 2, depth // GROUP, hidden), F32), ((clip_out.shape[2], 2, depth), F32)],
        raw=clips,
        limit=SMALL,
        free=(0, 1),
    )
    return grad_tokens, grad_in[None], grad_clip_out.transpose(1, 0, 2)[None]


def solution(mesh):
    return jax.shard_map(
        body,
        mesh=mesh,
        in_specs=(
            P(("expert", "dp"), None),
            P(("expert", "dp"), None),
            P(("expert", "dp"), None),
            P(("expert", "dp"), None),
            P("expert", None, "dp", None),
            P("expert", None, "dp"),
            P("expert", None, None, None, None),
            P("expert", None, None, None, None),
            P("expert", None, None, None),
            P("expert", None, None, None),
        ),
        out_specs=(
            P(("expert", "dp"), None),
            P("expert", None, None, "dp", None),
            P("expert", None, None, "dp"),
        ),
        check_vma=False,
    )
```

```python
import functools

import jax
import jax.numpy as jnp
from jax import lax
from jax.experimental import pallas as pl
from jax.experimental.pallas import tpu as pltpu
from jax.sharding import PartitionSpec as P

GROUP = 128
PACK = 3
CHUNK = 16
TILE = 256
LIMIT = 24 * 1024 * 1024
SMALL = 8 * 1024 * 1024
F32 = jnp.float32
BF16 = jnp.bfloat16


def dot_nn(a, b):
    return lax.dot_general(a, b, (((1,), (0,)), ((), ())), preferred_element_type=F32)


def dot_nt(a, b):
    return lax.dot_general(a, b, (((1,), (1,)), ((), ())), preferred_element_type=F32)


def dot_tn(a, b):
    return lax.dot_general(a, b, (((0,), (0,)), ((), ())), preferred_element_type=F32)


def sigmoid(v):
    return 1.0 / (1.0 + jnp.exp(-v))


def plane_order(size, back=False):
    third = size // PACK
    row = lax.broadcasted_iota(jnp.int32, (size, size), 1 if back else 0)
    col = lax.broadcasted_iota(jnp.int32, (size, size), 0 if back else 1)
    plane = jnp.zeros_like(col)
    for j in range(1, PACK):
        plane = plane + (col >= j * third).astype(jnp.int32)
    return (row == PACK * (col - plane * third) + plane).astype(F32).astype(BF16)


def three_parts(a):
    high = a.astype(BF16)
    rest = a - high.astype(F32)
    middle = rest.astype(BF16)
    low = (rest - middle.astype(F32)).astype(BF16)
    return high, middle, low


def placed(a, order):
    parts = [dot_nn(part, order) for part in three_parts(a)]
    return parts[0] + parts[1] + parts[2]


ANYWHERE = pl.BlockSpec(memory_space=pl.ANY)
INSIDE = pl.BlockSpec(memory_space=pltpu.VMEM)


class Calls:
    def __init__(self, keep):
        self.keep = keep

    def pin(self, array):
        return pltpu.with_memory_space_constraint(array, pltpu.VMEM) if self.keep else array

    def out(self, shape, dtype):
        return pltpu.VMEM(shape, dtype) if self.keep else jax.ShapeDtypeStruct(shape, dtype)

    def run(self, kernel, name, inputs, outputs, after=(), alias=None, limit=LIMIT, raw=(), free=(), flops=0):
        count, given = len(inputs), len(raw)

        def wrapped(*refs):
            outs = refs[given + count + len(after) : given + count + len(after) + len(outputs)]
            scratch = refs[len(refs) - given - 1 : len(refs) - 1] if raw else ()
            copies = [
                pltpu.make_async_copy(refs[i], scratch[i], refs[-1].at[i]) for i in range(given)
            ]
            for copy in copies:
                copy.start()
            for copy in copies:
                copy.wait()
            kernel(*scratch, *refs[given : given + count], *outs)

        scratch = [pltpu.VMEM(a.shape, a.dtype) for a in raw]
        return pl.pallas_call(
            wrapped,
            in_specs=[ANYWHERE] * given + [INSIDE] * count + [ANYWHERE] * len(after),
            out_specs=[INSIDE] * len(outputs),
            out_shape=[
                jax.ShapeDtypeStruct(shape, dtype) if i in free else self.out(shape, dtype)
                for i, (shape, dtype) in enumerate(outputs)
            ],
            scratch_shapes=scratch + ([pltpu.SemaphoreType.DMA((given,))] if raw else []),
            input_output_aliases=alias or {},
            compiler_params=pltpu.CompilerParams(vmem_limit_bytes=limit),
            cost_estimate=pl.CostEstimate(flops=int(flops), bytes_accessed=0, transcendentals=0),
            name=name,
        )(*[pltpu.with_memory_space_constraint(a, pltpu.HBM) for a in raw], *[self.pin(a) for a in inputs], *after)


def pack_kernel(experts, token_ref, grad_ref, ids_ref, weights_ref, out_ref):
    rows, width = grad_ref.shape
    extra = out_ref.shape[1] - 2 * width
    out_ref[:, :width] = token_ref[...]
    out_ref[:, width : 2 * width] = grad_ref[...]
    line = lax.broadcasted_iota(jnp.int32, (extra, rows), 0)
    part = sum((line >= i * experts).astype(jnp.int32) for i in range(1, 4))
    expert = jnp.where(part < 3, line - part * experts, -1)
    table = jnp.zeros((extra, rows), F32)
    for k in range(ids_ref.shape[0]):
        table = table + jnp.where(ids_ref[k : k + 1, :] == expert, weights_ref[k : k + 1, :], 0.0)
    high, middle, low = three_parts(table)
    split = jnp.where(
        part == 0,
        high.astype(F32),
        jnp.where(part == 1, middle.astype(F32), low.astype(F32)),
    ).astype(BF16)
    same = lax.broadcasted_iota(jnp.int32, (extra, extra), 0) == lax.broadcasted_iota(jnp.int32, (extra, extra), 1)
    out_ref[:, 2 * width :] = dot_tn(split, same.astype(F32).astype(BF16)).astype(BF16)


def weight_kernel(codes_in, codes_out, clip_in, range_in, clip_out, range_out, w_ref):
    dp = lax.axis_index("dp")
    depth, third = codes_in.shape[1:]
    hidden = clip_in.shape[3]
    groups = depth // GROUP
    own = pl.ds(pl.multiple_of(dp * groups, groups), groups)
    order = plane_order(hidden)
    for p in range(2):
        upper = sigmoid(clip_in[p, 0, own, :]) * range_in[p, 0, own, :]
        lower = sigmoid(clip_in[p, 1, own, :]) * range_in[p, 1, own, :]
        ends = placed(jnp.concatenate([(upper + lower) / 15.0, lower], axis=0), order)
        for g in range(groups):
            packed = codes_in[p, g * GROUP : (g + 1) * GROUP, :]
            for j in range(PACK):
                code = jnp.bitwise_and(jnp.right_shift(packed, 4 * j), 15).astype(F32)
                cols = slice(j * third, (j + 1) * third)
                w_ref[p, g * GROUP : (g + 1) * GROUP, cols] = (
                    ends[g : g + 1, cols] * code - ends[groups + g : groups + g + 1, cols]
                ).astype(BF16)
    own = pl.ds(pl.multiple_of(dp * depth, depth), depth)
    step, lower = [], []
    for g in range(clip_out.shape[0]):
        upper_end = sigmoid(clip_out[g, 0:1, own]) * range_out[g, 0:1, own]
        lower_end = sigmoid(clip_out[g, 1:2, own]) * range_out[g, 1:2, own]
        step.append((upper_end + lower_end) / 15.0)
        lower.append(lower_end)
    row = lax.broadcasted_iota(jnp.int32, (CHUNK, 1), 0)
    for start in range(0, third, CHUNK):
        packed = codes_out[start : start + CHUNK, :]
        for j in range(PACK):
            first = (PACK * start + j) // GROUP
            last = (PACK * (start + CHUNK - 1) + j) // GROUP
            step_rows, lower_rows = step[first], lower[first]
            for g in range(first + 1, last + 1):
                late = PACK * (row + start) + j >= g * GROUP
                step_rows = jnp.where(late, step[g], step_rows)
                lower_rows = jnp.where(late, lower[g], lower_rows)
            code = jnp.bitwise_and(jnp.right_shift(packed, 4 * j), 15).astype(F32)
            down = (step_rows * code - lower_rows).astype(BF16)
            for q in range(depth // third):
                w_ref[2, q * third + start : q * third + start + CHUNK, j * third : (j + 1) * third] = down[
                    :, q * third : (q + 1) * third
                ]


def set_kernel(experts, first, keep, count, *refs):
    blocks, sides = refs[:count], refs[count : count + 2]
    earlier = refs[count + 2 : count + 6]
    refs = refs[count + 2 :] if first == 0 else refs[count + 6 :]
    partials = refs[0:4]
    x_ref, s_ref, h_ref, g_ref = refs[4:8]
    rows, width = partials[0].shape
    half = width // 2
    hidden = h_ref.shape[1]
    third = hidden // PACK
    dp, mine = lax.axis_index("dp"), lax.axis_index("expert")
    spans = (
        pl.ds(pl.multiple_of(dp * half, half), half),
        pl.ds(pl.multiple_of((1 - dp) * half, half), half),
    )
    here = slice(first, first + 4 * rows)
    if first and not keep:
        for old, new in zip(earlier, refs[4:8]):
            new[..., :first, :] = old[..., :first, :]
    start = first
    for block in blocks:
        span = slice(start, start + block.shape[0])
        start = span.stop
        x_ref[span, :] = block[:, :width]
        beside = block[:, 2 * width :].astype(F32)
        lane = lax.broadcasted_iota(jnp.int32, beside.shape, 1)
        keep = (lane == mine) | (lane == mine + experts) | (lane == mine + 2 * experts)
        scale = jnp.sum(jnp.where(keep, beside, 0.0), axis=1, keepdims=True)
        s_ref[span, :] = (scale * block[:, width : 2 * width].astype(F32)).astype(BF16)
    for j in range(PACK):
        cols = slice(j * third, (j + 1) * third)
        gate_pre = dot_nn(x_ref[here, spans[0]], sides[0][0, :, cols]) + dot_nn(
            x_ref[here, spans[1]], sides[1][0, :, cols]
        )
        up_pre = dot_nn(x_ref[here, spans[0]], sides[0][1, :, cols]) + dot_nn(
            x_ref[here, spans[1]], sides[1][1, :, cols]
        )
        grad_hidden = 0.0
        for side in range(2):
            for q in range(half // third):
                tile = pl.ds(pl.multiple_of((dp if side == 0 else 1 - dp) * half + q * third, third), third)
                grad_hidden = grad_hidden + dot_nt(
                    s_ref[here, tile], sides[side][2, q * third : (q + 1) * third, cols]
                )
        sig = sigmoid(gate_pre)
        act = gate_pre * sig
        h_ref[here, cols] = (act * up_pre).astype(BF16)
        g_ref[0, here, cols] = (grad_hidden * up_pre * sig * (1.0 + gate_pre * (1.0 - sig))).astype(BF16)
        g_ref[1, here, cols] = (grad_hidden * act).astype(BF16)
    for side in range(2):
        base = jnp.where(side == 0, dp, 1 - dp) * half

        @pl.loop(0, half // TILE)
        def _(n):
            depth = pl.ds(pl.multiple_of(n * TILE, TILE), TILE)
            part = dot_nt(g_ref[0, here, :], sides[side][0, depth, :]) + dot_nt(
                g_ref[1, here, :], sides[side][1, depth, :]
            )
            cols = pl.ds(pl.multiple_of(base + n * TILE, TILE), TILE)
            for i in range(4):
                partials[i][:, cols] = part[i * rows : (i + 1) * rows, :].astype(BF16)


def run_set(calls, blocks, weights, experts, pair=None, after=()):
    rows, width = blocks[0].shape[0], 2 * weights[0].shape[1]
    hidden = weights[0].shape[2]
    both = 8 * rows
    stored = [((both, width), BF16), ((both, width), BF16), ((both, hidden), BF16), ((2, both, hidden), BF16)]
    out = calls.run(
        functools.partial(set_kernel, experts, 0 if pair is None else 4 * rows, calls.keep, len(blocks)),
        "expert_set",
        [*blocks, *weights, *(pair or ())],
        [((rows, width), BF16)] * 4 + stored,
        after=after,
        flops=40 * rows * width * hidden,
        alias=None if pair is None else {len(blocks) + 2 + i: 4 + i for i in range(4)},
    )
    return list(out[:4]), list(out[4:])


def group_marks(size, count, span, planes):
    row = lax.broadcasted_iota(jnp.int32, (size, count), 0)
    group = lax.broadcasted_iota(jnp.int32, (size, count), 1)
    if planes > 1:
        third = size // planes
        plane = jnp.zeros_like(row)
        for j in range(1, planes):
            plane = plane + (row >= j * third).astype(jnp.int32)
        row = planes * (row - plane * third) + plane
    return ((row >= group * span) & (row < (group + 1) * span)).astype(F32).astype(BF16)


def two_parts(a):
    high = a.astype(BF16)
    return high, (a - high.astype(F32)).astype(BF16)


def sums_kernel(other, more, x_ref, s_ref, h_ref, g_ref, weights, *refs):
    old_in, old_out = refs[:2] if more else (None, None)
    sums_in, sums_out = refs[-2:]
    width = x_ref.shape[1]
    half = width // 2
    hidden = h_ref.shape[1]
    third = hidden // PACK
    share = sums_in.shape[2]
    groups_out = sums_out.shape[1]
    dp = lax.axis_index("dp")
    base = (1 - dp if other else dp) * half
    span = pl.ds(pl.multiple_of(base, half), half)

    def since(old, found, *where):
        return old[where] + found if more else found

    row_sums = two_parts(dot_nn(x_ref[:, span], group_marks(half, share, GROUP, 1)))
    for p in range(2):
        found = dot_tn(row_sums[0], g_ref[p]) + dot_tn(row_sums[1], g_ref[p])
        sums_in[p, 1] = since(old_in, found, p, 1)
    hidden_sums = two_parts(dot_nn(h_ref[...], group_marks(hidden, groups_out, GROUP, PACK)))
    found = dot_tn(hidden_sums[0], s_ref[:, span]) + dot_tn(hidden_sums[1], s_ref[:, span])
    sums_out[1] = since(old_out, found, 1)

    @pl.loop(0, half // third)
    def _(t):
        rows = pl.ds(pl.multiple_of(t * third, third), third)
        span = pl.ds(pl.multiple_of(base + t * third, third), third)
        x_cols = x_ref[:, span]
        for p in range(2):
            weighted = dot_tn(x_cols, g_ref[p]) * weights[p, rows, :].astype(F32)
            for g in range(third // GROUP):
                spot = pl.ds(t * (third // GROUP) + g, 1)
                found = jnp.sum(weighted[g * GROUP : (g + 1) * GROUP], axis=0, keepdims=True)
                sums_in[p, 0, spot, :] = since(old_in, found, p, 0, spot, slice(None))
        down = jnp.concatenate([weights[2, rows, j * third : (j + 1) * third] for j in range(PACK)], axis=0)
        weighted = dot_tn(h_ref[...], s_ref[:, span]) * down.astype(F32)
        for g in range(groups_out):
            found = None
            for j in range(PACK):
                low = -((j - GROUP * g) // PACK)
                high = -((j - GROUP * (g + 1)) // PACK)
                inner, outer = -(-low // 8) * 8, high // 8 * 8
                part = jnp.sum(weighted[j * third + inner : j * third + outer], axis=0, keepdims=True)
                found = part if found is None else found + part
                for start in sorted(({low // 8 * 8} if low % 8 else set()) | ({outer} if high % 8 else set())):
                    block = weighted[j * third + start : j * third + start + 8]
                    row = lax.broadcasted_iota(jnp.int32, block.shape, 0) + start
                    inside = (row >= low) & (row < high)
                    found = found + jnp.sum(jnp.where(inside, block, 0.0), axis=0, keepdims=True)
            sums_out[0, g : g + 1, rows] = since(old_out, found, 0, slice(g, g + 1), rows)


def run_sums(calls, stored, weights, other, before, shapes, after=()):
    side = weights[1] if other else weights[0]
    return calls.run(
        functools.partial(sums_kernel, other, before is not None),
        "group_sums",
        [*stored, side, *(before or ())],
        [(shape, F32) for shape in shapes],
        after=after,
        flops=24 * stored[0].shape[0] * weights[0].size // 8,
    )


def clip_kernel(clip_in, range_in, clip_out, range_out, mine_in, got_in, mine_out, got_out, in_ref, out_ref):
    dp = lax.axis_index("dp")
    hidden = clip_in.shape[3]
    groups = in_ref.shape[2]
    share = out_ref.shape[2]
    back = plane_order(hidden, True)

    def finish(weighted, plain, clip, span):
        sig_upper, sig_lower = sigmoid(clip[0]), sigmoid(clip[1])
        upper, lower = sig_upper * span[0], sig_lower * span[1]
        upper_sum = (weighted + lower * plain) / (upper + lower)
        lower_sum = upper_sum - plain
        return (
            upper_sum * span[0] * sig_upper * (1.0 - sig_upper),
            lower_sum * span[1] * sig_lower * (1.0 - sig_lower),
        )

    own = pl.ds(pl.multiple_of(dp * groups, groups), groups)
    for p in range(2):
        sums = jnp.concatenate(
            [mine_in[p, 0] + got_in[p, 0], mine_in[p, 1] + got_in[p, 1]], axis=0
        )
        natural = placed(sums, back)
        in_ref[p, 0], in_ref[p, 1] = finish(
            natural[:groups],
            natural[groups:],
            [clip_in[p, i, own, :] for i in range(2)],
            [range_in[p, i, own, :] for i in range(2)],
        )
    own = pl.ds(pl.multiple_of(dp * share, share), share)
    for g in range(out_ref.shape[0]):
        out_ref[g, 0:1, :], out_ref[g, 1:2, :] = finish(
            mine_out[0, g : g + 1, :] + got_out[0, g : g + 1, :],
            mine_out[1, g : g + 1, :] + got_out[1, g : g + 1, :],
            [clip_out[g, i : i + 1, own] for i in range(2)],
            [range_out[g, i : i + 1, own] for i in range(2)],
        )


def add_kernel(*refs):
    total = refs[0][...].astype(F32)
    for ref in refs[1:-1]:
        total = total + ref[...].astype(F32)
    refs[-1][...] = total.astype(refs[-1].dtype)


def part_kernel(first, old, new):
    new[...] = old[first : first + new.shape[0], :]


def hold_kernel(old, new):
    new[...] = old[...]


def body(
    tokens,
    grad_out,
    expert_ids,
    router_weights,
    codes_in,
    codes_out,
    clip_in,
    range_in,
    clip_out,
    range_out,
):
    experts = lax.axis_size("expert")
    rows, width = tokens.shape
    hidden = clip_in.shape[4]
    depth = codes_in.shape[2]
    extra = -(-3 * experts // 128) * 128
    calls = Calls(experts * rows * (3 * width + extra) * 2 < 2**24)

    def swap(array, mask):
        return lax.ppermute(array, "expert", [(i, i ^ mask) for i in range(experts)])

    def swap_core(array):
        return lax.ppermute(array, "dp", [(0, 1), (1, 0)])

    def added(*parts, after=(), free=()):
        return calls.run(
            add_kernel, "add_rows", list(parts), [(parts[0].shape, BF16)], after=after, limit=SMALL, free=free
        )[0]

    def held(array, *after):
        return calls.run(hold_kernel, "hold", [array], [(array.shape, array.dtype)], after, limit=SMALL)[0]

    packed = calls.run(
        functools.partial(pack_kernel, experts),
        "pack_rows",
        [],
        [((rows, 2 * width + extra), BF16)],
        raw=(tokens, grad_out, expert_ids.T, router_weights.T),
        limit=SMALL,
    )[0]

    clips = (clip_in[0], range_in[0], clip_out[0].transpose(1, 0, 2), range_out[0].transpose(1, 0, 2))
    shapes = ((2, 2, depth // GROUP, hidden), (2, clip_out.shape[2], depth))
    sums = {True: None, False: None}

    def dequantized(*after):
        (own_weights,) = calls.run(
            weight_kernel,
            "make_weights",
            [],
            [((3, depth, hidden), BF16)],
            raw=(codes_in[0], codes_out[0], *clips),
            after=after,
        )
        return own_weights, swap_core(own_weights)

    cut = rows // 2

    def part(array, first, after):
        shape = (rows - cut if first else cut, array.shape[1])
        return calls.run(
            functools.partial(part_kernel, first), "part", [array], [(shape, array.dtype)], after, limit=SMALL
        )[0]

    def crossed(over_x, over_y):
        return swap(part(over_x, 0, ()), 2), swap(part(over_y, cut, ()), 1)

    def quad(head, weights, after):
        near = swap(head, 4)
        x0, y0 = swap(head, 1), swap(head, 2)
        far = swap(near, 12)
        if weights is None:
            weights = dequantized(head)
        d0 = crossed(x0, y0)
        ready = held(near, x0, y0, weights[1])
        x1, y1 = swap(ready, 1), swap(ready, 2)
        d1 = tuple(swap(half, 4) for half in d0)
        p0, stored = run_set(calls, (head, x0, y0, *d0), weights, experts, after=after)
        ready = held(far, x1, y1, p0[0])
        x2, y2, last = swap(ready, 1), swap(ready, 2), swap(ready, 4)
        p1, stored = run_set(calls, (near, x1, y1, *d1), weights, experts, stored)
        halves = part(x2, 0, (p1[0],)), part(y2, cut, (p1[0],))
        d2 = swap(halves[0], 2), swap(halves[1], 1)
        ready = held(last, *halves)
        x3, y3 = swap(ready, 1), swap(ready, 2)
        other = run_sums(calls, stored, weights, True, sums[True], shapes, (ready,))
        d3 = tuple(swap(half, 4) for half in d2)
        p2, later = run_set(calls, (far, x2, y2, *d2), weights, experts, after=(other[0],))
        mine = run_sums(calls, stored, weights, False, sums[False], shapes, (p2[0],))
        p3, later = run_set(calls, (last, x3, y3, *d3), weights, experts, later, (mine[0],))
        x_sum0 = added(p0[1], swap(held(p0[3], x3, y3), 2))
        y_sum1 = added(p1[2], swap(held(p1[3], x3, y3), 1))
        x_sum2 = added(p2[1], swap(p2[3], 2), after=(mine[0],))
        total2 = added(p2[0], swap(x_sum2, 1), swap(p2[2], 2), after=(p3[0],))
        far_sum = swap(total2, 8)
        sums[True] = run_sums(calls, later, weights, True, other, shapes, (total2,))
        y_sum3 = added(p3[2], swap(p3[3], 1), after=(sums[True][0],))
        sums[False] = run_sums(calls, later, weights, False, mine, shapes, (y_sum3,))
        total3 = added(p3[0], swap(p3[1], 1), swap(y_sum3, 2), after=(sums[False][0], far_sum))
        late0, late1 = held(p0[2], total2), held(p1[1], total2)
        total1 = added(p1[0], swap(late1, 1), swap(held(y_sum1, total2), 2))
        parts = (
            p0[0],
            swap(held(x_sum0, total2), 1),
            swap(late0, 2),
            swap(total1, 4),
            far_sum,
            swap(total3, 12),
        )
        return parts, weights, total3

    final, after, weights = [], (), None
    for base in range(0, experts, 16):
        parts, weights, last_sum = quad(swap(packed, base) if base else packed, weights, after)
        final += [swap(added(*parts), base)] if base else parts
        after = (sums[False][0],)
    grad_tokens = added(*final, free=(0,))

    mine_in, mine_out = sums[False]
    got_in, got_out = (swap_core(held(a, last_sum)) for a in sums[True])
    grad_in, grad_clip_out = calls.run(
        clip_kernel,
        "clip_gradients",
        [mine_in, got_in, mine_out, got_out],
        [((2, 2, depth // GROUP, hidden), F32), ((clip_out.shape[2], 2, depth), F32)],
        raw=clips,
        limit=SMALL,
        free=(0, 1),
    )
    return grad_tokens, grad_in[None], grad_clip_out.transpose(1, 0, 2)[None]


def solution(mesh):
    return jax.shard_map(
        body,
        mesh=mesh,
        in_specs=(
            P(("expert", "dp"), None),
            P(("expert", "dp"), None),
            P(("expert", "dp"), None),
            P(("expert", "dp"), None),
            P("expert", None, "dp", None),
            P("expert", None, "dp"),
            P("expert", None, None, None, None),
            P("expert", None, None, None, None),
            P("expert", None, None, None),
            P("expert", None, None, None),
        ),
        out_specs=(
            P(("expert", "dp"), None),
            P("expert", None, None, "dp", None),
            P("expert", None, None, "dp"),
        ),
        check_vma=False,
    )
```

```python
import functools

import jax
import jax.numpy as jnp
from jax import lax
from jax.experimental import pallas as pl
from jax.experimental.pallas import tpu as pltpu
from jax.sharding import PartitionSpec as P

GROUP = 128
PACK = 3
CHUNK = 16
TILE = 256
LIMIT = 24 * 1024 * 1024
SMALL = 8 * 1024 * 1024
F32 = jnp.float32
BF16 = jnp.bfloat16


def dot_nn(a, b):
    return lax.dot_general(a, b, (((1,), (0,)), ((), ())), preferred_element_type=F32)


def dot_nt(a, b):
    return lax.dot_general(a, b, (((1,), (1,)), ((), ())), preferred_element_type=F32)


def dot_tn(a, b):
    return lax.dot_general(a, b, (((0,), (0,)), ((), ())), preferred_element_type=F32)


def sigmoid(v):
    return 1.0 / (1.0 + jnp.exp(-v))


def plane_order(size, back=False):
    third = size // PACK
    row = lax.broadcasted_iota(jnp.int32, (size, size), 1 if back else 0)
    col = lax.broadcasted_iota(jnp.int32, (size, size), 0 if back else 1)
    plane = jnp.zeros_like(col)
    for j in range(1, PACK):
        plane = plane + (col >= j * third).astype(jnp.int32)
    return (row == PACK * (col - plane * third) + plane).astype(F32).astype(BF16)


def three_parts(a):
    high = a.astype(BF16)
    rest = a - high.astype(F32)
    middle = rest.astype(BF16)
    low = (rest - middle.astype(F32)).astype(BF16)
    return high, middle, low


def placed(a, order):
    parts = [dot_nn(part, order) for part in three_parts(a)]
    return parts[0] + parts[1] + parts[2]


ANYWHERE = pl.BlockSpec(memory_space=pl.ANY)
INSIDE = pl.BlockSpec(memory_space=pltpu.VMEM)


class Calls:
    def __init__(self, keep):
        self.keep = keep

    def pin(self, array):
        return pltpu.with_memory_space_constraint(array, pltpu.VMEM) if self.keep else array

    def out(self, shape, dtype):
        return pltpu.VMEM(shape, dtype) if self.keep else jax.ShapeDtypeStruct(shape, dtype)

    def run(self, kernel, name, inputs, outputs, after=(), alias=None, limit=LIMIT, raw=(), free=(), flops=0):
        count, given = len(inputs), len(raw)

        def wrapped(*refs):
            outs = refs[given + count + len(after) : given + count + len(after) + len(outputs)]
            scratch = refs[len(refs) - given - 1 : len(refs) - 1] if raw else ()
            copies = [
                pltpu.make_async_copy(refs[i], scratch[i], refs[-1].at[i]) for i in range(given)
            ]
            for copy in copies:
                copy.start()
            for copy in copies:
                copy.wait()
            kernel(*scratch, *refs[given : given + count], *outs)

        scratch = [pltpu.VMEM(a.shape, a.dtype) for a in raw]
        return pl.pallas_call(
            wrapped,
            in_specs=[ANYWHERE] * given + [INSIDE] * count + [ANYWHERE] * len(after),
            out_specs=[INSIDE] * len(outputs),
            out_shape=[
                jax.ShapeDtypeStruct(shape, dtype) if i in free else self.out(shape, dtype)
                for i, (shape, dtype) in enumerate(outputs)
            ],
            scratch_shapes=scratch + ([pltpu.SemaphoreType.DMA((given,))] if raw else []),
            input_output_aliases=alias or {},
            compiler_params=pltpu.CompilerParams(vmem_limit_bytes=limit),
            cost_estimate=pl.CostEstimate(flops=int(flops), bytes_accessed=0, transcendentals=0),
            name=name,
        )(*[pltpu.with_memory_space_constraint(a, pltpu.HBM) for a in raw], *[self.pin(a) for a in inputs], *after)


def pack_kernel(experts, token_ref, grad_ref, ids_ref, weights_ref, out_ref):
    rows, width = grad_ref.shape
    extra = out_ref.shape[1] - 2 * width
    out_ref[:, :width] = token_ref[...]
    out_ref[:, width : 2 * width] = grad_ref[...]
    line = lax.broadcasted_iota(jnp.int32, (extra, rows), 0)
    part = sum((line >= i * experts).astype(jnp.int32) for i in range(1, 4))
    expert = jnp.where(part < 3, line - part * experts, -1)
    table = jnp.zeros((extra, rows), F32)
    for k in range(ids_ref.shape[0]):
        table = table + jnp.where(ids_ref[k : k + 1, :] == expert, weights_ref[k : k + 1, :], 0.0)
    high, middle, low = three_parts(table)
    split = jnp.where(
        part == 0,
        high.astype(F32),
        jnp.where(part == 1, middle.astype(F32), low.astype(F32)),
    ).astype(BF16)
    same = lax.broadcasted_iota(jnp.int32, (extra, extra), 0) == lax.broadcasted_iota(jnp.int32, (extra, extra), 1)
    out_ref[:, 2 * width :] = dot_tn(split, same.astype(F32).astype(BF16)).astype(BF16)


def weight_kernel(codes_in, codes_out, clip_in, range_in, clip_out, range_out, w_ref):
    dp = lax.axis_index("dp")
    depth, third = codes_in.shape[1:]
    hidden = clip_in.shape[3]
    groups = depth // GROUP
    own = pl.ds(pl.multiple_of(dp * groups, groups), groups)
    order = plane_order(hidden)
    for p in range(2):
        upper = sigmoid(clip_in[p, 0, own, :]) * range_in[p, 0, own, :]
        lower = sigmoid(clip_in[p, 1, own, :]) * range_in[p, 1, own, :]
        ends = placed(jnp.concatenate([(upper + lower) / 15.0, lower], axis=0), order)
        for g in range(groups):
            packed = codes_in[p, g * GROUP : (g + 1) * GROUP, :]
            for j in range(PACK):
                code = jnp.bitwise_and(jnp.right_shift(packed, 4 * j), 15).astype(F32)
                cols = slice(j * third, (j + 1) * third)
                w_ref[p, g * GROUP : (g + 1) * GROUP, cols] = (
                    ends[g : g + 1, cols] * code - ends[groups + g : groups + g + 1, cols]
                ).astype(BF16)
    own = pl.ds(pl.multiple_of(dp * depth, depth), depth)
    step, lower = [], []
    for g in range(clip_out.shape[0]):
        upper_end = sigmoid(clip_out[g, 0:1, own]) * range_out[g, 0:1, own]
        lower_end = sigmoid(clip_out[g, 1:2, own]) * range_out[g, 1:2, own]
        step.append((upper_end + lower_end) / 15.0)
        lower.append(lower_end)
    row = lax.broadcasted_iota(jnp.int32, (CHUNK, 1), 0)
    for start in range(0, third, CHUNK):
        packed = codes_out[start : start + CHUNK, :]
        for j in range(PACK):
            first = (PACK * start + j) // GROUP
            last = (PACK * (start + CHUNK - 1) + j) // GROUP
            step_rows, lower_rows = step[first], lower[first]
            for g in range(first + 1, last + 1):
                late = PACK * (row + start) + j >= g * GROUP
                step_rows = jnp.where(late, step[g], step_rows)
                lower_rows = jnp.where(late, lower[g], lower_rows)
            code = jnp.bitwise_and(jnp.right_shift(packed, 4 * j), 15).astype(F32)
            down = (step_rows * code - lower_rows).astype(BF16)
            for q in range(depth // third):
                w_ref[2, q * third + start : q * third + start + CHUNK, j * third : (j + 1) * third] = down[
                    :, q * third : (q + 1) * third
                ]


def set_kernel(experts, first, keep, count, *refs):
    blocks, sides = refs[:count], refs[count : count + 2]
    earlier = refs[count + 2 : count + 6]
    refs = refs[count + 2 :] if first == 0 else refs[count + 6 :]
    partials = refs[0:4]
    x_ref, s_ref, h_ref, g_ref = refs[4:8]
    rows, width = partials[0].shape
    half = width // 2
    hidden = h_ref.shape[1]
    third = hidden // PACK
    dp, mine = lax.axis_index("dp"), lax.axis_index("expert")
    spans = (
        pl.ds(pl.multiple_of(dp * half, half), half),
        pl.ds(pl.multiple_of((1 - dp) * half, half), half),
    )
    here = slice(first, first + 4 * rows)
    if first and not keep:
        for old, new in zip(earlier, refs[4:8]):
            new[..., :first, :] = old[..., :first, :]
    start = first
    for block in blocks:
        span = slice(start, start + block.shape[0])
        start = span.stop
        x_ref[span, :] = block[:, :width]
        beside = block[:, 2 * width :].astype(F32)
        lane = lax.broadcasted_iota(jnp.int32, beside.shape, 1)
        keep = (lane == mine) | (lane == mine + experts) | (lane == mine + 2 * experts)
        scale = jnp.sum(jnp.where(keep, beside, 0.0), axis=1, keepdims=True)
        s_ref[span, :] = (scale * block[:, width : 2 * width].astype(F32)).astype(BF16)
    for j in range(PACK):
        cols = slice(j * third, (j + 1) * third)
        gate_pre = dot_nn(x_ref[here, spans[0]], sides[0][0, :, cols]) + dot_nn(
            x_ref[here, spans[1]], sides[1][0, :, cols]
        )
        up_pre = dot_nn(x_ref[here, spans[0]], sides[0][1, :, cols]) + dot_nn(
            x_ref[here, spans[1]], sides[1][1, :, cols]
        )
        grad_hidden = 0.0
        for side in range(2):
            for q in range(half // third):
                tile = pl.ds(pl.multiple_of((dp if side == 0 else 1 - dp) * half + q * third, third), third)
                grad_hidden = grad_hidden + dot_nt(
                    s_ref[here, tile], sides[side][2, q * third : (q + 1) * third, cols]
                )
        sig = sigmoid(gate_pre)
        act = gate_pre * sig
        h_ref[here, cols] = (act * up_pre).astype(BF16)
        g_ref[0, here, cols] = (grad_hidden * up_pre * sig * (1.0 + gate_pre * (1.0 - sig))).astype(BF16)
        g_ref[1, here, cols] = (grad_hidden * act).astype(BF16)
    for side in range(2):
        base = jnp.where(side == 0, dp, 1 - dp) * half

        @pl.loop(0, half // TILE)
        def _(n):
            depth = pl.ds(pl.multiple_of(n * TILE, TILE), TILE)
            part = dot_nt(g_ref[0, here, :], sides[side][0, depth, :]) + dot_nt(
                g_ref[1, here, :], sides[side][1, depth, :]
            )
            cols = pl.ds(pl.multiple_of(base + n * TILE, TILE), TILE)
            for i in range(4):
                partials[i][:, cols] = part[i * rows : (i + 1) * rows, :].astype(BF16)


def run_set(calls, blocks, weights, experts, pair=None, after=()):
    rows, width = blocks[0].shape[0], 2 * weights[0].shape[1]
    hidden = weights[0].shape[2]
    both = 8 * rows
    stored = [((both, width), BF16), ((both, width), BF16), ((both, hidden), BF16), ((2, both, hidden), BF16)]
    out = calls.run(
        functools.partial(set_kernel, experts, 0 if pair is None else 4 * rows, calls.keep, len(blocks)),
        "expert_set",
        [*blocks, *weights, *(pair or ())],
        [((rows, width), BF16)] * 4 + stored,
        after=after,
        flops=40 * rows * width * hidden,
        alias=None if pair is None else {len(blocks) + 2 + i: 4 + i for i in range(4)},
    )
    return list(out[:4]), list(out[4:])


def group_marks(size, count, span, planes):
    row = lax.broadcasted_iota(jnp.int32, (size, count), 0)
    group = lax.broadcasted_iota(jnp.int32, (size, count), 1)
    if planes > 1:
        third = size // planes
        plane = jnp.zeros_like(row)
        for j in range(1, planes):
            plane = plane + (row >= j * third).astype(jnp.int32)
        row = planes * (row - plane * third) + plane
    return ((row >= group * span) & (row < (group + 1) * span)).astype(F32).astype(BF16)


def two_parts(a):
    high = a.astype(BF16)
    return high, (a - high.astype(F32)).astype(BF16)


def sums_kernel(other, more, x_ref, s_ref, h_ref, g_ref, weights, *refs):
    old_in, old_out = refs[:2] if more else (None, None)
    sums_in, sums_out = refs[-2:]
    width = x_ref.shape[1]
    half = width // 2
    hidden = h_ref.shape[1]
    third = hidden // PACK
    share = sums_in.shape[2]
    groups_out = sums_out.shape[1]
    dp = lax.axis_index("dp")
    base = (1 - dp if other else dp) * half
    span = pl.ds(pl.multiple_of(base, half), half)

    def since(old, found, *where):
        return old[where] + found if more else found

    row_sums = two_parts(dot_nn(x_ref[:, span], group_marks(half, share, GROUP, 1)))
    for p in range(2):
        found = dot_tn(row_sums[0], g_ref[p]) + dot_tn(row_sums[1], g_ref[p])
        sums_in[p, 1] = since(old_in, found, p, 1)
    hidden_sums = two_parts(dot_nn(h_ref[...], group_marks(hidden, groups_out, GROUP, PACK)))
    found = dot_tn(hidden_sums[0], s_ref[:, span]) + dot_tn(hidden_sums[1], s_ref[:, span])
    sums_out[1] = since(old_out, found, 1)

    @pl.loop(0, half // third)
    def _(t):
        rows = pl.ds(pl.multiple_of(t * third, third), third)
        span = pl.ds(pl.multiple_of(base + t * third, third), third)
        x_cols = x_ref[:, span]
        for p in range(2):
            weighted = dot_tn(x_cols, g_ref[p]) * weights[p, rows, :].astype(F32)
            for g in range(third // GROUP):
                spot = pl.ds(t * (third // GROUP) + g, 1)
                found = jnp.sum(weighted[g * GROUP : (g + 1) * GROUP], axis=0, keepdims=True)
                sums_in[p, 0, spot, :] = since(old_in, found, p, 0, spot, slice(None))
        down = jnp.concatenate([weights[2, rows, j * third : (j + 1) * third] for j in range(PACK)], axis=0)
        weighted = dot_tn(h_ref[...], s_ref[:, span]) * down.astype(F32)
        for g in range(groups_out):
            found = None
            for j in range(PACK):
                low = -((j - GROUP * g) // PACK)
                high = -((j - GROUP * (g + 1)) // PACK)
                inner, outer = -(-low // 8) * 8, high // 8 * 8
                part = jnp.sum(weighted[j * third + inner : j * third + outer], axis=0, keepdims=True)
                found = part if found is None else found + part
                for start in sorted(({low // 8 * 8} if low % 8 else set()) | ({outer} if high % 8 else set())):
                    block = weighted[j * third + start : j * third + start + 8]
                    row = lax.broadcasted_iota(jnp.int32, block.shape, 0) + start
                    inside = (row >= low) & (row < high)
                    found = found + jnp.sum(jnp.where(inside, block, 0.0), axis=0, keepdims=True)
            sums_out[0, g : g + 1, rows] = since(old_out, found, 0, slice(g, g + 1), rows)


def run_sums(calls, stored, weights, other, before, shapes, after=()):
    side = weights[1] if other else weights[0]
    return calls.run(
        functools.partial(sums_kernel, other, before is not None),
        "group_sums",
        [*stored, side, *(before or ())],
        [(shape, F32) for shape in shapes],
        after=after,
        flops=24 * stored[0].shape[0] * weights[0].size // 8,
    )


def clip_kernel(clip_in, range_in, clip_out, range_out, mine_in, got_in, mine_out, got_out, in_ref, out_ref):
    dp = lax.axis_index("dp")
    hidden = clip_in.shape[3]
    groups = in_ref.shape[2]
    share = out_ref.shape[2]
    back = plane_order(hidden, True)

    def finish(weighted, plain, clip, span):
        sig_upper, sig_lower = sigmoid(clip[0]), sigmoid(clip[1])
        upper, lower = sig_upper * span[0], sig_lower * span[1]
        upper_sum = (weighted + lower * plain) / (upper + lower)
        lower_sum = upper_sum - plain
        return (
            upper_sum * span[0] * sig_upper * (1.0 - sig_upper),
            lower_sum * span[1] * sig_lower * (1.0 - sig_lower),
        )

    own = pl.ds(pl.multiple_of(dp * groups, groups), groups)
    for p in range(2):
        sums = jnp.concatenate(
            [mine_in[p, 0] + got_in[p, 0], mine_in[p, 1] + got_in[p, 1]], axis=0
        )
        natural = placed(sums, back)
        in_ref[p, 0], in_ref[p, 1] = finish(
            natural[:groups],
            natural[groups:],
            [clip_in[p, i, own, :] for i in range(2)],
            [range_in[p, i, own, :] for i in range(2)],
        )
    own = pl.ds(pl.multiple_of(dp * share, share), share)
    for g in range(out_ref.shape[0]):
        out_ref[g, 0:1, :], out_ref[g, 1:2, :] = finish(
            mine_out[0, g : g + 1, :] + got_out[0, g : g + 1, :],
            mine_out[1, g : g + 1, :] + got_out[1, g : g + 1, :],
            [clip_out[g, i : i + 1, own] for i in range(2)],
            [range_out[g, i : i + 1, own] for i in range(2)],
        )


def add_kernel(*refs):
    total = refs[0][...].astype(F32)
    for ref in refs[1:-1]:
        total = total + ref[...].astype(F32)
    refs[-1][...] = total.astype(refs[-1].dtype)


def part_kernel(first, old, new):
    new[...] = old[first : first + new.shape[0], :]


def hold_kernel(old, new):
    new[...] = old[...]


def body(
    tokens,
    grad_out,
    expert_ids,
    router_weights,
    codes_in,
    codes_out,
    clip_in,
    range_in,
    clip_out,
    range_out,
):
    experts = lax.axis_size("expert")
    rows, width = tokens.shape
    hidden = clip_in.shape[4]
    depth = codes_in.shape[2]
    extra = -(-3 * experts // 128) * 128
    calls = Calls(experts * rows * (3 * width + extra) * 2 < 2**24)

    def swap(array, mask):
        return lax.ppermute(array, "expert", [(i, i ^ mask) for i in range(experts)])

    def swap_core(array):
        return lax.ppermute(array, "dp", [(0, 1), (1, 0)])

    def added(*parts, after=(), free=()):
        return calls.run(
            add_kernel, "add_rows", list(parts), [(parts[0].shape, BF16)], after=after, limit=SMALL, free=free
        )[0]

    def held(array, *after):
        return calls.run(hold_kernel, "hold", [array], [(array.shape, array.dtype)], after, limit=SMALL)[0]

    packed = calls.run(
        functools.partial(pack_kernel, experts),
        "pack_rows",
        [],
        [((rows, 2 * width + extra), BF16)],
        raw=(tokens, grad_out, expert_ids.T, router_weights.T),
        limit=SMALL,
    )[0]

    clips = (clip_in[0], range_in[0], clip_out[0].transpose(1, 0, 2), range_out[0].transpose(1, 0, 2))
    shapes = ((2, 2, depth // GROUP, hidden), (2, clip_out.shape[2], depth))
    sums = {True: None, False: None}

    def dequantized(*after):
        (own_weights,) = calls.run(
            weight_kernel,
            "make_weights",
            [],
            [((3, depth, hidden), BF16)],
            raw=(codes_in[0], codes_out[0], *clips),
            after=after,
        )
        return own_weights, swap_core(own_weights)

    cut = rows // 2

    def part(array, first, after):
        shape = (rows - cut if first else cut, array.shape[1])
        return calls.run(
            functools.partial(part_kernel, first), "part", [array], [(shape, array.dtype)], after, limit=SMALL
        )[0]

    def crossed(over_x, over_y):
        return swap(part(over_x, 0, ()), 2), swap(part(over_y, cut, ()), 1)

    def quad(head, weights, after):
        near = swap(head, 4)
        x0, y0 = swap(head, 1), swap(head, 2)
        far = swap(near, 12)
        if weights is None:
            weights = dequantized(head)
        d0 = crossed(x0, y0)
        ready = held(near, x0, y0, weights[1])
        x1, y1 = swap(ready, 1), swap(ready, 2)
        d1 = tuple(swap(half, 4) for half in d0)
        p0, stored = run_set(calls, (head, x0, y0, *d0), weights, experts, after=after)
        ready = held(far, x1, y1, p0[0])
        x2, y2, last = swap(ready, 1), swap(ready, 2), swap(ready, 4)
        p1, stored = run_set(calls, (near, x1, y1, *d1), weights, experts, stored)
        halves = part(x2, 0, (p1[0],)), part(y2, cut, (p1[0],))
        d2 = swap(halves[0], 2), swap(halves[1], 1)
        ready = held(last, *halves)
        x3, y3 = swap(ready, 1), swap(ready, 2)
        other = run_sums(calls, stored, weights, True, sums[True], shapes, (ready,))
        d3 = tuple(swap(half, 4) for half in d2)
        p2, later = run_set(calls, (far, x2, y2, *d2), weights, experts, after=(other[0],))
        mine = run_sums(calls, stored, weights, False, sums[False], shapes, (p2[0],))
        p3, later = run_set(calls, (last, x3, y3, *d3), weights, experts, later, (mine[0],))
        x_sum0 = added(p0[1], swap(held(p0[3], x3, y3), 2))
        y_sum1 = added(p1[2], swap(held(p1[3], x3, y3), 1))
        x_sum2 = added(p2[1], swap(p2[3], 2), after=(mine[0],))
        total2 = added(p2[0], swap(x_sum2, 1), swap(p2[2], 2), after=(p3[0],))
        far_sum = swap(total2, 8)
        sums[True] = run_sums(calls, later, weights, True, other, shapes, (total2,))
        y_sum3 = added(p3[2], swap(p3[3], 1), after=(sums[True][0],))
        sums[False] = run_sums(calls, later, weights, False, mine, shapes, (y_sum3,))
        total3 = added(p3[0], swap(p3[1], 1), swap(y_sum3, 2), after=(sums[False][0], far_sum))
        late0, late1 = held(p0[2], y_sum3), held(p1[1], y_sum3)
        total1 = added(p1[0], swap(late1, 1), swap(held(y_sum1, y_sum3), 2))
        parts = (
            p0[0],
            swap(held(x_sum0, y_sum3), 1),
            swap(late0, 2),
            swap(total1, 4),
            far_sum,
            swap(total3, 12),
        )
        return parts, weights, total3

    final, after, weights = [], (), None
    for base in range(0, experts, 16):
        parts, weights, last_sum = quad(swap(packed, base) if base else packed, weights, after)
        final += [swap(added(*parts), base)] if base else parts
        after = (sums[False][0],)
    grad_tokens = added(*final, free=(0,))

    mine_in, mine_out = sums[False]
    got_in, got_out = (swap_core(held(a, last_sum)) for a in sums[True])
    grad_in, grad_clip_out = calls.run(
        clip_kernel,
        "clip_gradients",
        [mine_in, got_in, mine_out, got_out],
        [((2, 2, depth // GROUP, hidden), F32), ((clip_out.shape[2], 2, depth), F32)],
        raw=clips,
        limit=SMALL,
        free=(0, 1),
    )
    return grad_tokens, grad_in[None], grad_clip_out.transpose(1, 0, 2)[None]


def solution(mesh):
    return jax.shard_map(
        body,
        mesh=mesh,
        in_specs=(
            P(("expert", "dp"), None),
            P(("expert", "dp"), None),
            P(("expert", "dp"), None),
            P(("expert", "dp"), None),
            P("expert", None, "dp", None),
            P("expert", None, "dp"),
            P("expert", None, None, None, None),
            P("expert", None, None, None, None),
            P("expert", None, None, None),
            P("expert", None, None, None),
        ),
        out_specs=(
            P(("expert", "dp"), None),
            P("expert", None, None, "dp", None),
            P("expert", None, None, "dp"),
        ),
        check_vma=False,
    )
```
